32 devices in a mesh: dp: 8 (over y, x, core), space: 4 (over z).
Axes of the slice: x: 2, y: 2, z: 4, core: 2. Of those that a mesh axis runs over, the one named last changes fastest.
Arguments:
- scenes: bfloat16 [16, 56, 8, 768], P('dp', 'space'), may hold values from -8 to 8
- kernel: bfloat16 [7, 7, 768], replicated, may hold values from -0.875 to 0.875
- weight_in: bfloat16 [768, 1536], replicated, may hold values from -0.21875 to 0.21875
- weight_out: bfloat16 [1536, 768], replicated, may hold values from -0.15625 to 0.15625
- captions: bfloat16 [16, 768], P('dp'), may hold values from -0.21972656 to 0.21972656
- positives: int32 [16], P('dp'), may hold values from 0 to 15, each once
Outputs:
- loss: float32 [], replicated
- text_grad: float32 [16, 768], P('dp')
- kernel_grad: float32 [7, 7, 768], replicated
The draws below stay inside these ranges and needn't reach their ends.
Inputs may be any that keep to these rules, and one draw needn't show every extreme that they name: `positives`: every caption index appears exactly once.
All inputs are finite; a program needn't handle non-finite values.
Results may differ from the reference program's by a relative error of at most 0.0054.
Values may be sent and summed in bfloat16 or wider, within the bound.
No kernel may reach another device: no remote copies, remote signals or barrier semaphores. Data moves between devices by JAX's collectives and lax.ppermute only.
A program may use at most 64 MiB of HBM per device.

```python
import jax
import jax.numpy as jnp
from jax import lax

C = 768
HID = 1536
COLS = 8
IMAGES = 16
HEIGHT = 56


def draw_scenes(key, part):
    key_offset = jax.random.fold_in(key, 11)
    key_noise = jax.random.fold_in(key, 12)
    offset = jax.random.normal(key_offset, (IMAGES, 1, 1, C), jnp.float32)
    noise_part = jax.random.normal(key_noise, (IMAGES, HEIGHT, COLS, C), jnp.float32)
    result = noise_part + offset
    return jnp.clip(result, -8.0, 8.0).astype(jnp.bfloat16)


def block_levels(own_key, dims, split, low, high):
    level = 1.0
    for dim, blocks in split:
        steps = jax.random.uniform(jax.random.fold_in(jax.random.fold_in(own_key, 6), dim), (blocks,), jnp.float32, low / len(split), high / len(split))
        level = level * jnp.repeat(jnp.exp(steps), dims[dim] // blocks).reshape((-1,) + (1,) * (len(dims) - 1 - dim))
    return level


def normal_values(stream_key, shape, scale, bound, shards=(), kind=jnp.bfloat16):
    drawn = jax.random.normal(stream_key, shape, jnp.float32) * scale
    if len(shards) > 0:
        drawn = block_levels(stream_key, shape, shards, -0.22, 0.18) * drawn
    return jnp.clip(drawn, min=-bound, max=bound).astype(kind)


def setup_inputs(seed: int = 0) -> dict:
    splits = jax.random.split(jax.random.key(seed), 7)
    scenes = draw_scenes(jax.random.fold_in(splits[6], 71), 0)
    kernel = normal_values(splits[1], (7, 7, C), 49 ** -0.5, 0.875)
    weight_in = normal_values(splits[2], (C, HID), C ** -0.5, 0.21875)
    weight_out = normal_values(splits[3], (HID, C), HID ** -0.5, 0.15625)
    captions = normal_values(splits[4], (IMAGES, C), 0.036, 0.21972656, ((0, 8),))
    positives = jax.random.permutation(splits[5], IMAGES).astype(jnp.int32)
    return {"scenes": scenes, "kernel": kernel, "weight_in": weight_in, "weight_out": weight_out, "captions": captions, "positives": positives}


EPS = 1e-06
LOGIT_SCALE = 10.0
LOGIT_BIAS = -1.0
GELU_C = 0.7978845608028654

def gelu_tanh(values):
    return 0.5 * values * (1.0 + jnp.tanh(GELU_C * (values + 0.044715 * values * values * values)))

def gelu_slope(values):
    tangent = jnp.tanh(GELU_C * (values + 0.044715 * values * values * values))
    return 0.5 * (1.0 + tangent) + 0.5 * values * (1.0 - tangent * tangent) * GELU_C * (1.0 + 3.0 * 0.044715 * values * values)

def depthwise(padded, kernel, tile_rows, tile_cols):
    total = jnp.zeros(padded.shape[:-3] + (tile_rows, tile_cols, padded.shape[-1]), jnp.float32)
    for row_shift in range(7):
        for col_shift in range(7):
            total = total + kernel[row_shift, col_shift].astype(jnp.float32) * padded[..., row_shift:row_shift + tile_rows, col_shift:col_shift + tile_cols, :]
    return total

def kernel_terms(padded, conv_grad, tile_rows, tile_cols):
    summed_axes = tuple(range(conv_grad.ndim - 1))
    listed = []
    for row_shift in range(7):
        for col_shift in range(7):
            window = padded[..., row_shift:row_shift + tile_rows, col_shift:col_shift + tile_cols, :]
            listed.append(lax.optimization_barrier(jnp.sum(window * conv_grad, axis=summed_axes)))
    return jnp.stack(listed).reshape(7, 7, conv_grad.shape[-1])

def normalize_rows(conv_out):
    center = conv_out - lax.optimization_barrier(jnp.mean(conv_out, axis=-1, keepdims=True))
    inv_scale = lax.rsqrt(lax.optimization_barrier(jnp.mean(center * center, axis=-1, keepdims=True)) + EPS)
    return (center * inv_scale, inv_scale)

def one_forward(one_scene, kernel, weight_in, weight_out):
    padded = jnp.pad(one_scene.astype(jnp.float32), ((3, 3), (3, 3), (0, 0)))
    conv_out = depthwise(padded, kernel, HEIGHT, COLS)
    normed, inv_scale = normalize_rows(conv_out)
    flat_rows = normed.reshape(-1, C).astype(jnp.bfloat16)
    hidden = jnp.dot(flat_rows, weight_in, preferred_element_type=jnp.float32)
    activated = gelu_tanh(hidden).astype(jnp.bfloat16)
    mixed_out = jnp.dot(activated, weight_out, preferred_element_type=jnp.float32)
    block_out = one_scene.reshape(-1, C).astype(jnp.float32) + mixed_out
    return lax.optimization_barrier(jnp.sum(block_out, axis=0))

def one_backward(one_scene, slope_row, kernel, weight_in, weight_out):
    padded = jnp.pad(one_scene.astype(jnp.float32), ((3, 3), (3, 3), (0, 0)))
    conv_out = depthwise(padded, kernel, HEIGHT, COLS)
    normed, inv_scale = normalize_rows(conv_out)
    flat_rows = normed.reshape(-1, C).astype(jnp.bfloat16)
    hidden = jnp.dot(flat_rows, weight_in, preferred_element_type=jnp.float32)
    act_grad = jnp.dot(slope_row[None, :], weight_out.T, preferred_element_type=jnp.float32)
    hidden_grad = (act_grad * gelu_slope(hidden)).astype(jnp.bfloat16)
    normed_grad = jnp.dot(hidden_grad, weight_in.T, preferred_element_type=jnp.float32).reshape(HEIGHT, COLS, C)
    conv_grad = inv_scale * (normed_grad - lax.optimization_barrier(jnp.mean(normed_grad, axis=-1, keepdims=True)) - normed * lax.optimization_barrier(jnp.mean(normed_grad * normed, axis=-1, keepdims=True)))
    return kernel_terms(padded, conv_grad, HEIGHT, COLS)

def unit_rows(values):
    norms = jnp.sqrt(lax.optimization_barrier(jnp.sum(values * values, axis=-1, keepdims=True)) + EPS)
    return (values / norms, norms)

def reference(scenes, kernel, weight_in, weight_out, captions, positives):
    pixels = HEIGHT * COLS
    sums = lax.map(lambda one_scene: one_forward(one_scene, kernel, weight_in, weight_out), scenes)
    pooled = sums / pixels
    image_unit, pooled_norm = unit_rows(pooled)
    text_unit, text_norm = unit_rows(captions.astype(jnp.float32))
    image_cast = image_unit.astype(jnp.bfloat16)
    text_cast = text_unit.astype(jnp.bfloat16)
    logits = LOGIT_SCALE * jnp.dot(image_cast, text_cast.T, preferred_element_type=jnp.float32) + LOGIT_BIAS
    labels = jnp.where(positives[:, None] == jnp.arange(IMAGES, dtype=jnp.int32)[None, :], 1.0, -1.0).astype(jnp.float32)
    loss = jnp.sum(jax.nn.softplus(-labels * logits)) / IMAGES
    pair_grad = (-labels * jax.nn.sigmoid(-labels * logits)).astype(jnp.bfloat16)
    image_side = LOGIT_SCALE * jnp.dot(pair_grad, text_cast, preferred_element_type=jnp.float32)
    caption_side = LOGIT_SCALE * jnp.dot(pair_grad.T, image_cast, preferred_element_type=jnp.float32)
    text_grad = (caption_side - text_unit * lax.optimization_barrier(jnp.sum(text_unit * caption_side, axis=-1, keepdims=True))) / text_norm
    pooled_grad = (image_side - image_unit * lax.optimization_barrier(jnp.sum(image_unit * image_side, axis=-1, keepdims=True))) / pooled_norm
    slope = (pooled_grad / pixels).astype(jnp.bfloat16)
    parts = lax.map(lambda paired: one_backward(paired[0], paired[1], kernel, weight_in, weight_out), (scenes, slope))
    kernel_grad = lax.optimization_barrier(jnp.sum(parts, axis=0))
    return (loss, text_grad, kernel_grad)
```

```python
import functools

import jax
import jax.numpy as jnp
from jax import lax
from jax.experimental import pallas as pl
from jax.experimental.pallas import tpu as pltpu
from jax.sharding import PartitionSpec as P

EPS = 1e-06
LOGIT_SCALE = 10.0
LOGIT_BIAS = -1.0
GELU_C = 0.7978845608028654
TAPS = 7
SIDE = 3
LANES = 128
BF = jnp.bfloat16
F32 = jnp.float32


def in_vmem(array):
    return pltpu.with_memory_space_constraint(array, pltpu.VMEM)


def vmem_out(shape, dtype):
    return pltpu.VMEM(shape, dtype)


def call(body, outs, args, scratch=(), smem=(), limit=40, flops=0):
    specs = [
        pl.BlockSpec(memory_space=pltpu.SMEM if k in smem else pltpu.VMEM)
        for k in range(len(args))
    ]
    args = [a if k in smem else in_vmem(a) for k, a in enumerate(args)]
    return pl.pallas_call(
        body,
        out_shape=[vmem_out(shape, dtype) for shape, dtype in outs],
        in_specs=specs,
        out_specs=[pl.BlockSpec(memory_space=pltpu.VMEM) for _ in outs],
        scratch_shapes=list(scratch),
        compiler_params=pltpu.CompilerParams(vmem_limit_bytes=limit * 1024 * 1024),
        cost_estimate=pl.CostEstimate(flops=flops, bytes_accessed=0, transcendentals=0),
    )(*args)


def column_masks(cols, lanes=LANES):
    at = lax.broadcasted_iota(jnp.int32, (cols, lanes), 0)
    return [
        (at - (j - SIDE) >= 0) & (at - (j - SIDE) < cols) for j in range(TAPS)
    ]


def tile_at(t):
    return pl.ds(pl.multiple_of(t * LANES, LANES), LANES)


def conv_body(x_ref, k_ref, part_ref, kw_ref):
    images, rows, cols, channels = x_ref.shape
    masks = column_masks(cols, channels)
    for i in range(TAPS):
        taps = k_ref[i].astype(F32)
        for j in range(TAPS):
            spread = jnp.broadcast_to(taps[j : j + 1], (cols, channels))
            kw_ref[i * TAPS + j] = jnp.where(masks[j], spread, 0.0)

    def tile(t, carry):
        at = tile_at(t)
        for b in range(images):
            xs = [x_ref[b, r, :, at].astype(F32) for r in range(rows)]
            outs = [None] * rows
            for j in range(TAPS):
                ws = [kw_ref[i * TAPS + j, :, at] for i in range(TAPS)]
                for r in range(rows):
                    total = None
                    for i in range(TAPS):
                        if 0 <= r + i - SIDE < rows:
                            term = ws[i] * xs[r + i - SIDE]
                            total = term if total is None else total + term
                    if j != SIDE:
                        total = pltpu.roll(total, (SIDE - j) % cols, 0)
                    outs[r] = total if outs[r] is None else outs[r] + total
            for r in range(rows):
                part_ref[b, r, :, at] = outs[r]
        return carry

    lax.fori_loop(0, channels // LANES, tile, 0)


def gelu_tanh(values):
    return 0.5 * values * (1.0 + jnp.tanh(GELU_C * (values + 0.044715 * values * values * values)))


def gelu_slope(values):
    tangent = jnp.tanh(GELU_C * (values + 0.044715 * values * values * values))
    return 0.5 * (1.0 + tangent) + 0.5 * values * (1.0 - tangent * tangent) * GELU_C * (
        1.0 + 3.0 * 0.044715 * values * values
    )


def three_terms(value):
    high = value.astype(BF).astype(F32)
    rest = value - high
    mid = rest.astype(BF).astype(F32)
    return high, mid, rest - mid


def forward_body(
    part_ref, before_ref, after_ref, kw_ref, x_ref, win_ref, wout_ref,
    sums_ref, normed_ref, inv_ref, hid_ref, conv_ref, cast_ref,
):
    images, rows, cols, channels = x_ref.shape
    hidden_units = win_ref.shape[1]
    pixels = rows * cols

    def tile(t, carry):
        at = tile_at(t)
        for b in range(images):
            heads = [before_ref[b, q, :, at].astype(F32) for q in range(SIDE)]
            tails = [after_ref[b, q, :, at].astype(F32) for q in range(SIDE)]
            outs = [part_ref[b, r, :, at] for r in range(rows)]
            for j in range(TAPS):
                ws = [kw_ref[i * TAPS + j, :, at] for i in range(TAPS)]
                for r in list(range(SIDE)) + list(range(rows - SIDE, rows)):
                    total = None
                    for i in range(TAPS):
                        q = r + i
                        if q < SIDE:
                            term = ws[i] * heads[q]
                        elif q >= rows + SIDE:
                            term = ws[i] * tails[q - rows - SIDE]
                        else:
                            continue
                        total = term if total is None else total + term
                    if j != SIDE:
                        total = pltpu.roll(total, (SIDE - j) % cols, 0)
                    outs[r] = outs[r] + total
            for r in range(rows):
                conv_ref[pl.ds((b * rows + r) * cols, cols), at] = outs[r]
        return carry

    lax.fori_loop(0, channels // LANES, tile, 0)

    for start in range(0, images * pixels, 32):
        some = pl.ds(start, 32)
        conv_out = conv_ref[some, :]
        center = conv_out - jnp.mean(conv_out, axis=-1, keepdims=True)
        inv = lax.rsqrt(jnp.mean(center * center, axis=-1, keepdims=True) + EPS)
        normed = center * inv
        normed_ref[some, :] = normed
        inv_ref[some, :] = jnp.broadcast_to(inv, (32, LANES))
        cast_ref[some, :] = normed.astype(BF)

    width = 256
    mixed = jnp.zeros((8, channels), F32)
    for start in range(0, hidden_units, width):
        some = pl.ds(start, width)
        hidden = jnp.dot(cast_ref[...], win_ref[:, some], preferred_element_type=F32)
        hid_ref[:, some] = hidden
        activated = gelu_tanh(hidden).astype(BF).astype(F32)
        listed = []
        for b in range(images):
            total = jnp.sum(activated[b * pixels : (b + 1) * pixels], axis=0, keepdims=True)
            listed.extend(three_terms(total))
        listed.append(jnp.zeros((8 - 3 * images, width), F32))
        terms = jnp.concatenate(listed, axis=0).astype(BF)
        mixed = mixed + jnp.dot(terms, wout_ref[some, :], preferred_element_type=F32)
    for b in range(images):
        own = x_ref[b, 0].astype(F32)
        for r in range(1, rows):
            own = own + x_ref[b, r].astype(F32)
        sums_ref[b : b + 1, :] = jnp.sum(own, axis=0, keepdims=True) + jnp.sum(
            mixed[3 * b : 3 * b + 3], axis=0, keepdims=True
        )


def slope_body(hid_ref, slope_ref):
    for start in range(0, hid_ref.shape[1], 256):
        some = pl.ds(start, 256)
        slope_ref[:, some] = gelu_slope(hid_ref[:, some])


def unit_rows(values):
    norms = jnp.sqrt(jnp.sum(values * values, axis=-1, keepdims=True) + EPS)
    return (values / norms, norms)


def kernel_sums(grad_ref, x_ref, before_ref, after_ref, list_ref, half):
    images, rows, cols, channels = x_ref.shape
    masks = column_masks(cols)
    tiles = channels // LANES // 2

    def tile(t, carry):
        at = tile_at(half * tiles + t)
        for j in range(TAPS):
            sums = [None] * TAPS
            for b in range(images):
                grads = []
                for r in range(rows):
                    grad = grad_ref[pl.ds((b * rows + r) * cols, cols), at]
                    grads.append(grad if j == SIDE else pltpu.roll(grad, (j - SIDE) % cols, 0))
                for q in range(rows + 2 * SIDE):
                    if q < SIDE:
                        here = before_ref[b, q, :, at]
                    elif q < rows + SIDE:
                        here = x_ref[b, q - SIDE, :, at]
                    else:
                        here = after_ref[b, q - rows - SIDE, :, at]
                    here = here.astype(F32)
                    for i in range(TAPS):
                        if 0 <= q - i < rows:
                            term = here * grads[q - i]
                            sums[i] = term if sums[i] is None else sums[i] + term
            for i in range(TAPS):
                kept = jnp.where(masks[j], sums[i], 0.0)
                list_ref[pl.ds(t * TAPS * TAPS + i * TAPS + j, 1), :] = jnp.sum(
                    kept, axis=0, keepdims=True
                )
        return carry

    list_ref[...] = jnp.zeros_like(list_ref)
    lax.fori_loop(0, tiles, tile, 0)


def backward_body(
    scene_pixels, total_ref, caps_ref, pos_ref, slope_ref, normed_ref, inv_ref, win_ref, wout_ref,
    x_ref, before_ref, after_ref,
    grad_ref, pay_ref, list_ref, hg_ref, row_ref,
):
    images, rows, cols, channels = x_ref.shape
    pixels = rows * cols
    count = caps_ref.shape[0]
    pooled = total_ref[...] / scene_pixels
    image_unit, pooled_norm = unit_rows(pooled)
    image_cast = image_unit.astype(BF)
    text_unit, _ = unit_rows(caps_ref[...].astype(F32))
    text_cast = text_unit.astype(BF)
    logits = (
        LOGIT_SCALE
        * lax.dot_general(
            image_cast, text_cast, (((1,), (1,)), ((), ())), preferred_element_type=F32
        )
        + LOGIT_BIAS
    )
    row_at = lax.broadcasted_iota(jnp.int32, (images, count), 0)
    positive = jnp.zeros((images, count), jnp.int32)
    for b in range(images):
        positive = jnp.where(row_at == b, pos_ref[b], positive)
    labels = jnp.where(
        positive == lax.broadcasted_iota(jnp.int32, (images, count), 1), 1.0, -1.0
    ).astype(F32)
    margin = -labels * logits
    losses = jnp.maximum(margin, 0.0) + jnp.log(1.0 + jnp.exp(-jnp.abs(margin)))
    loss_part = jnp.sum(jnp.sum(losses, axis=1, keepdims=True), axis=0, keepdims=True)
    pair_grad = (-labels / (1.0 + jnp.exp(-margin))).astype(BF)
    image_side = LOGIT_SCALE * jnp.dot(pair_grad, text_cast, preferred_element_type=F32)
    pooled_grad = (
        image_side - image_unit * jnp.sum(image_unit * image_side, axis=-1, keepdims=True)
    ) / pooled_norm
    slope = (pooled_grad / scene_pixels).astype(BF)
    act_grad = lax.dot_general(
        slope, wout_ref[...], (((1,), (1,)), ((), ())), preferred_element_type=F32
    )
    for b in range(images):
        some = pl.ds(b * pixels, pixels)
        hg_ref[some, :] = (act_grad[b : b + 1] * slope_ref[some, :]).astype(BF)
    normed_grad = lax.dot_general(
        hg_ref[...], win_ref[...], (((1,), (1,)), ((), ())), preferred_element_type=F32
    )
    normed = normed_ref[...]
    grad_ref[...] = inv_ref[:, 0:1] * (
        normed_grad
        - jnp.mean(normed_grad, axis=-1, keepdims=True)
        - normed * jnp.mean(normed_grad * normed, axis=-1, keepdims=True)
    )
    half = 1 - lax.rem(lax.axis_index("dp"), 2)
    kernel_sums(grad_ref, x_ref, before_ref, after_ref, list_ref, half)
    listed = list_ref.shape[0]
    pay_ref[0:listed, :] = list_ref[...].astype(BF)

    row_ref[...] = jnp.zeros_like(row_ref)
    chunks = channels // LANES
    high, mid, low = three_terms(loss_part)
    lane = lax.broadcasted_iota(jnp.int32, (1, LANES), 1)
    for b in range(images):
        for c in range(chunks):
            row_ref[b * (chunks + 1) + c : b * (chunks + 1) + c + 1, :] = image_cast[
                b : b + 1, c * LANES : (c + 1) * LANES
            ].astype(F32)
        at = b * (chunks + 1) + chunks
        row_ref[at : at + 1, 0:count] = pair_grad[b : b + 1, :].astype(F32)
        if b == 0:
            known = row_ref[at : at + 1, :]
            known = jnp.where(lane == LANES - 3, high, known)
            known = jnp.where(lane == LANES - 2, mid, known)
            known = jnp.where(lane == LANES - 1, low, known)
            row_ref[at : at + 1, :] = known
    pay_ref[listed:, :] = row_ref[...].astype(BF)


def own_half_body(grad_ref, x_ref, before_ref, after_ref, list_ref):
    half = lax.rem(lax.axis_index("dp"), 2)
    kernel_sums(grad_ref, x_ref, before_ref, after_ref, list_ref, half)


def text_body(rows_ref, caps_ref, text_ref, loss_ref, wide_ref):
    images, channels = caps_ref.shape
    chunks = channels // LANES
    stride = wide_ref.shape[0] // lax.axis_size("dp")
    groups = lax.axis_size("dp")
    wide_ref[...] = rows_ref[...].astype(F32)
    lane = lax.broadcasted_iota(jnp.int32, (groups, LANES), 1)
    first = lax.axis_index("dp") * images
    caption_side = [[jnp.zeros((1, LANES), F32) for _ in range(chunks)] for _ in range(images)]
    loss = jnp.zeros((1, 1), F32)
    for b in range(images):
        base = b * (chunks + 1)
        pairs = wide_ref[pl.ds(base + chunks, groups, stride=stride), :]
        if b == 0:
            terms = jnp.where(lane >= LANES - 3, pairs, 0.0)
            loss = jnp.sum(jnp.sum(terms, axis=1, keepdims=True), axis=0, keepdims=True)
        weights = [
            jnp.sum(jnp.where(lane == first + k, pairs, 0.0), axis=1, keepdims=True)
            for k in range(images)
        ]
        for c in range(chunks):
            unit = wide_ref[pl.ds(base + c, groups, stride=stride), :]
            for k in range(images):
                caption_side[k][c] = caption_side[k][c] + jnp.sum(
                    weights[k] * unit, axis=0, keepdims=True
                )
    loss_ref[...] = loss / (groups * images)
    text_unit, text_norm = unit_rows(caps_ref[...].astype(F32))
    for k in range(images):
        side = LOGIT_SCALE * jnp.concatenate(caption_side[k], axis=1)
        unit = text_unit[k : k + 1]
        text_ref[k : k + 1, :] = (
            side - unit * jnp.sum(unit * side, axis=-1, keepdims=True)
        ) / text_norm[k : k + 1]


def merge_body(own_ref, other_ref, out_ref, wide_ref):
    tiles = out_ref.shape[2] // LANES // 2
    half = lax.rem(lax.axis_index("dp"), 2)
    for source, side in ((own_ref, half), (other_ref, 1 - half)):
        wide_ref[...] = source[...].astype(F32)
        for t in range(tiles):
            at = tile_at(side * tiles + t)
            for i in range(TAPS):
                out_ref[i, :, at] = wide_ref[pl.ds((t * TAPS + i) * TAPS, TAPS), :]


def flip(array, axis, bit):
    return lax.ppermute(array, axis, [(i, i ^ bit) for i in range(lax.axis_size(axis))])


def bits(axis):
    size = lax.axis_size(axis)
    return [1 << k for k in range(size.bit_length() - 1)]


def join(mine, theirs, axis, bit):
    upper = lax.rem(lax.axis_index(axis) // bit, 2) == 1
    return jnp.where(
        upper,
        jnp.concatenate([theirs, mine], axis=0),
        jnp.concatenate([mine, theirs], axis=0),
    )


def rounded(values):
    return lax.reduce_precision(values, 8, 7).astype(BF)


def per_device(scenes, kernel, weight_in, weight_out, captions, positives):
    images, rows, cols, channels = scenes.shape
    hidden_units = weight_in.shape[1]
    space_count = lax.axis_size("space")
    pixels = images * rows * cols
    scene_pixels = rows * space_count * cols

    up = [(i, i + 1) for i in range(space_count - 1)]
    down = [(j, i) for i, j in up]
    before = lax.ppermute(scenes[:, rows - SIDE :], "space", up)
    after = lax.ppermute(scenes[:, :SIDE], "space", down)
    macs = 2 * TAPS * TAPS * pixels * channels
    part, spread = call(
        conv_body,
        [((images, rows, cols, channels), F32), ((TAPS * TAPS, cols, channels), F32)],
        [scenes, kernel],
        flops=macs,
    )
    gathered = captions
    for bit in bits("dp"):
        gathered = join(gathered, flip(gathered, "dp", bit), "dp", bit)

    sums, normed, inv, hidden = call(
        forward_body,
        [
            ((images, channels), F32),
            ((pixels, channels), F32),
            ((pixels, LANES), F32),
            ((pixels, hidden_units), F32),
        ],
        [part, before, after, spread, scenes, weight_in, weight_out],
        scratch=[pltpu.VMEM((pixels, channels), F32), pltpu.VMEM((pixels, channels), BF)],
        flops=2 * pixels * channels * hidden_units,
    )
    for bit in bits("space"):
        sums = sums + flip(sums, "space", bit)
    (slope,) = call(slope_body, [((pixels, hidden_units), F32)], [hidden], flops=1000000)

    listed = channels // LANES // 2 * TAPS * TAPS
    listed += -listed % 16
    own_rows = images * (channels // LANES + 1)
    own_rows += -own_rows % 16
    grad, pay = call(
        functools.partial(backward_body, scene_pixels),
        [((pixels, channels), F32), ((listed + own_rows, LANES), BF)],
        [sums, gathered, positives, slope, normed, inv, weight_in, weight_out, scenes, before, after],
        scratch=[
            pltpu.VMEM((listed, LANES), F32),
            pltpu.VMEM((pixels, hidden_units), BF),
            pltpu.VMEM((own_rows, LANES), F32),
        ],
        smem=(2,),
        flops=macs,
    )
    other = flip(pay, "dp", 1)
    (own,) = call(
        own_half_body, [((listed, LANES), F32)], [grad, scenes, before, after], flops=macs // 2
    )
    total = own + other[:listed].astype(F32)
    units = join(pay[listed:], other[listed:], "dp", 1)
    for bit in bits("dp")[1:]:
        mine = rounded(total)
        other = flip(jnp.concatenate([mine, units], axis=0), "dp", bit)
        total = mine.astype(F32) + other[:listed].astype(F32)
        units = join(units, other[listed:], "dp", bit)
    text_grad, loss = call(
        text_body,
        [((images, channels), F32), ((1, 1), F32)],
        [units, captions],
        scratch=[pltpu.VMEM(units.shape, F32)],
    )
    for bit in bits("space"):
        mine = rounded(total)
        total = mine.astype(F32) + flip(mine, "space", bit).astype(F32)
    mine = rounded(total)
    other = flip(mine, "dp", 1)
    (kernel_grad,) = call(
        merge_body,
        [((TAPS, TAPS, channels), F32)],
        [mine, other],
        scratch=[pltpu.VMEM((listed, LANES), F32)],
    )
    return (loss.reshape(()), text_grad, kernel_grad)


def solution(mesh):
    return jax.shard_map(
        per_device,
        mesh=mesh,
        in_specs=(P("dp", "space", None, None), P(), P(), P(), P("dp", None), P("dp")),
        out_specs=(P(), P("dp", None), P()),
        check_vma=False,
    )
```

```python
import functools

import jax
import jax.numpy as jnp
from jax import lax
from jax.experimental import pallas as pl
from jax.experimental.pallas import tpu as pltpu
from jax.sharding import PartitionSpec as P

EPS = 1e-06
LOGIT_SCALE = 10.0
LOGIT_BIAS = -1.0
GELU_C = 0.7978845608028654
TAPS = 7
SIDE = 3
LANES = 128
BF = jnp.bfloat16
F32 = jnp.float32


def in_vmem(array):
    return pltpu.with_memory_space_constraint(array, pltpu.VMEM)


def vmem_out(shape, dtype):
    return pltpu.VMEM(shape, dtype)


def in_hbm(array):
    return pltpu.with_memory_space_constraint(array, pltpu.HBM)


def call(body, outs, args, scratch=(), smem=(), hbm=(), limit=40, micros=1):
    specs = []
    placed = []
    for k, arg in enumerate(args):
        if k in smem:
            specs.append(pl.BlockSpec(memory_space=pltpu.SMEM))
            placed.append(arg)
        elif k in hbm:
            specs.append(pl.BlockSpec(memory_space=pl.ANY))
            placed.append(in_hbm(arg))
        else:
            specs.append(pl.BlockSpec(memory_space=pltpu.VMEM))
            placed.append(in_vmem(arg))
    return pl.pallas_call(
        body,
        out_shape=[vmem_out(shape, dtype) for shape, dtype in outs],
        in_specs=specs,
        out_specs=[pl.BlockSpec(memory_space=pltpu.VMEM) for _ in outs],
        scratch_shapes=list(scratch),
        compiler_params=pltpu.CompilerParams(vmem_limit_bytes=limit * 1024 * 1024),
        cost_estimate=pl.CostEstimate(
            flops=int(micros * 1.15e9), bytes_accessed=0, transcendentals=0
        ),
    )(*placed)


def column_masks(cols, lanes=LANES):
    at = lax.broadcasted_iota(jnp.int32, (cols, lanes), 0)
    return [
        (at - (j - SIDE) >= 0) & (at - (j - SIDE) < cols) for j in range(TAPS)
    ]


def tile_at(t):
    return pl.ds(pl.multiple_of(t * LANES, LANES), LANES)


def load_body(x_hbm, k_hbm, x_ref, first_ref, last_ref, kw_ref, taps_ref, sems):
    rows, cols, channels = x_hbm.shape[1:]
    copies = [
        pltpu.make_async_copy(k_hbm, taps_ref, sems.at[0]),
        pltpu.make_async_copy(x_hbm.at[:, :SIDE], first_ref, sems.at[1]),
        pltpu.make_async_copy(x_hbm.at[:, rows - SIDE :], last_ref, sems.at[2]),
        pltpu.make_async_copy(x_hbm, x_ref, sems.at[3]),
    ]
    for copy in copies:
        copy.start()
    masks = column_masks(cols, channels)
    copies[0].wait()
    for i in range(TAPS):
        taps = taps_ref[i].astype(F32)
        for j in range(TAPS):
            spread = jnp.broadcast_to(taps[j : j + 1], (cols, channels))
            kw_ref[i * TAPS + j] = jnp.where(masks[j], spread, 0.0)
    for copy in copies[1:]:
        copy.wait()


def conv_body(
    x_ref, kw_ref, win_hbm, wout_hbm, part_ref, win_ref, wout_ref, sems
):
    images, rows, cols, channels = x_ref.shape
    copies = [
        pltpu.make_async_copy(win_hbm, win_ref, sems.at[0]),
        pltpu.make_async_copy(wout_hbm, wout_ref, sems.at[1]),
    ]
    for copy in copies:
        copy.start()

    def tile(t, carry):
        at = tile_at(t)
        for b in range(images):
            xs = [x_ref[b, r, :, at].astype(F32) for r in range(rows)]
            outs = [None] * rows
            for j in range(TAPS):
                ws = [kw_ref[i * TAPS + j, :, at] for i in range(TAPS)]
                for r in range(rows):
                    total = None
                    for i in range(TAPS):
                        if 0 <= r + i - SIDE < rows:
                            term = ws[i] * xs[r + i - SIDE]
                            total = term if total is None else total + term
                    if j != SIDE:
                        total = pltpu.roll(total, (SIDE - j) % cols, 0)
                    outs[r] = total if outs[r] is None else outs[r] + total
            for r in range(rows):
                part_ref[b, r, :, at] = outs[r]
        return carry

    lax.fori_loop(0, channels // LANES, tile, 0)
    for copy in copies:
        copy.wait()


def gelu_tanh(values):
    return 0.5 * values * (1.0 + jnp.tanh(GELU_C * (values + 0.044715 * values * values * values)))


def gelu_slope(values):
    tangent = jnp.tanh(GELU_C * (values + 0.044715 * values * values * values))
    return 0.5 * (1.0 + tangent) + 0.5 * values * (1.0 - tangent * tangent) * GELU_C * (
        1.0 + 3.0 * 0.044715 * values * values
    )


def three_terms(value):
    high = value.astype(BF).astype(F32)
    rest = value - high
    mid = rest.astype(BF).astype(F32)
    return high, mid, rest - mid


def forward_body(
    part_ref, below_ref, above_ref, kw_ref, x_ref, win_ref, wout_ref,
    sums_ref, normed_ref, inv_ref, hid_ref, before_ref, after_ref, conv_ref, cast_ref,
):
    images, rows, cols, channels = x_ref.shape
    hidden_units = win_ref.shape[1]
    pixels = rows * cols
    place = lax.axis_index("space")
    zeros = jnp.zeros((cols, channels), BF)
    for b in range(images):
        for q in range(SIDE):
            before_ref[b, q] = jnp.where(place > 0, below_ref[b, q], zeros)
            after_ref[b, q] = jnp.where(
                place < lax.axis_size("space") - 1, above_ref[b, q], zeros
            )

    def tile(t, carry):
        at = tile_at(t)
        for b in range(images):
            heads = [before_ref[b, q, :, at].astype(F32) for q in range(SIDE)]
            tails = [after_ref[b, q, :, at].astype(F32) for q in range(SIDE)]
            outs = [part_ref[b, r, :, at] for r in range(rows)]
            for j in range(TAPS):
                ws = [kw_ref[i * TAPS + j, :, at] for i in range(TAPS)]
                for r in list(range(SIDE)) + list(range(rows - SIDE, rows)):
                    total = None
                    for i in range(TAPS):
                        q = r + i
                        if q < SIDE:
                            term = ws[i] * heads[q]
                        elif q >= rows + SIDE:
                            term = ws[i] * tails[q - rows - SIDE]
                        else:
                            continue
                        total = term if total is None else total + term
                    if j != SIDE:
                        total = pltpu.roll(total, (SIDE - j) % cols, 0)
                    outs[r] = outs[r] + total
            for r in range(rows):
                conv_ref[pl.ds((b * rows + r) * cols, cols), at] = outs[r]
        return carry

    lax.fori_loop(0, channels // LANES, tile, 0)

    for start in range(0, images * pixels, 32):
        some = pl.ds(start, 32)
        conv_out = conv_ref[some, :]
        center = conv_out - jnp.mean(conv_out, axis=-1, keepdims=True)
        inv = lax.rsqrt(jnp.mean(center * center, axis=-1, keepdims=True) + EPS)
        normed = center * inv
        normed_ref[some, :] = normed
        inv_ref[some, :] = jnp.broadcast_to(inv, (32, LANES))
        cast_ref[some, :] = normed.astype(BF)

    width = 256
    mixed = jnp.zeros((8, channels), F32)
    for start in range(0, hidden_units, width):
        some = pl.ds(start, width)
        hidden = jnp.dot(cast_ref[...], win_ref[:, some], preferred_element_type=F32)
        hid_ref[:, some] = hidden
        activated = gelu_tanh(hidden).astype(BF).astype(F32)
        listed = []
        for b in range(images):
            total = jnp.sum(activated[b * pixels : (b + 1) * pixels], axis=0, keepdims=True)
            listed.extend(three_terms(total))
        listed.append(jnp.zeros((8 - 3 * images, width), F32))
        terms = jnp.concatenate(listed, axis=0).astype(BF)
        mixed = mixed + jnp.dot(terms, wout_ref[some, :], preferred_element_type=F32)
    for b in range(images):
        own = x_ref[b, 0].astype(F32)
        for r in range(1, rows):
            own = own + x_ref[b, r].astype(F32)
        sums_ref[b : b + 1, :] = jnp.sum(own, axis=0, keepdims=True) + jnp.sum(
            mixed[3 * b : 3 * b + 3], axis=0, keepdims=True
        )


def slope_body(hid_ref, slope_ref):
    for start in range(0, hid_ref.shape[1], 256):
        some = pl.ds(start, 256)
        slope_ref[:, some] = gelu_slope(hid_ref[:, some])


def unit_rows(values):
    norms = jnp.sqrt(jnp.sum(values * values, axis=-1, keepdims=True) + EPS)
    return (values / norms, norms)


def kernel_sums(grad_ref, x_ref, before_ref, after_ref, list_ref, half):
    images, rows, cols, channels = x_ref.shape
    masks = column_masks(cols)
    tiles = channels // LANES // 2

    def tile(t, carry):
        at = tile_at(half * tiles + t)
        for j in range(TAPS):
            sums = [None] * TAPS
            for b in range(images):
                grads = []
                for r in range(rows):
                    grad = grad_ref[pl.ds((b * rows + r) * cols, cols), at]
                    grads.append(grad if j == SIDE else pltpu.roll(grad, (j - SIDE) % cols, 0))
                for q in range(rows + 2 * SIDE):
                    if q < SIDE:
                        here = before_ref[b, q, :, at]
                    elif q < rows + SIDE:
                        here = x_ref[b, q - SIDE, :, at]
                    else:
                        here = after_ref[b, q - rows - SIDE, :, at]
                    here = here.astype(F32)
                    for i in range(TAPS):
                        if 0 <= q - i < rows:
                            term = here * grads[q - i]
                            sums[i] = term if sums[i] is None else sums[i] + term
            for i in range(TAPS):
                kept = jnp.where(masks[j], sums[i], 0.0)
                list_ref[pl.ds(t * TAPS * TAPS + i * TAPS + j, 1), :] = jnp.sum(
                    kept, axis=0, keepdims=True
                )
        return carry

    list_ref[...] = jnp.zeros_like(list_ref)
    lax.fori_loop(0, tiles, tile, 0)


def backward_body(
    scene_pixels, total_ref, caps_ref, pos_ref, slope_ref, normed_ref, inv_ref, win_ref, wout_ref,
    x_ref, before_ref, after_ref,
    grad_ref, pay_ref, list_ref, hg_ref, row_ref,
):
    images, rows, cols, channels = x_ref.shape
    pixels = rows * cols
    count = caps_ref.shape[0]
    pooled = total_ref[...] / scene_pixels
    image_unit, pooled_norm = unit_rows(pooled)
    image_cast = image_unit.astype(BF)
    text_unit, _ = unit_rows(caps_ref[...].astype(F32))
    text_cast = text_unit.astype(BF)
    logits = (
        LOGIT_SCALE
        * lax.dot_general(
            image_cast, text_cast, (((1,), (1,)), ((), ())), preferred_element_type=F32
        )
        + LOGIT_BIAS
    )
    row_at = lax.broadcasted_iota(jnp.int32, (images, count), 0)
    positive = jnp.zeros((images, count), jnp.int32)
    for b in range(images):
        positive = jnp.where(row_at == b, pos_ref[b], positive)
    labels = jnp.where(
        positive == lax.broadcasted_iota(jnp.int32, (images, count), 1), 1.0, -1.0
    ).astype(F32)
    margin = -labels * logits
    losses = jnp.maximum(margin, 0.0) + jnp.log(1.0 + jnp.exp(-jnp.abs(margin)))
    loss_part = jnp.sum(jnp.sum(losses, axis=1, keepdims=True), axis=0, keepdims=True)
    pair_grad = (-labels / (1.0 + jnp.exp(-margin))).astype(BF)
    image_side = LOGIT_SCALE * jnp.dot(pair_grad, text_cast, preferred_element_type=F32)
    pooled_grad = (
        image_side - image_unit * jnp.sum(image_unit * image_side, axis=-1, keepdims=True)
    ) / pooled_norm
    slope = (pooled_grad / scene_pixels).astype(BF)
    act_grad = lax.dot_general(
        slope, wout_ref[...], (((1,), (1,)), ((), ())), preferred_element_type=F32
    )
    for b in range(images):
        some = pl.ds(b * pixels, pixels)
        hg_ref[some, :] = (act_grad[b : b + 1] * slope_ref[some, :]).astype(BF)
    normed_grad = lax.dot_general(
        hg_ref[...], win_ref[...], (((1,), (1,)), ((), ())), preferred_element_type=F32
    )
    normed = normed_ref[...]
    grad_ref[...] = inv_ref[:, 0:1] * (
        normed_grad
        - jnp.mean(normed_grad, axis=-1, keepdims=True)
        - normed * jnp.mean(normed_grad * normed, axis=-1, keepdims=True)
    )
    half = 1 - lax.rem(lax.axis_index("dp"), 2)
    kernel_sums(grad_ref, x_ref, before_ref, after_ref, list_ref, half)
    listed = list_ref.shape[0]
    pay_ref[0:listed, :] = list_ref[...].astype(BF)

    row_ref[...] = jnp.zeros_like(row_ref)
    chunks = channels // LANES
    high, mid, low = three_terms(loss_part)
    lane = lax.broadcasted_iota(jnp.int32, (1, LANES), 1)
    for b in range(images):
        for c in range(chunks):
            row_ref[b * (chunks + 1) + c : b * (chunks + 1) + c + 1, :] = image_cast[
                b : b + 1, c * LANES : (c + 1) * LANES
            ].astype(F32)
        at = b * (chunks + 1) + chunks
        row_ref[at : at + 1, 0:count] = pair_grad[b : b + 1, :].astype(F32)
        if b == 0:
            known = row_ref[at : at + 1, :]
            known = jnp.where(lane == LANES - 3, high, known)
            known = jnp.where(lane == LANES - 2, mid, known)
            known = jnp.where(lane == LANES - 1, low, known)
            row_ref[at : at + 1, :] = known
    pay_ref[listed:, :] = row_ref[...].astype(BF)


def own_half_body(grad_ref, x_ref, before_ref, after_ref, list_ref):
    half = lax.rem(lax.axis_index("dp"), 2)
    kernel_sums(grad_ref, x_ref, before_ref, after_ref, list_ref, half)


def text_body(rows_ref, caps_ref, text_ref, loss_ref, wide_ref):
    images, channels = caps_ref.shape
    chunks = channels // LANES
    stride = wide_ref.shape[0] // lax.axis_size("dp")
    groups = lax.axis_size("dp")
    wide_ref[...] = rows_ref[...].astype(F32)
    lane = lax.broadcasted_iota(jnp.int32, (groups, LANES), 1)
    first = lax.axis_index("dp") * images
    caption_side = [[jnp.zeros((1, LANES), F32) for _ in range(chunks)] for _ in range(images)]
    loss = jnp.zeros((1, 1), F32)
    for b in range(images):
        base = b * (chunks + 1)
        pairs = wide_ref[pl.ds(base + chunks, groups, stride=stride), :]
        if b == 0:
            terms = jnp.where(lane >= LANES - 3, pairs, 0.0)
            loss = jnp.sum(jnp.sum(terms, axis=1, keepdims=True), axis=0, keepdims=True)
        weights = [
            jnp.sum(jnp.where(lane == first + k, pairs, 0.0), axis=1, keepdims=True)
            for k in range(images)
        ]
        for c in range(chunks):
            unit = wide_ref[pl.ds(base + c, groups, stride=stride), :]
            for k in range(images):
                caption_side[k][c] = caption_side[k][c] + jnp.sum(
                    weights[k] * unit, axis=0, keepdims=True
                )
    loss_ref[...] = loss / (groups * images)
    text_unit, text_norm = unit_rows(caps_ref[...].astype(F32))
    for k in range(images):
        side = LOGIT_SCALE * jnp.concatenate(caption_side[k], axis=1)
        unit = text_unit[k : k + 1]
        text_ref[k : k + 1, :] = (
            side - unit * jnp.sum(unit * side, axis=-1, keepdims=True)
        ) / text_norm[k : k + 1]


def merge_body(own_ref, other_ref, out_ref, wide_ref):
    tiles = out_ref.shape[2] // LANES // 2
    half = lax.rem(lax.axis_index("dp"), 2)
    for source, side in ((own_ref, half), (other_ref, 1 - half)):
        wide_ref[...] = source[...].astype(F32)
        for t in range(tiles):
            at = tile_at(side * tiles + t)
            for i in range(TAPS):
                out_ref[i, :, at] = wide_ref[pl.ds((t * TAPS + i) * TAPS, TAPS), :]


def shifted(array, axis, stride, step, size=4):
    pairs = []
    for i in range(lax.axis_size(axis)):
        place = i // stride % size
        pairs.append((i, i + ((place + step) % size - place) * stride))
    return lax.ppermute(array, axis, pairs)


def flip(array, axis, mask):
    return lax.ppermute(array, axis, [(i, i ^ mask) for i in range(lax.axis_size(axis))])


def groups(size, stride):
    listed = []
    while stride < size:
        members = 4 if size // stride % 4 == 0 else 2
        listed.append((stride, members))
        stride *= members
    return listed


def bits(axis):
    size = lax.axis_size(axis)
    return [1 << k for k in range(size.bit_length() - 1)]


def join(mine, theirs, axis, bit):
    upper = lax.rem(lax.axis_index(axis) // bit, 2) == 1
    return jnp.where(
        upper,
        jnp.concatenate([theirs, mine], axis=0),
        jnp.concatenate([mine, theirs], axis=0),
    )


def rounded(values):
    return lax.reduce_precision(values, 8, 7).astype(BF)


def group_sum(mine, axis, stride, members):
    if members == 2:
        return mine.astype(F32) + flip(mine, axis, stride).astype(F32)
    one, two, three = [shifted(mine, axis, stride, k).astype(F32) for k in (1, 2, 3)]
    return (mine.astype(F32) + two) + (one + three)


def per_device(scenes, kernel, weight_in, weight_out, captions, positives):
    images, rows, cols, channels = scenes.shape
    hidden_units = weight_in.shape[1]
    space_count = lax.axis_size("space")
    pixels = images * rows * cols
    scene_pixels = rows * space_count * cols
    edge = (images, SIDE, cols, channels)

    x, first, last, spread = call(
        load_body,
        [
            (scenes.shape, BF),
            (edge, BF),
            (edge, BF),
            ((TAPS * TAPS, cols, channels), F32),
        ],
        [scenes, kernel],
        scratch=[pltpu.VMEM(kernel.shape, BF), pltpu.SemaphoreType.DMA((4,))],
        hbm=(0, 1),
    )
    below = shifted(last, "space", 1, 1, space_count)
    above = shifted(first, "space", 1, space_count - 1, space_count)
    gathered = captions
    for bit in bits("dp"):
        gathered = join(gathered, flip(gathered, "dp", bit), "dp", bit)
    part, win, wout = call(
        conv_body,
        [
            (scenes.shape, F32),
            (weight_in.shape, BF),
            (weight_out.shape, BF),
        ],
        [x, spread, weight_in, weight_out],
        scratch=[pltpu.SemaphoreType.DMA((2,))],
        hbm=(2, 3),
        micros=2.3,
    )

    sums, normed, inv, hidden, before, after = call(
        forward_body,
        [
            ((images, channels), F32),
            ((pixels, channels), F32),
            ((pixels, LANES), F32),
            ((pixels, hidden_units), F32),
            (edge, BF),
            (edge, BF),
        ],
        [part, below, above, spread, x, win, wout],
        scratch=[pltpu.VMEM((pixels, channels), F32), pltpu.VMEM((pixels, channels), BF)],
        micros=3,
    )
    for stride, members in groups(space_count, 1):
        sums = group_sum(sums, "space", stride, members)
    (slope,) = call(slope_body, [((pixels, hidden_units), F32)], [hidden], micros=0.8)

    listed = channels // LANES // 2 * TAPS * TAPS
    listed += -listed % 16
    own_rows = images * (channels // LANES + 1)
    own_rows += -own_rows % 16
    grad, pay = call(
        functools.partial(backward_body, scene_pixels),
        [((pixels, channels), F32), ((listed + own_rows, LANES), BF)],
        [sums, gathered, positives, slope, normed, inv, win, wout, x, before, after],
        scratch=[
            pltpu.VMEM((listed, LANES), F32),
            pltpu.VMEM((pixels, hidden_units), BF),
            pltpu.VMEM((own_rows, LANES), F32),
        ],
        smem=(2,),
        micros=4,
    )
    other = flip(pay, "dp", 1)
    (own,) = call(
        own_half_body, [((listed, LANES), F32)], [grad, x, before, after], micros=1.6
    )
    total = own + other[:listed].astype(F32)
    units = join(pay[listed:], other[listed:], "dp", 1)
    for stride, members in groups(lax.axis_size("dp"), 2):
        mine = rounded(total)
        both = jnp.concatenate([mine, units], axis=0)
        near = flip(both, "dp", stride)
        total = mine.astype(F32) + near[:listed].astype(F32)
        joined = join(units, near[listed:], "dp", stride)
        if members == 4:
            far = flip(both, "dp", 2 * stride)
            cross = flip(both, "dp", 3 * stride)
            total = total + (far[:listed].astype(F32) + cross[:listed].astype(F32))
            joined = join(
                joined, join(far[listed:], cross[listed:], "dp", stride), "dp", 2 * stride
            )
        units = joined
    text_grad, loss = call(
        text_body,
        [((images, channels), F32), ((1, 1), F32)],
        [units, captions],
        scratch=[pltpu.VMEM(units.shape, F32)],
    )
    for stride, members in groups(space_count, 1):
        total = group_sum(rounded(total), "space", stride, members)
    mine = rounded(total)
    other = flip(mine, "dp", 1)
    (kernel_grad,) = call(
        merge_body,
        [((TAPS, TAPS, channels), F32)],
        [mine, other],
        scratch=[pltpu.VMEM((listed, LANES), F32)],
    )
    return (loss.reshape(()), text_grad, kernel_grad)


def solution(mesh):
    return jax.shard_map(
        per_device,
        mesh=mesh,
        in_specs=(P("dp", "space", None, None), P(), P(), P(), P("dp", None), P("dp")),
        out_specs=(P(), P("dp", None), P()),
        check_vma=False,
    )
```

```python
import functools

import jax
import jax.numpy as jnp
from jax import lax
from jax.experimental import pallas as pl
from jax.experimental.pallas import tpu as pltpu
from jax.sharding import PartitionSpec as P

EPS = 1e-06
LOGIT_SCALE = 10.0
LOGIT_BIAS = -1.0
GELU_C = 0.7978845608028654
TAPS = 7
SIDE = 3
LANES = 128
BF = jnp.bfloat16
F32 = jnp.float32


def in_vmem(array):
    return pltpu.with_memory_space_constraint(array, pltpu.VMEM)


def vmem_out(shape, dtype):
    return pltpu.VMEM(shape, dtype)


def in_hbm(array):
    return pltpu.with_memory_space_constraint(array, pltpu.HBM)


def call(body, outs, args, scratch=(), smem=(), hbm=(), limit=10):
    specs = []
    placed = []
    for k, arg in enumerate(args):
        if k in smem:
            specs.append(pl.BlockSpec(memory_space=pltpu.SMEM))
            placed.append(arg)
        elif k in hbm:
            specs.append(pl.BlockSpec(memory_space=pl.ANY))
            placed.append(in_hbm(arg))
        else:
            specs.append(pl.BlockSpec(memory_space=pltpu.VMEM))
            placed.append(in_vmem(arg))
    return pl.pallas_call(
        body,
        out_shape=[vmem_out(shape, dtype) for shape, dtype in outs],
        in_specs=specs,
        out_specs=[pl.BlockSpec(memory_space=pltpu.VMEM) for _ in outs],
        scratch_shapes=list(scratch),
        compiler_params=pltpu.CompilerParams(vmem_limit_bytes=limit * 1024 * 1024),
        cost_estimate=pl.CostEstimate(flops=0, bytes_accessed=0, transcendentals=0),
    )(*placed)


def column_masks(cols, lanes=LANES):
    at = lax.broadcasted_iota(jnp.int32, (cols, lanes), 0)
    return [
        (at - (j - SIDE) >= 0) & (at - (j - SIDE) < cols) for j in range(TAPS)
    ]


def tile_at(t):
    return pl.ds(pl.multiple_of(t * LANES, LANES), LANES)


def load_body(
    x_hbm, k_hbm, caps_hbm, x_ref, first_ref, last_ref, kw_ref, caps_ref, taps_ref, sems
):
    rows, cols, channels = x_hbm.shape[1:]
    copies = [
        pltpu.make_async_copy(k_hbm, taps_ref, sems.at[0]),
        pltpu.make_async_copy(x_hbm.at[:, :SIDE], first_ref, sems.at[1]),
        pltpu.make_async_copy(x_hbm.at[:, rows - SIDE :], last_ref, sems.at[2]),
        pltpu.make_async_copy(x_hbm, x_ref, sems.at[3]),
        pltpu.make_async_copy(caps_hbm, caps_ref, sems.at[4]),
    ]
    for copy in copies:
        copy.start()
    masks = column_masks(cols, channels)
    copies[0].wait()
    for i in range(TAPS):
        taps = taps_ref[i].astype(F32)
        for j in range(TAPS):
            spread = jnp.broadcast_to(taps[j : j + 1], (cols, channels))
            kw_ref[i * TAPS + j] = jnp.where(masks[j], spread, 0.0)
    for copy in copies[1:]:
        copy.wait()


def conv_body(
    x_ref, kw_ref, win_hbm, wout_hbm, part_ref, win_ref, wout_ref, sems
):
    images, rows, cols, channels = x_ref.shape
    copies = [
        pltpu.make_async_copy(win_hbm, win_ref, sems.at[0]),
        pltpu.make_async_copy(wout_hbm, wout_ref, sems.at[1]),
    ]
    for copy in copies:
        copy.start()

    def tile(t, carry):
        at = tile_at(t)
        for b in range(images):
            xs = [x_ref[b, r, :, at].astype(F32) for r in range(rows)]
            outs = [None] * rows
            for j in range(TAPS):
                ws = [kw_ref[i * TAPS + j, :, at] for i in range(TAPS)]
                for r in range(rows):
                    total = None
                    for i in range(TAPS):
                        if 0 <= r + i - SIDE < rows:
                            term = ws[i] * xs[r + i - SIDE]
                            total = term if total is None else total + term
                    if j != SIDE:
                        total = pltpu.roll(total, (SIDE - j) % cols, 0)
                    outs[r] = total if outs[r] is None else outs[r] + total
            for r in range(rows):
                part_ref[b, r, :, at] = outs[r]
        return carry

    lax.fori_loop(0, channels // LANES, tile, 0)
    for copy in copies:
        copy.wait()


def gelu_tanh(values):
    return 0.5 * values * (1.0 + jnp.tanh(GELU_C * (values + 0.044715 * values * values * values)))


def gelu_slope(values):
    tangent = jnp.tanh(GELU_C * (values + 0.044715 * values * values * values))
    return 0.5 * (1.0 + tangent) + 0.5 * values * (1.0 - tangent * tangent) * GELU_C * (
        1.0 + 3.0 * 0.044715 * values * values
    )


def three_terms(value):
    high = value.astype(BF).astype(F32)
    rest = value - high
    mid = rest.astype(BF).astype(F32)
    return high, mid, rest - mid


def forward_body(
    part_ref, below_ref, above_ref, kw_ref, x_ref, win_ref, wout_ref,
    sums_ref, normed_ref, inv_ref, hid_ref, before_ref, after_ref, conv_ref, cast_ref,
):
    images, rows, cols, channels = x_ref.shape
    hidden_units = win_ref.shape[1]
    pixels = rows * cols
    place = lax.axis_index("space")
    zeros = jnp.zeros((cols, channels), BF)
    for b in range(images):
        for q in range(SIDE):
            before_ref[b, q] = jnp.where(place > 0, below_ref[b, q], zeros)
            after_ref[b, q] = jnp.where(
                place < lax.axis_size("space") - 1, above_ref[b, q], zeros
            )

    def tile(t, carry):
        at = tile_at(t)
        for b in range(images):
            heads = [before_ref[b, q, :, at].astype(F32) for q in range(SIDE)]
            tails = [after_ref[b, q, :, at].astype(F32) for q in range(SIDE)]
            outs = [part_ref[b, r, :, at] for r in range(rows)]
            for j in range(TAPS):
                ws = [kw_ref[i * TAPS + j, :, at] for i in range(TAPS)]
                for r in list(range(SIDE)) + list(range(rows - SIDE, rows)):
                    total = None
                    for i in range(TAPS):
                        q = r + i
                        if q < SIDE:
                            term = ws[i] * heads[q]
                        elif q >= rows + SIDE:
                            term = ws[i] * tails[q - rows - SIDE]
                        else:
                            continue
                        total = term if total is None else total + term
                    if j != SIDE:
                        total = pltpu.roll(total, (SIDE - j) % cols, 0)
                    outs[r] = outs[r] + total
            for r in range(rows):
                conv_ref[pl.ds((b * rows + r) * cols, cols), at] = outs[r]
        return carry

    lax.fori_loop(0, channels // LANES, tile, 0)

    for start in range(0, images * pixels, 32):
        some = pl.ds(start, 32)
        conv_out = conv_ref[some, :]
        center = conv_out - jnp.mean(conv_out, axis=-1, keepdims=True)
        inv = lax.rsqrt(jnp.mean(center * center, axis=-1, keepdims=True) + EPS)
        normed = center * inv
        normed_ref[some, :] = normed
        inv_ref[some, :] = jnp.broadcast_to(inv, (32, LANES))
        cast_ref[some, :] = normed.astype(BF)

    width = 256
    mixed = jnp.zeros((8, channels), F32)
    for start in range(0, hidden_units, width):
        some = pl.ds(start, width)
        hidden = jnp.dot(cast_ref[...], win_ref[:, some], preferred_element_type=F32)
        hid_ref[:, some] = hidden
        activated = gelu_tanh(hidden).astype(BF).astype(F32)
        listed = []
        for b in range(images):
            total = jnp.sum(activated[b * pixels : (b + 1) * pixels], axis=0, keepdims=True)
            listed.extend(three_terms(total))
        listed.append(jnp.zeros((8 - 3 * images, width), F32))
        terms = jnp.concatenate(listed, axis=0).astype(BF)
        mixed = mixed + jnp.dot(terms, wout_ref[some, :], preferred_element_type=F32)
    for b in range(images):
        own = x_ref[b, 0].astype(F32)
        for r in range(1, rows):
            own = own + x_ref[b, r].astype(F32)
        sums_ref[b : b + 1, :] = jnp.sum(own, axis=0, keepdims=True) + jnp.sum(
            mixed[3 * b : 3 * b + 3], axis=0, keepdims=True
        )


def slope_body(hid_ref, slope_ref):
    for start in range(0, hid_ref.shape[1], 256):
        some = pl.ds(start, 256)
        slope_ref[:, some] = gelu_slope(hid_ref[:, some])


def unit_rows(values):
    norms = jnp.sqrt(jnp.sum(values * values, axis=-1, keepdims=True) + EPS)
    return (values / norms, norms)


def kernel_sums(grad_ref, x_ref, before_ref, after_ref, list_ref, half):
    images, rows, cols, channels = x_ref.shape
    masks = column_masks(cols)
    tiles = channels // LANES // 2

    def tile(t, carry):
        at = tile_at(half * tiles + t)
        for j in range(TAPS):
            sums = [None] * TAPS
            for b in range(images):
                grads = []
                for r in range(rows):
                    grad = grad_ref[pl.ds((b * rows + r) * cols, cols), at]
                    grads.append(grad if j == SIDE else pltpu.roll(grad, (j - SIDE) % cols, 0))
                for q in range(rows + 2 * SIDE):
                    if q < SIDE:
                        here = before_ref[b, q, :, at]
                    elif q < rows + SIDE:
                        here = x_ref[b, q - SIDE, :, at]
                    else:
                        here = after_ref[b, q - rows - SIDE, :, at]
                    here = here.astype(F32)
                    for i in range(TAPS):
                        if 0 <= q - i < rows:
                            term = here * grads[q - i]
                            sums[i] = term if sums[i] is None else sums[i] + term
            for i in range(TAPS):
                kept = jnp.where(masks[j], sums[i], 0.0)
                list_ref[pl.ds(t * TAPS * TAPS + i * TAPS + j, 1), :] = jnp.sum(
                    kept, axis=0, keepdims=True
                )
        return carry

    list_ref[...] = jnp.zeros_like(list_ref)
    lax.fori_loop(0, tiles, tile, 0)


def backward_body(
    scene_pixels, total_ref, caps_ref, pos_ref, slope_ref, normed_ref, inv_ref, win_ref, wout_ref,
    x_ref, before_ref, after_ref,
    grad_ref, pay_ref, list_ref, hg_ref, row_ref,
):
    images, rows, cols, channels = x_ref.shape
    pixels = rows * cols
    count = caps_ref.shape[0]
    pooled = total_ref[...] / scene_pixels
    image_unit, pooled_norm = unit_rows(pooled)
    image_cast = image_unit.astype(BF)
    text_unit, _ = unit_rows(caps_ref[...].astype(F32))
    text_cast = text_unit.astype(BF)
    logits = (
        LOGIT_SCALE
        * lax.dot_general(
            image_cast, text_cast, (((1,), (1,)), ((), ())), preferred_element_type=F32
        )
        + LOGIT_BIAS
    )
    row_at = lax.broadcasted_iota(jnp.int32, (images, count), 0)
    positive = jnp.zeros((images, count), jnp.int32)
    for b in range(images):
        positive = jnp.where(row_at == b, pos_ref[b], positive)
    place = lax.broadcasted_iota(jnp.int32, (images, count), 1)
    core = (place >= count // 2).astype(jnp.int32)
    rest = place - core * (count // 2)
    group = rest // images
    caption = (group * 2 + core) * images + (rest - group * images)
    labels = jnp.where(positive == caption, 1.0, -1.0).astype(F32)
    margin = -labels * logits
    losses = jnp.maximum(margin, 0.0) + jnp.log(1.0 + jnp.exp(-jnp.abs(margin)))
    loss_part = jnp.sum(jnp.sum(losses, axis=1, keepdims=True), axis=0, keepdims=True)
    pair_grad = (-labels / (1.0 + jnp.exp(-margin))).astype(BF)
    image_side = LOGIT_SCALE * jnp.dot(pair_grad, text_cast, preferred_element_type=F32)
    pooled_grad = (
        image_side - image_unit * jnp.sum(image_unit * image_side, axis=-1, keepdims=True)
    ) / pooled_norm
    slope = (pooled_grad / scene_pixels).astype(BF)
    act_grad = lax.dot_general(
        slope, wout_ref[...], (((1,), (1,)), ((), ())), preferred_element_type=F32
    )
    for b in range(images):
        some = pl.ds(b * pixels, pixels)
        hg_ref[some, :] = (act_grad[b : b + 1] * slope_ref[some, :]).astype(BF)
    normed_grad = lax.dot_general(
        hg_ref[...], win_ref[...], (((1,), (1,)), ((), ())), preferred_element_type=F32
    )
    normed = normed_ref[...]
    grad_ref[...] = inv_ref[:, 0:1] * (
        normed_grad
        - jnp.mean(normed_grad, axis=-1, keepdims=True)
        - normed * jnp.mean(normed_grad * normed, axis=-1, keepdims=True)
    )
    half = 1 - lax.rem(lax.axis_index("dp"), 2)
    kernel_sums(grad_ref, x_ref, before_ref, after_ref, list_ref, half)
    listed = list_ref.shape[0]
    pay_ref[0:listed, :] = list_ref[...].astype(BF)

    row_ref[...] = jnp.zeros_like(row_ref)
    chunks = channels // LANES
    high, mid, low = three_terms(loss_part)
    lane = lax.broadcasted_iota(jnp.int32, (1, LANES), 1)
    for b in range(images):
        for c in range(chunks):
            row_ref[b * (chunks + 1) + c : b * (chunks + 1) + c + 1, :] = image_cast[
                b : b + 1, c * LANES : (c + 1) * LANES
            ].astype(F32)
        at = b * (chunks + 1) + chunks
        row_ref[at : at + 1, 0:count] = pair_grad[b : b + 1, :].astype(F32)
        if b == 0:
            known = row_ref[at : at + 1, :]
            known = jnp.where(lane == LANES - 3, high, known)
            known = jnp.where(lane == LANES - 2, mid, known)
            known = jnp.where(lane == LANES - 1, low, known)
            row_ref[at : at + 1, :] = known
    pay_ref[listed:, :] = row_ref[...].astype(BF)


def own_half_body(grad_ref, x_ref, before_ref, after_ref, list_ref):
    half = lax.rem(lax.axis_index("dp"), 2)
    kernel_sums(grad_ref, x_ref, before_ref, after_ref, list_ref, half)


def text_body(rows_ref, caps_ref, text_ref, loss_ref, wide_ref):
    images, channels = caps_ref.shape
    chunks = channels // LANES
    stride = wide_ref.shape[0] // lax.axis_size("dp")
    groups = lax.axis_size("dp")
    wide_ref[...] = rows_ref[...].astype(F32)
    lane = lax.broadcasted_iota(jnp.int32, (groups, LANES), 1)
    me = lax.axis_index("dp")
    first = (lax.rem(me, 2) * (groups // 2) + me // 2) * images
    caption_side = [[jnp.zeros((1, LANES), F32) for _ in range(chunks)] for _ in range(images)]
    loss = jnp.zeros((1, 1), F32)
    for b in range(images):
        base = b * (chunks + 1)
        pairs = wide_ref[pl.ds(base + chunks, groups, stride=stride), :]
        if b == 0:
            terms = jnp.where(lane >= LANES - 3, pairs, 0.0)
            loss = jnp.sum(jnp.sum(terms, axis=1, keepdims=True), axis=0, keepdims=True)
        weights = [
            jnp.sum(jnp.where(lane == first + k, pairs, 0.0), axis=1, keepdims=True)
            for k in range(images)
        ]
        for c in range(chunks):
            unit = wide_ref[pl.ds(base + c, groups, stride=stride), :]
            for k in range(images):
                caption_side[k][c] = caption_side[k][c] + jnp.sum(
                    weights[k] * unit, axis=0, keepdims=True
                )
    loss_ref[...] = loss / (groups * images)
    text_unit, text_norm = unit_rows(caps_ref[...].astype(F32))
    for k in range(images):
        side = LOGIT_SCALE * jnp.concatenate(caption_side[k], axis=1)
        unit = text_unit[k : k + 1]
        text_ref[k : k + 1, :] = (
            side - unit * jnp.sum(unit * side, axis=-1, keepdims=True)
        ) / text_norm[k : k + 1]


def merge_body(own_ref, other_ref, out_ref, wide_ref):
    tiles = out_ref.shape[2] // LANES // 2
    half = lax.rem(lax.axis_index("dp"), 2)
    for source, side in ((own_ref, half), (other_ref, 1 - half)):
        wide_ref[...] = source[...].astype(F32)
        for t in range(tiles):
            at = tile_at(side * tiles + t)
            for i in range(TAPS):
                out_ref[i, :, at] = wide_ref[pl.ds((t * TAPS + i) * TAPS, TAPS), :]


def shifted(array, axis, stride, step, size=4):
    pairs = []
    for i in range(lax.axis_size(axis)):
        place = i // stride % size
        pairs.append((i, i + ((place + step) % size - place) * stride))
    return lax.ppermute(array, axis, pairs)


def flip(array, axis, mask):
    return lax.ppermute(array, axis, [(i, i ^ mask) for i in range(lax.axis_size(axis))])


def groups(size, stride):
    listed = []
    while stride < size:
        members = 4 if size // stride % 4 == 0 else 2
        listed.append((stride, members))
        stride *= members
    return listed


def bits(axis):
    size = lax.axis_size(axis)
    return [1 << k for k in range(size.bit_length() - 1)]


def join(mine, theirs, axis, bit):
    upper = lax.rem(lax.axis_index(axis) // bit, 2) == 1
    return jnp.where(
        upper,
        jnp.concatenate([theirs, mine], axis=0),
        jnp.concatenate([mine, theirs], axis=0),
    )


def rounded(values):
    return lax.reduce_precision(values, 8, 7).astype(BF)


def group_sum(mine, axis, stride, members):
    if members == 2:
        return mine.astype(F32) + flip(mine, axis, stride).astype(F32)
    one, two, three = [shifted(mine, axis, stride, k).astype(F32) for k in (1, 2, 3)]
    return (mine.astype(F32) + two) + (one + three)


def per_device(scenes, kernel, weight_in, weight_out, captions, positives):
    images, rows, cols, channels = scenes.shape
    hidden_units = weight_in.shape[1]
    space_count = lax.axis_size("space")
    pixels = images * rows * cols
    scene_pixels = rows * space_count * cols
    edge = (images, SIDE, cols, channels)

    x, first, last, spread, own_captions = call(
        load_body,
        [
            (scenes.shape, BF),
            (edge, BF),
            (edge, BF),
            ((TAPS * TAPS, cols, channels), F32),
            (captions.shape, BF),
        ],
        [scenes, kernel, captions],
        scratch=[pltpu.VMEM(kernel.shape, BF), pltpu.SemaphoreType.DMA((5,))],
        hbm=(0, 1, 2),
    )
    below = shifted(last, "space", 1, 1, space_count)
    above = shifted(first, "space", 1, space_count - 1, space_count)
    theirs = captions
    gathered = own_captions
    for bit in bits("dp")[1:] + [1]:
        theirs = flip(theirs, "dp", bit)
        gathered = theirs = join(gathered, theirs, "dp", bit)
    part, win, wout = call(
        conv_body,
        [
            (scenes.shape, F32),
            (weight_in.shape, BF),
            (weight_out.shape, BF),
        ],
        [x, spread, weight_in, weight_out],
        scratch=[pltpu.SemaphoreType.DMA((2,))],
        hbm=(2, 3),
    )

    sums, normed, inv, hidden, before, after = call(
        forward_body,
        [
            ((images, channels), F32),
            ((pixels, channels), F32),
            ((pixels, LANES), F32),
            ((pixels, hidden_units), F32),
            (edge, BF),
            (edge, BF),
        ],
        [part, below, above, spread, x, win, wout],
        scratch=[pltpu.VMEM((pixels, channels), F32), pltpu.VMEM((pixels, channels), BF)],
    )
    for stride, members in groups(space_count, 1):
        sums = group_sum(sums, "space", stride, members)
    (slope,) = call(slope_body, [((pixels, hidden_units), F32)], [hidden])

    listed = channels // LANES // 2 * TAPS * TAPS
    listed += -listed % 16
    own_rows = images * (channels // LANES + 1)
    own_rows += -own_rows % 16
    grad, pay = call(
        functools.partial(backward_body, scene_pixels),
        [((pixels, channels), F32), ((listed + own_rows, LANES), BF)],
        [sums, gathered, positives, slope, normed, inv, win, wout, x, before, after],
        scratch=[
            pltpu.VMEM((listed, LANES), F32),
            pltpu.VMEM((pixels, hidden_units), BF),
            pltpu.VMEM((own_rows, LANES), F32),
        ],
        smem=(2,),
    )
    other = flip(pay, "dp", 1)
    (own,) = call(
        own_half_body, [((listed, LANES), F32)], [grad, x, before, after]
    )
    total = own + other[:listed].astype(F32)
    units = join(pay[listed:], other[listed:], "dp", 1)
    for stride, members in groups(lax.axis_size("dp"), 2):
        mine = rounded(total)
        both = jnp.concatenate([mine, units], axis=0)
        near = flip(both, "dp", stride)
        total = mine.astype(F32) + near[:listed].astype(F32)
        joined = join(units, near[listed:], "dp", stride)
        if members == 4:
            far = flip(both, "dp", 2 * stride)
            cross = flip(both, "dp", 3 * stride)
            total = total + (far[:listed].astype(F32) + cross[:listed].astype(F32))
            joined = join(
                joined, join(far[listed:], cross[listed:], "dp", stride), "dp", 2 * stride
            )
        units = joined
    text_grad, loss = call(
        text_body,
        [((images, channels), F32), ((1, 1), F32)],
        [units, own_captions],
        scratch=[pltpu.VMEM(units.shape, F32)],
    )
    for stride, members in groups(space_count, 1):
        total = group_sum(rounded(total), "space", stride, members)
    mine = rounded(total)
    other = flip(mine, "dp", 1)
    (kernel_grad,) = call(
        merge_body,
        [((TAPS, TAPS, channels), F32)],
        [mine, other],
        scratch=[pltpu.VMEM((listed, LANES), F32)],
    )
    return (loss.reshape(()), text_grad, kernel_grad)


def solution(mesh):
    return jax.shard_map(
        per_device,
        mesh=mesh,
        in_specs=(P("dp", "space", None, None), P(), P(), P(), P("dp", None), P("dp")),
        out_specs=(P(), P("dp", None), P()),
        check_vma=False,
    )
```

```python
import functools

import jax
import jax.numpy as jnp
from jax import lax
from jax.experimental import pallas as pl
from jax.experimental.pallas import tpu as pltpu
from jax.sharding import PartitionSpec as P

EPS = 1e-06
LOGIT_SCALE = 10.0
LOGIT_BIAS = -1.0
GELU_C = 0.7978845608028654
TAPS = 7
SIDE = 3
LANES = 128
BF = jnp.bfloat16
F32 = jnp.float32


def in_vmem(array):
    return pltpu.with_memory_space_constraint(array, pltpu.VMEM)


def vmem_out(shape, dtype):
    return pltpu.VMEM(shape, dtype)


def in_hbm(array):
    return pltpu.with_memory_space_constraint(array, pltpu.HBM)


def call(body, outs, args, scratch=(), smem=(), hbm=(), limit=10, placed_out=vmem_out):
    specs = []
    placed = []
    for k, arg in enumerate(args):
        if k in smem:
            specs.append(pl.BlockSpec(memory_space=pltpu.SMEM))
            placed.append(arg)
        elif k in hbm:
            specs.append(pl.BlockSpec(memory_space=pl.ANY))
            placed.append(in_hbm(arg))
        else:
            specs.append(pl.BlockSpec(memory_space=pltpu.VMEM))
            placed.append(in_vmem(arg))
    return pl.pallas_call(
        body,
        out_shape=[placed_out(shape, dtype) for shape, dtype in outs],
        in_specs=specs,
        out_specs=[pl.BlockSpec(memory_space=pltpu.VMEM) for _ in outs],
        scratch_shapes=list(scratch),
        compiler_params=pltpu.CompilerParams(vmem_limit_bytes=limit * 1024 * 1024),
        cost_estimate=pl.CostEstimate(flops=0, bytes_accessed=0, transcendentals=0),
    )(*placed)


def column_masks(cols, lanes=LANES):
    at = lax.broadcasted_iota(jnp.int32, (cols, lanes), 0)
    return [
        (at - (j - SIDE) >= 0) & (at - (j - SIDE) < cols) for j in range(TAPS)
    ]


def tile_at(t):
    return pl.ds(pl.multiple_of(t * LANES, LANES), LANES)


def own_half():
    me = lax.axis_index("dp")
    odd = 0
    for k in range(lax.axis_size("dp").bit_length() - 1):
        odd = odd + lax.rem(me // (1 << k), 2)
    return lax.rem(odd, 2)


def load_body(
    x_hbm, k_hbm, caps_hbm, x_ref, first_ref, last_ref, taps_ref, caps_ref, sems
):
    rows, cols, channels = x_hbm.shape[1:]
    copies = [
        pltpu.make_async_copy(k_hbm, taps_ref, sems.at[0]),
        pltpu.make_async_copy(x_hbm.at[:, :SIDE], first_ref, sems.at[1]),
        pltpu.make_async_copy(x_hbm.at[:, rows - SIDE :], last_ref, sems.at[2]),
        pltpu.make_async_copy(x_hbm, x_ref, sems.at[3]),
        pltpu.make_async_copy(caps_hbm, caps_ref, sems.at[4]),
    ]
    for copy in copies:
        copy.start()
    for copy in copies:
        copy.wait()


def conv_body(
    x_ref, taps_ref, caps_ref, win_hbm, wout_hbm, part_ref, win_ref, wout_ref, same_caps_ref,
    kw_ref, sems,
):
    images, rows, cols, channels = x_ref.shape
    copies = [
        pltpu.make_async_copy(win_hbm, win_ref, sems.at[0]),
        pltpu.make_async_copy(wout_hbm, wout_ref, sems.at[1]),
    ]
    for copy in copies:
        copy.start()
    same_caps_ref[...] = caps_ref[...]
    masks = column_masks(cols, channels)
    for i in range(TAPS):
        taps = taps_ref[i].astype(F32)
        for j in range(TAPS):
            spread = jnp.broadcast_to(taps[j : j + 1], (cols, channels))
            kw_ref[i * TAPS + j] = jnp.where(masks[j], spread, 0.0)

    def tile(t, carry):
        at = tile_at(t)
        for b in range(images):
            xs = [x_ref[b, r, :, at].astype(F32) for r in range(rows)]
            outs = [None] * rows
            for j in range(TAPS):
                ws = [kw_ref[i * TAPS + j, :, at] for i in range(TAPS)]
                for r in range(rows):
                    total = None
                    for i in range(TAPS):
                        if 0 <= r + i - SIDE < rows:
                            term = ws[i] * xs[r + i - SIDE]
                            total = term if total is None else total + term
                    if j != SIDE:
                        total = pltpu.roll(total, (SIDE - j) % cols, 0)
                    outs[r] = total if outs[r] is None else outs[r] + total
            for r in range(rows):
                part_ref[b, r, :, at] = outs[r]
        return carry

    lax.fori_loop(0, channels // LANES, tile, 0)
    for copy in copies:
        copy.wait()


def gelu_tanh(values):
    return 0.5 * values * (1.0 + jnp.tanh(GELU_C * (values + 0.044715 * values * values * values)))


def gelu_slope(values):
    tangent = jnp.tanh(GELU_C * (values + 0.044715 * values * values * values))
    return 0.5 * (1.0 + tangent) + 0.5 * values * (1.0 - tangent * tangent) * GELU_C * (
        1.0 + 3.0 * 0.044715 * values * values
    )


def three_terms(value):
    high = value.astype(BF).astype(F32)
    rest = value - high
    mid = rest.astype(BF).astype(F32)
    return high, mid, rest - mid


def forward_body(
    part_ref, below_ref, above_ref, kw_ref, x_ref, win_ref, wout_ref, caps_ref,
    sums_ref, normed_ref, inv_ref, hid_ref, before_ref, after_ref, same_caps_ref,
    conv_ref, cast_ref, act_ref,
):
    images, rows, cols, channels = x_ref.shape
    hidden_units = win_ref.shape[1]
    pixels = rows * cols
    place = lax.axis_index("space")
    zeros = jnp.zeros((cols, channels), BF)
    for b in range(images):
        for q in range(SIDE):
            before_ref[b, q] = jnp.where(place > 0, below_ref[b, q], zeros)
            after_ref[b, q] = jnp.where(
                place < lax.axis_size("space") - 1, above_ref[b, q], zeros
            )

    def tile(t, carry):
        at = tile_at(t)
        for b in range(images):
            heads = [before_ref[b, q, :, at].astype(F32) for q in range(SIDE)]
            tails = [after_ref[b, q, :, at].astype(F32) for q in range(SIDE)]
            outs = [part_ref[b, r, :, at] for r in range(rows)]
            for j in range(TAPS):
                ws = [kw_ref[i * TAPS + j, :, at] for i in range(TAPS)]
                for r in list(range(SIDE)) + list(range(rows - SIDE, rows)):
                    total = None
                    for i in range(TAPS):
                        q = r + i
                        if q < SIDE:
                            term = ws[i] * heads[q]
                        elif q >= rows + SIDE:
                            term = ws[i] * tails[q - rows - SIDE]
                        else:
                            continue
                        total = term if total is None else total + term
                    if j != SIDE:
                        total = pltpu.roll(total, (SIDE - j) % cols, 0)
                    outs[r] = outs[r] + total
            for r in range(rows):
                conv_ref[pl.ds((b * rows + r) * cols, cols), at] = outs[r]
        return carry

    lax.fori_loop(0, channels // LANES, tile, 0)

    for start in range(0, images * pixels, 32):
        some = pl.ds(start, 32)
        conv_out = conv_ref[some, :]
        center = conv_out - jnp.mean(conv_out, axis=-1, keepdims=True)
        inv = lax.rsqrt(jnp.mean(center * center, axis=-1, keepdims=True) + EPS)
        normed = center * inv
        normed_ref[some, :] = normed
        inv_ref[some, :] = jnp.broadcast_to(inv, (32, LANES))
        cast_ref[some, :] = normed.astype(BF)

    same_caps_ref[...] = caps_ref[...]
    width = 256
    for start in range(0, hidden_units, width):
        some = pl.ds(start, width)
        hidden = jnp.dot(cast_ref[...], win_ref[:, some], preferred_element_type=F32)
        hid_ref[:, some] = hidden
        activated = gelu_tanh(hidden).astype(BF).astype(F32)
        listed = []
        for b in range(images):
            total = jnp.sum(activated[b * pixels : (b + 1) * pixels], axis=0, keepdims=True)
            listed.extend(three_terms(total))
        listed.append(jnp.zeros((act_ref.shape[0] - 3 * images, width), F32))
        act_ref[:, some] = jnp.concatenate(listed, axis=0)
    mixed = jnp.dot(act_ref[...].astype(BF), wout_ref[...], preferred_element_type=F32)
    for b in range(images):
        own = x_ref[b, 0].astype(F32)
        for r in range(1, rows):
            own = own + x_ref[b, r].astype(F32)
        sums_ref[b : b + 1, :] = jnp.sum(own, axis=0, keepdims=True) + jnp.sum(
            mixed[3 * b : 3 * b + 3], axis=0, keepdims=True
        )


def slope_body(hid_ref, slope_ref):
    for start in range(0, hid_ref.shape[1], 256):
        some = pl.ds(start, 256)
        slope_ref[:, some] = gelu_slope(hid_ref[:, some])


def unit_rows(values):
    norms = jnp.sqrt(jnp.sum(values * values, axis=-1, keepdims=True) + EPS)
    return (values / norms, norms)


def joined(bit, mine_ref, theirs_ref):
    upper = lax.rem(lax.axis_index("dp") // bit, 2) == 1
    mine, theirs = mine_ref[...].astype(F32), theirs_ref[...].astype(F32)
    return jnp.concatenate(
        [jnp.where(upper, theirs, mine), jnp.where(upper, mine, theirs)], axis=0
    )


def join_body(bit, mine_ref, theirs_ref, out_ref):
    out_ref[...] = joined(bit, mine_ref, theirs_ref).astype(BF)


def text_cast_body(bit, mine_ref, theirs_ref, cast_ref):
    cast_ref[...] = unit_rows(joined(bit, mine_ref, theirs_ref))[0].astype(BF)


def kernel_sums(grad_ref, x_ref, before_ref, after_ref, list_ref, half):
    images, rows, cols, channels = x_ref.shape
    masks = column_masks(cols)
    tiles = channels // LANES // 2

    def tile(t, carry):
        at = tile_at(half * tiles + t)
        for j in range(TAPS):
            sums = [None] * TAPS
            for b in range(images):
                grads = []
                for r in range(rows):
                    grad = grad_ref[pl.ds((b * rows + r) * cols, cols), at]
                    grads.append(grad if j == SIDE else pltpu.roll(grad, (j - SIDE) % cols, 0))
                for q in range(rows + 2 * SIDE):
                    if q < SIDE:
                        here = before_ref[b, q, :, at]
                    elif q < rows + SIDE:
                        here = x_ref[b, q - SIDE, :, at]
                    else:
                        here = after_ref[b, q - rows - SIDE, :, at]
                    here = here.astype(F32)
                    for i in range(TAPS):
                        if 0 <= q - i < rows:
                            term = here * grads[q - i]
                            sums[i] = term if sums[i] is None else sums[i] + term
            for i in range(TAPS):
                kept = jnp.where(masks[j], sums[i], 0.0)
                list_ref[pl.ds(t * TAPS * TAPS + i * TAPS + j, 1), :] = jnp.sum(
                    kept, axis=0, keepdims=True
                )
        return carry

    list_ref[...] = jnp.zeros_like(list_ref)
    lax.fori_loop(0, tiles, tile, 0)


def backward_body(
    scene_pixels, text_ref, pos_ref, slope_ref, normed_ref, inv_ref, win_ref, wout_ref,
    x_ref, before_ref, after_ref, *refs,
):
    *part_refs, grad_ref, pay_ref, list_ref, hg_ref, row_ref = refs
    images, rows, cols, channels = x_ref.shape
    pixels = rows * cols
    count = text_ref.shape[0]
    pooled = pair_sum([ref[...] for ref in part_refs]) / scene_pixels
    image_unit, pooled_norm = unit_rows(pooled)
    image_cast = image_unit.astype(BF)
    text_cast = text_ref[...]
    logits = (
        LOGIT_SCALE
        * lax.dot_general(
            image_cast, text_cast, (((1,), (1,)), ((), ())), preferred_element_type=F32
        )
        + LOGIT_BIAS
    )
    row_at = lax.broadcasted_iota(jnp.int32, (images, count), 0)
    positive = jnp.zeros((images, count), jnp.int32)
    for b in range(images):
        positive = jnp.where(row_at == b, pos_ref[b], positive)
    place = lax.broadcasted_iota(jnp.int32, (images, count), 1)
    core = (place >= count // 2).astype(jnp.int32)
    rest = place - core * (count // 2)
    group = rest // images
    caption = (group * 2 + core) * images + (rest - group * images)
    labels = jnp.where(positive == caption, 1.0, -1.0).astype(F32)
    margin = -labels * logits
    losses = jnp.maximum(margin, 0.0) + jnp.log(1.0 + jnp.exp(-jnp.abs(margin)))
    loss_part = jnp.sum(jnp.sum(losses, axis=1, keepdims=True), axis=0, keepdims=True)
    pair_grad = (-labels / (1.0 + jnp.exp(-margin))).astype(BF)
    image_side = LOGIT_SCALE * jnp.dot(pair_grad, text_cast, preferred_element_type=F32)
    pooled_grad = (
        image_side - image_unit * jnp.sum(image_unit * image_side, axis=-1, keepdims=True)
    ) / pooled_norm
    slope = (pooled_grad / scene_pixels).astype(BF)
    act_grad = lax.dot_general(
        slope, wout_ref[...], (((1,), (1,)), ((), ())), preferred_element_type=F32
    )
    for b in range(images):
        some = pl.ds(b * pixels, pixels)
        hg_ref[some, :] = (act_grad[b : b + 1] * slope_ref[some, :]).astype(BF)
    normed_grad = lax.dot_general(
        hg_ref[...], win_ref[...], (((1,), (1,)), ((), ())), preferred_element_type=F32
    )
    normed = normed_ref[...]
    grad_ref[...] = inv_ref[:, 0:1] * (
        normed_grad
        - jnp.mean(normed_grad, axis=-1, keepdims=True)
        - normed * jnp.mean(normed_grad * normed, axis=-1, keepdims=True)
    )
    half = 1 - own_half()
    kernel_sums(grad_ref, x_ref, before_ref, after_ref, list_ref, half)
    listed = list_ref.shape[0]
    pay_ref[0:listed, :] = list_ref[...].astype(BF)

    row_ref[...] = jnp.zeros_like(row_ref)
    chunks = channels // LANES
    high, mid, low = three_terms(loss_part)
    lane = lax.broadcasted_iota(jnp.int32, (1, LANES), 1)
    for b in range(images):
        for c in range(chunks):
            row_ref[b * (chunks + 1) + c : b * (chunks + 1) + c + 1, :] = image_cast[
                b : b + 1, c * LANES : (c + 1) * LANES
            ].astype(F32)
        at = b * (chunks + 1) + chunks
        row_ref[at : at + 1, 0:count] = pair_grad[b : b + 1, :].astype(F32)
        if b == 0:
            known = row_ref[at : at + 1, :]
            known = jnp.where(lane == LANES - 3, high, known)
            known = jnp.where(lane == LANES - 2, mid, known)
            known = jnp.where(lane == LANES - 1, low, known)
            row_ref[at : at + 1, :] = known
    pay_ref[listed:, :] = row_ref[...].astype(BF)


def own_half_body(grad_ref, x_ref, before_ref, after_ref, list_ref):
    half = own_half()
    kernel_sums(grad_ref, x_ref, before_ref, after_ref, list_ref, half)


def text_body(rows_ref, caps_ref, text_ref, loss_ref, wide_ref):
    images, channels = caps_ref.shape
    chunks = channels // LANES
    stride = wide_ref.shape[0] // lax.axis_size("dp")
    groups = lax.axis_size("dp")
    wide_ref[...] = rows_ref[...].astype(F32)
    lane = lax.broadcasted_iota(jnp.int32, (groups, LANES), 1)
    me = lax.axis_index("dp")
    first = (lax.rem(me, 2) * (groups // 2) + me // 2) * images
    caption_side = [[jnp.zeros((1, LANES), F32) for _ in range(chunks)] for _ in range(images)]
    loss = jnp.zeros((1, 1), F32)
    for b in range(images):
        base = b * (chunks + 1)
        pairs = wide_ref[pl.ds(base + chunks, groups, stride=stride), :]
        if b == 0:
            terms = jnp.where(lane >= LANES - 3, pairs, 0.0)
            loss = jnp.sum(jnp.sum(terms, axis=1, keepdims=True), axis=0, keepdims=True)
        weights = [
            jnp.sum(jnp.where(lane == first + k, pairs, 0.0), axis=1, keepdims=True)
            for k in range(images)
        ]
        for c in range(chunks):
            unit = wide_ref[pl.ds(base + c, groups, stride=stride), :]
            for k in range(images):
                caption_side[k][c] = caption_side[k][c] + jnp.sum(
                    weights[k] * unit, axis=0, keepdims=True
                )
    loss_ref[...] = loss / (groups * images)
    text_unit, text_norm = unit_rows(caps_ref[...].astype(F32))
    for k in range(images):
        side = LOGIT_SCALE * jnp.concatenate(caption_side[k], axis=1)
        unit = text_unit[k : k + 1]
        text_ref[k : k + 1, :] = (
            side - unit * jnp.sum(unit * side, axis=-1, keepdims=True)
        ) / text_norm[k : k + 1]


def merge_body(own_ref, other_ref, out_ref, wide_ref):
    tiles = out_ref.shape[2] // LANES // 2
    half = own_half()
    for source, side in ((own_ref, half), (other_ref, 1 - half)):
        wide_ref[...] = source[...].astype(F32)
        for t in range(tiles):
            at = tile_at(side * tiles + t)
            for i in range(TAPS):
                out_ref[i, :, at] = wide_ref[pl.ds((t * TAPS + i) * TAPS, TAPS), :]


def shifted(array, axis, stride, step, size=4):
    pairs = []
    for i in range(lax.axis_size(axis)):
        place = i // stride % size
        pairs.append((i, i + ((place + step) % size - place) * stride))
    return lax.ppermute(array, axis, pairs)


def flip(array, axis, mask):
    return lax.ppermute(array, axis, [(i, i ^ mask) for i in range(lax.axis_size(axis))])


def groups(size, stride):
    listed = []
    while stride < size:
        members = 4 if size // stride % 4 == 0 else 2
        listed.append((stride, members))
        stride *= members
    return listed


def bits(axis):
    size = lax.axis_size(axis)
    return [1 << k for k in range(size.bit_length() - 1)]


def join(mine, theirs, axis, bit):
    upper = lax.rem(lax.axis_index(axis) // bit, 2) == 1
    return jnp.where(
        upper,
        jnp.concatenate([theirs, mine], axis=0),
        jnp.concatenate([mine, theirs], axis=0),
    )


def rounded(values):
    return lax.reduce_precision(values, 8, 7).astype(BF)


def group_parts(mine, axis, stride, members):
    if members == 2:
        return [mine, flip(mine, axis, stride)]
    one, two, three = [shifted(mine, axis, stride, k) for k in (1, 2, 3)]
    return [mine, two, one, three]


def pair_sum(parts):
    parts = [part.astype(F32) for part in parts]
    while len(parts) > 1:
        parts = [parts[k] + parts[k + 1] for k in range(0, len(parts), 2)]
    return parts[0]


def group_sum(mine, axis, stride, members):
    return pair_sum(group_parts(mine, axis, stride, members))


def rows_joined(body, mine, theirs, bit):
    shape = (2 * mine.shape[0], mine.shape[1])
    (out,) = call(functools.partial(body, bit), [(shape, BF)], [mine, theirs])
    return out


def per_device(scenes, kernel, weight_in, weight_out, captions, positives):
    images, rows, cols, channels = scenes.shape
    hidden_units = weight_in.shape[1]
    space_count = lax.axis_size("space")
    pixels = images * rows * cols
    scene_pixels = rows * space_count * cols
    edge = (images, SIDE, cols, channels)

    x, first, last, taps, own_captions = call(
        load_body,
        [
            (scenes.shape, BF),
            (edge, BF),
            (edge, BF),
            (kernel.shape, BF),
            (captions.shape, BF),
        ],
        [scenes, kernel, captions],
        scratch=[pltpu.SemaphoreType.DMA((5,))],
        hbm=(0, 1, 2),
    )
    below = shifted(last, "space", 1, 1, space_count)
    above = shifted(first, "space", 1, space_count - 1, space_count)
    dp_bits = bits("dp")
    theirs = flip(captions, "dp", dp_bits[1])
    part, win, wout, same_captions, spread = call(
        conv_body,
        [
            (scenes.shape, F32),
            (weight_in.shape, BF),
            (weight_out.shape, BF),
            (captions.shape, BF),
            ((TAPS * TAPS, cols, channels), F32),
        ],
        [x, taps, own_captions, weight_in, weight_out],
        scratch=[pltpu.SemaphoreType.DMA((2,))],
        hbm=(3, 4),
    )

    gathered = rows_joined(join_body, same_captions, theirs, dp_bits[1])
    theirs = flip(gathered, "dp", dp_bits[2])
    sums, normed, inv, hidden, before, after, gathered = call(
        forward_body,
        [
            ((images, channels), F32),
            ((pixels, channels), F32),
            ((pixels, LANES), F32),
            ((pixels, hidden_units), F32),
            (edge, BF),
            (edge, BF),
            (gathered.shape, BF),
        ],
        [part, below, above, spread, x, win, wout, gathered],
        scratch=[
            pltpu.VMEM((pixels, channels), F32),
            pltpu.VMEM((pixels, channels), BF),
            pltpu.VMEM((3 * images + -3 * images % 8, hidden_units), F32),
        ],
    )
    for bit in dp_bits[2:]:
        gathered = rows_joined(join_body, gathered, theirs, bit)
        theirs = flip(gathered, "dp", 1 if bit == dp_bits[-1] else 2 * bit)
    text_cast = rows_joined(text_cast_body, gathered, theirs, 1)
    space_groups = groups(space_count, 1)
    for stride, members in space_groups[:-1]:
        sums = group_sum(sums, "space", stride, members)
    parts = group_parts(sums, "space", *space_groups[-1])
    (slope,) = call(slope_body, [((pixels, hidden_units), F32)], [hidden])

    listed = channels // LANES // 2 * TAPS * TAPS
    listed += -listed % 16
    own_rows = images * (channels // LANES + 1)
    own_rows += -own_rows % 16
    grad, pay = call(
        functools.partial(backward_body, scene_pixels),
        [((pixels, channels), F32), ((listed + own_rows, LANES), BF)],
        [
            text_cast, positives, slope, normed, inv, weight_in, weight_out, x, before, after,
            *parts,
        ],
        scratch=[
            pltpu.VMEM((listed, LANES), F32),
            pltpu.VMEM((pixels, hidden_units), BF),
            pltpu.VMEM((own_rows, LANES), F32),
        ],
        smem=(1,),
    )
    other = flip(pay, "dp", 1)
    (own,) = call(
        own_half_body, [((listed, LANES), F32)], [grad, x, before, after]
    )
    total = own + other[:listed].astype(F32)
    units = join(pay[listed:], other[listed:], "dp", 1)
    for stride, members in groups(lax.axis_size("dp"), 2):
        mine = rounded(total)
        both = jnp.concatenate([mine, units], axis=0)
        near = flip(both, "dp", stride + 1)
        total = mine.astype(F32) + near[:listed].astype(F32)
        joined = join(units, near[listed:], "dp", stride)
        if members == 4:
            far = flip(both, "dp", 2 * stride + 1)
            cross = flip(both, "dp", 3 * stride)
            total = total + (far[:listed].astype(F32) + cross[:listed].astype(F32))
            joined = join(
                joined, join(far[listed:], cross[listed:], "dp", stride), "dp", 2 * stride
            )
        units = joined
    text_grad, loss = call(
        text_body,
        [((images, channels), F32), ((1, 1), F32)],
        [units, own_captions],
        scratch=[pltpu.VMEM(units.shape, F32)],
        placed_out=jax.ShapeDtypeStruct,
    )
    for stride, members in groups(space_count, 1):
        total = group_sum(rounded(total), "space", stride, members)
    mine = rounded(total)
    other = flip(mine, "dp", 1)
    (kernel_grad,) = call(
        merge_body,
        [((TAPS, TAPS, channels), F32)],
        [mine, other],
        scratch=[pltpu.VMEM((listed, LANES), F32)],
        placed_out=jax.ShapeDtypeStruct,
    )
    return (loss.reshape(()), text_grad, kernel_grad)


def solution(mesh):
    return jax.shard_map(
        per_device,
        mesh=mesh,
        in_specs=(P("dp", "space", None, None), P(), P(), P(), P("dp", None), P("dp")),
        out_specs=(P(), P("dp", None), P()),
        check_vma=False,
    )
```

```python
import functools

import jax
import jax.numpy as jnp
from jax import lax
from jax.experimental import pallas as pl
from jax.experimental.pallas import tpu as pltpu
from jax.sharding import PartitionSpec as P

EPS = 1e-06
LOGIT_SCALE = 10.0
LOGIT_BIAS = -1.0
GELU_C = 0.7978845608028654
TAPS = 7
SIDE = 3
LANES = 128
BF = jnp.bfloat16
F32 = jnp.float32


def in_vmem(array):
    return pltpu.with_memory_space_constraint(array, pltpu.VMEM)


def vmem_out(shape, dtype):
    return pltpu.VMEM(shape, dtype)


def in_hbm(array):
    return pltpu.with_memory_space_constraint(array, pltpu.HBM)


def call(body, outs, args, scratch=(), smem=(), hbm=(), limit=10, placed_out=vmem_out):
    specs = []
    placed = []
    for k, arg in enumerate(args):
        if k in smem:
            specs.append(pl.BlockSpec(memory_space=pltpu.SMEM))
            placed.append(arg)
        elif k in hbm:
            specs.append(pl.BlockSpec(memory_space=pl.ANY))
            placed.append(in_hbm(arg))
        else:
            specs.append(pl.BlockSpec(memory_space=pltpu.VMEM))
            placed.append(in_vmem(arg))
    return pl.pallas_call(
        body,
        out_shape=[placed_out(shape, dtype) for shape, dtype in outs],
        in_specs=specs,
        out_specs=[pl.BlockSpec(memory_space=pltpu.VMEM) for _ in outs],
        scratch_shapes=list(scratch),
        compiler_params=pltpu.CompilerParams(vmem_limit_bytes=limit * 1024 * 1024),
        cost_estimate=pl.CostEstimate(flops=0, bytes_accessed=0, transcendentals=0),
    )(*placed)


def column_masks(cols, lanes=LANES):
    at = lax.broadcasted_iota(jnp.int32, (cols, lanes), 0)
    return [
        (at - (j - SIDE) >= 0) & (at - (j - SIDE) < cols) for j in range(TAPS)
    ]


def tile_at(t):
    return pl.ds(pl.multiple_of(t * LANES, LANES), LANES)


def own_half():
    me = lax.axis_index("dp")
    odd = 0
    for k in range(lax.axis_size("dp").bit_length() - 1):
        odd = odd + lax.rem(me // (1 << k), 2)
    return lax.rem(odd, 2)


def load_body(
    x_hbm, k_hbm, caps_hbm, x_ref, one_ref, two_ref, taps_ref, caps_ref, sems
):
    rows = x_hbm.shape[1]
    odd = lax.rem(lax.axis_index("space"), 2)
    low, high = odd * (rows - SIDE), (1 - odd) * (rows - SIDE)
    copies = [
        pltpu.make_async_copy(k_hbm, taps_ref, sems.at[0]),
        pltpu.make_async_copy(x_hbm.at[:, pl.ds(high, SIDE)], one_ref, sems.at[1]),
        pltpu.make_async_copy(x_hbm.at[:, pl.ds(low, SIDE)], two_ref, sems.at[2]),
        pltpu.make_async_copy(x_hbm, x_ref, sems.at[3]),
        pltpu.make_async_copy(caps_hbm, caps_ref, sems.at[4]),
    ]
    for copy in copies:
        copy.start()
    for copy in copies:
        copy.wait()


def conv_rows(x_ref, kw_ref, part_ref, image):
    rows, cols, channels = x_ref.shape[1:]

    def tile(t, carry):
        at = tile_at(t)
        xs = [x_ref[image, r, :, at].astype(F32) for r in range(rows)]
        outs = [None] * rows
        for j in range(TAPS):
            ws = [kw_ref[i * TAPS + j, :, at] for i in range(TAPS)]
            for r in range(rows):
                total = None
                for i in range(TAPS):
                    if 0 <= r + i - SIDE < rows:
                        term = ws[i] * xs[r + i - SIDE]
                        total = term if total is None else total + term
                if j != SIDE:
                    total = pltpu.roll(total, (SIDE - j) % cols, 0)
                outs[r] = total if outs[r] is None else outs[r] + total
        for r in range(rows):
            part_ref[r, :, at] = outs[r]
        return carry

    lax.fori_loop(0, channels // LANES, tile, 0)


def first_conv_body(x_ref, taps_ref, caps_ref, w_hbm, part_ref, kw_ref, same_caps_ref, w_ref, sem):
    cols, channels = x_ref.shape[2:]
    copy = pltpu.make_async_copy(w_hbm, w_ref, sem)
    copy.start()
    same_caps_ref[...] = caps_ref[...]
    masks = column_masks(cols, channels)
    for i in range(TAPS):
        taps = taps_ref[i].astype(F32)
        for j in range(TAPS):
            spread = jnp.broadcast_to(taps[j : j + 1], (cols, channels))
            kw_ref[i * TAPS + j] = jnp.where(masks[j], spread, 0.0)
    conv_rows(x_ref, kw_ref, part_ref, 0)
    copy.wait()


def later_conv_body(image, x_ref, kw_ref, w_hbm, part_ref, w_ref, sem):
    copy = pltpu.make_async_copy(w_hbm, w_ref, sem)
    copy.start()
    conv_rows(x_ref, kw_ref, part_ref, image)
    copy.wait()


def gelu_tanh(values):
    return 0.5 * values * (1.0 + jnp.tanh(GELU_C * (values + 0.044715 * values * values * values)))


def gelu_slope(values):
    tangent = jnp.tanh(GELU_C * (values + 0.044715 * values * values * values))
    return 0.5 * (1.0 + tangent) + 0.5 * values * (1.0 - tangent * tangent) * GELU_C * (
        1.0 + 3.0 * 0.044715 * values * values
    )


def three_terms(value):
    high = value.astype(BF).astype(F32)
    rest = value - high
    mid = rest.astype(BF).astype(F32)
    return high, mid, rest - mid


def forward_body(
    one_ref, two_ref, kw_ref, x_ref, win_ref, wout_ref, caps_ref, first_ref, second_ref,
    sums_ref, normed_ref, inv_ref, hid_ref, before_ref, after_ref, same_caps_ref,
    conv_ref, cast_ref, act_ref,
):
    images, rows, cols, channels = x_ref.shape
    hidden_units = win_ref.shape[1]
    pixels = rows * cols
    place = lax.axis_index("space")
    odd = lax.rem(place, 2) == 1
    zeros = jnp.zeros((cols, channels), BF)
    for b in range(images):
        for q in range(SIDE):
            one, two = one_ref[b, q], two_ref[b, q]
            before_ref[b, q] = jnp.where(place > 0, jnp.where(odd, one, two), zeros)
            after_ref[b, q] = jnp.where(
                place < lax.axis_size("space") - 1, jnp.where(odd, two, one), zeros
            )

    def tile(t, carry):
        at = tile_at(t)
        for b in range(images):
            heads = [before_ref[b, q, :, at].astype(F32) for q in range(SIDE)]
            tails = [after_ref[b, q, :, at].astype(F32) for q in range(SIDE)]
            part_ref = (first_ref, second_ref)[b]
            outs = [part_ref[r, :, at] for r in range(rows)]
            for j in range(TAPS):
                ws = [kw_ref[i * TAPS + j, :, at] for i in range(TAPS)]
                for r in list(range(SIDE)) + list(range(rows - SIDE, rows)):
                    total = None
                    for i in range(TAPS):
                        q = r + i
                        if q < SIDE:
                            term = ws[i] * heads[q]
                        elif q >= rows + SIDE:
                            term = ws[i] * tails[q - rows - SIDE]
                        else:
                            continue
                        total = term if total is None else total + term
                    if j != SIDE:
                        total = pltpu.roll(total, (SIDE - j) % cols, 0)
                    outs[r] = outs[r] + total
            for r in range(rows):
                conv_ref[pl.ds((b * rows + r) * cols, cols), at] = outs[r]
        return carry

    lax.fori_loop(0, channels // LANES, tile, 0)

    for start in range(0, images * pixels, 32):
        some = pl.ds(start, 32)
        conv_out = conv_ref[some, :]
        center = conv_out - jnp.mean(conv_out, axis=-1, keepdims=True)
        inv = lax.rsqrt(jnp.mean(center * center, axis=-1, keepdims=True) + EPS)
        normed = center * inv
        normed_ref[some, :] = normed
        inv_ref[some, :] = jnp.broadcast_to(inv, (32, LANES))
        cast_ref[some, :] = normed.astype(BF)

    same_caps_ref[...] = caps_ref[...]
    width = 256
    for start in range(0, hidden_units, width):
        some = pl.ds(start, width)
        hidden = jnp.dot(cast_ref[...], win_ref[:, some], preferred_element_type=F32)
        hid_ref[:, some] = hidden
        activated = gelu_tanh(hidden).astype(BF).astype(F32)
        listed = []
        for b in range(images):
            total = jnp.sum(activated[b * pixels : (b + 1) * pixels], axis=0, keepdims=True)
            listed.extend(three_terms(total))
        listed.append(jnp.zeros((act_ref.shape[0] - 3 * images, width), F32))
        act_ref[:, some] = jnp.concatenate(listed, axis=0)
    mixed = jnp.dot(act_ref[...].astype(BF), wout_ref[...], preferred_element_type=F32)
    for b in range(images):
        own = x_ref[b, 0].astype(F32)
        for r in range(1, rows):
            own = own + x_ref[b, r].astype(F32)
        sums_ref[b : b + 1, :] = jnp.sum(own, axis=0, keepdims=True) + jnp.sum(
            mixed[3 * b : 3 * b + 3], axis=0, keepdims=True
        )


def slope_body(hid_ref, x_ref, before_ref, after_ref, slope_ref, wide_ref):
    images, rows = x_ref.shape[:2]
    for b in range(images):
        for q in range(SIDE):
            wide_ref[b, q] = before_ref[b, q].astype(F32)
            wide_ref[b, rows + SIDE + q] = after_ref[b, q].astype(F32)
        for r in range(rows):
            wide_ref[b, SIDE + r] = x_ref[b, r].astype(F32)
    for start in range(0, hid_ref.shape[1], 256):
        some = pl.ds(start, 256)
        slope_ref[:, some] = gelu_slope(hid_ref[:, some])


def unit_rows(values):
    norms = jnp.sqrt(jnp.sum(values * values, axis=-1, keepdims=True) + EPS)
    return (values / norms, norms)


def joined(bit, mine_ref, theirs_ref):
    upper = lax.rem(lax.axis_index("dp") // bit, 2) == 1
    mine, theirs = mine_ref[...].astype(F32), theirs_ref[...].astype(F32)
    return jnp.concatenate(
        [jnp.where(upper, theirs, mine), jnp.where(upper, mine, theirs)], axis=0
    )


def join_body(bit, mine_ref, theirs_ref, out_ref):
    out_ref[...] = joined(bit, mine_ref, theirs_ref).astype(BF)


def text_cast_body(bit, mine_ref, theirs_ref, cast_ref):
    cast_ref[...] = unit_rows(joined(bit, mine_ref, theirs_ref))[0].astype(BF)


def kernel_sums(grad_ref, wide_ref, list_ref, tap_ref, half):
    images, padded_rows, cols, channels = wide_ref.shape
    rows = padded_rows - 2 * SIDE
    masks = column_masks(cols)
    tiles = channels // LANES // 2
    taps = TAPS * TAPS

    def tile(t, carry):
        at = tile_at(half * tiles + t)
        for j in range(TAPS):
            sums = [None] * TAPS
            for b in range(images):
                grads = []
                for r in range(rows):
                    grad = grad_ref[pl.ds((b * rows + r) * cols, cols), at]
                    grads.append(grad if j == SIDE else pltpu.roll(grad, (j - SIDE) % cols, 0))
                for q in range(padded_rows):
                    here = wide_ref[b, q, :, at]
                    for i in range(TAPS):
                        if 0 <= q - i < rows:
                            term = here * grads[q - i]
                            sums[i] = term if sums[i] is None else sums[i] + term
            for i in range(TAPS):
                tap_ref[pl.ds((i * TAPS + j) * cols, cols), :] = jnp.where(masks[j], sums[i], 0.0)
        total = tap_ref[pl.ds(0, taps, stride=cols), :]
        for w in range(1, cols):
            total = total + tap_ref[pl.ds(w, taps, stride=cols), :]
        list_ref[pl.ds(t * taps, taps), :] = total
        return carry

    list_ref[...] = jnp.zeros_like(list_ref)
    lax.fori_loop(0, tiles, tile, 0)


def backward_body(
    scene_pixels, text_ref, pos_ref, slope_ref, normed_ref, inv_ref, win_ref, wout_ref,
    wide_ref, *refs,
):
    *part_refs, grad_ref, pay_ref, list_ref, tap_ref, hg_ref, row_ref = refs
    images, padded_rows, cols, channels = wide_ref.shape
    pixels = (padded_rows - 2 * SIDE) * cols
    count = text_ref.shape[0]
    pooled = pair_sum([ref[...] for ref in part_refs]) / scene_pixels
    image_unit, pooled_norm = unit_rows(pooled)
    image_cast = image_unit.astype(BF)
    text_cast = text_ref[...]
    logits = (
        LOGIT_SCALE
        * lax.dot_general(
            image_cast, text_cast, (((1,), (1,)), ((), ())), preferred_element_type=F32
        )
        + LOGIT_BIAS
    )
    row_at = lax.broadcasted_iota(jnp.int32, (images, count), 0)
    positive = jnp.zeros((images, count), jnp.int32)
    for b in range(images):
        positive = jnp.where(row_at == b, pos_ref[b], positive)
    labels = jnp.where(
        positive == lax.broadcasted_iota(jnp.int32, (images, count), 1), 1.0, -1.0
    ).astype(F32)
    margin = -labels * logits
    losses = jnp.maximum(margin, 0.0) + jnp.log(1.0 + jnp.exp(-jnp.abs(margin)))
    loss_part = jnp.sum(jnp.sum(losses, axis=1, keepdims=True), axis=0, keepdims=True)
    pair_grad = (-labels / (1.0 + jnp.exp(-margin))).astype(BF)
    image_side = LOGIT_SCALE * jnp.dot(pair_grad, text_cast, preferred_element_type=F32)
    pooled_grad = (
        image_side - image_unit * jnp.sum(image_unit * image_side, axis=-1, keepdims=True)
    ) / pooled_norm
    slope = (pooled_grad / scene_pixels).astype(BF)
    act_grad = lax.dot_general(
        slope, wout_ref[...], (((1,), (1,)), ((), ())), preferred_element_type=F32
    )
    for b in range(images):
        some = pl.ds(b * pixels, pixels)
        hg_ref[some, :] = (act_grad[b : b + 1] * slope_ref[some, :]).astype(BF)
    normed_grad = lax.dot_general(
        hg_ref[...], win_ref[...], (((1,), (1,)), ((), ())), preferred_element_type=F32
    )
    normed = normed_ref[...]
    grad_ref[...] = inv_ref[:, 0:1] * (
        normed_grad
        - jnp.mean(normed_grad, axis=-1, keepdims=True)
        - normed * jnp.mean(normed_grad * normed, axis=-1, keepdims=True)
    )
    half = 1 - own_half()
    kernel_sums(grad_ref, wide_ref, list_ref, tap_ref, half)
    listed = list_ref.shape[0]
    pay_ref[0:listed, :] = list_ref[...].astype(BF)

    row_ref[...] = jnp.zeros_like(row_ref)
    chunks = channels // LANES
    high, mid, low = three_terms(loss_part)
    lane = lax.broadcasted_iota(jnp.int32, (1, LANES), 1)
    for b in range(images):
        for c in range(chunks):
            row_ref[b * (chunks + 1) + c : b * (chunks + 1) + c + 1, :] = image_cast[
                b : b + 1, c * LANES : (c + 1) * LANES
            ].astype(F32)
        at = b * (chunks + 1) + chunks
        row_ref[at : at + 1, 0:count] = pair_grad[b : b + 1, :].astype(F32)
        if b == 0:
            known = row_ref[at : at + 1, :]
            known = jnp.where(lane == LANES - 3, high, known)
            known = jnp.where(lane == LANES - 2, mid, known)
            known = jnp.where(lane == LANES - 1, low, known)
            row_ref[at : at + 1, :] = known
    pay_ref[listed:, :] = row_ref[...].astype(BF)


def own_half_body(grad_ref, wide_ref, list_ref, tap_ref):
    half = own_half()
    kernel_sums(grad_ref, wide_ref, list_ref, tap_ref, half)


def text_body(rows_ref, caps_ref, text_ref, loss_ref, wide_ref):
    images, channels = caps_ref.shape
    chunks = channels // LANES
    stride = wide_ref.shape[0] // lax.axis_size("dp")
    groups = lax.axis_size("dp")
    wide_ref[...] = rows_ref[...].astype(F32)
    lane = lax.broadcasted_iota(jnp.int32, (groups, LANES), 1)
    first = lax.axis_index("dp") * images
    caption_side = [[jnp.zeros((1, LANES), F32) for _ in range(chunks)] for _ in range(images)]
    loss = jnp.zeros((1, 1), F32)
    for b in range(images):
        base = b * (chunks + 1)
        pairs = wide_ref[pl.ds(base + chunks, groups, stride=stride), :]
        if b == 0:
            terms = jnp.where(lane >= LANES - 3, pairs, 0.0)
            loss = jnp.sum(jnp.sum(terms, axis=1, keepdims=True), axis=0, keepdims=True)
        weights = [
            jnp.sum(jnp.where(lane == first + k, pairs, 0.0), axis=1, keepdims=True)
            for k in range(images)
        ]
        for c in range(chunks):
            unit = wide_ref[pl.ds(base + c, groups, stride=stride), :]
            for k in range(images):
                caption_side[k][c] = caption_side[k][c] + jnp.sum(
                    weights[k] * unit, axis=0, keepdims=True
                )
    loss_ref[...] = loss / (groups * images)
    text_unit, text_norm = unit_rows(caps_ref[...].astype(F32))
    for k in range(images):
        side = LOGIT_SCALE * jnp.concatenate(caption_side[k], axis=1)
        unit = text_unit[k : k + 1]
        text_ref[k : k + 1, :] = (
            side - unit * jnp.sum(unit * side, axis=-1, keepdims=True)
        ) / text_norm[k : k + 1]


def merge_body(own_ref, other_ref, out_ref, wide_ref):
    tiles = out_ref.shape[2] // LANES // 2
    half = own_half()
    for source, side in ((own_ref, half), (other_ref, 1 - half)):
        wide_ref[...] = source[...].astype(F32)
        for t in range(tiles):
            at = tile_at(side * tiles + t)
            for i in range(TAPS):
                out_ref[i, :, at] = wide_ref[pl.ds((t * TAPS + i) * TAPS, TAPS), :]


def shifted(array, axis, stride, step, size=4):
    pairs = []
    for i in range(lax.axis_size(axis)):
        place = i // stride % size
        pairs.append((i, i + ((place + step) % size - place) * stride))
    return lax.ppermute(array, axis, pairs)


def flip(array, axis, mask):
    return lax.ppermute(array, axis, [(i, i ^ mask) for i in range(lax.axis_size(axis))])


def groups(size, stride):
    listed = []
    while stride < size:
        members = 4 if size // stride % 4 == 0 else 2
        listed.append((stride, members))
        stride *= members
    return listed


def bits(axis):
    size = lax.axis_size(axis)
    return [1 << k for k in range(size.bit_length() - 1)]


def join(mine, theirs, axis, bit):
    upper = lax.rem(lax.axis_index(axis) // bit, 2) == 1
    return jnp.where(
        upper,
        jnp.concatenate([theirs, mine], axis=0),
        jnp.concatenate([mine, theirs], axis=0),
    )


def rounded(values):
    return lax.reduce_precision(values, 8, 7).astype(BF)


def group_parts(mine, axis, stride, members):
    if members == 2:
        return [mine, flip(mine, axis, stride)]
    one, two, three = [shifted(mine, axis, stride, k) for k in (1, 2, 3)]
    return [mine, two, one, three]


def flipped_parts(mine, axis, stride, members):
    return [mine] + [flip(mine, axis, k * stride) for k in range(1, members)]


def swap_edges(array, second):
    dp, space = lax.axis_size("dp"), lax.axis_size("space")
    pairs = []
    for d in range(dp):
        for s in range(space):
            if not second:
                other = d * space + (s ^ 1)
            elif s in (0, space - 1):
                other = (d ^ 1) * space + s
            else:
                other = d * space + ((s + 1) ^ 1) - 1
            pairs.append((d * space + s, other))
    return lax.ppermute(array, ("dp", "space"), pairs)


def pair_sum(parts):
    parts = [part.astype(F32) for part in parts]
    while len(parts) > 1:
        parts = [parts[k] + parts[k + 1] for k in range(0, len(parts), 2)]
    return parts[0]


def group_sum(mine, axis, stride, members):
    return pair_sum(group_parts(mine, axis, stride, members))


def rows_joined(body, mine, theirs, bit):
    shape = (2 * mine.shape[0], mine.shape[1])
    (out,) = call(functools.partial(body, bit), [(shape, BF)], [mine, theirs])
    return out


def per_device(scenes, kernel, weight_in, weight_out, captions, positives):
    images, rows, cols, channels = scenes.shape
    hidden_units = weight_in.shape[1]
    space_count = lax.axis_size("space")
    pixels = images * rows * cols
    scene_pixels = rows * space_count * cols
    edge = (images, SIDE, cols, channels)

    x, one, two, taps, own_captions = call(
        load_body,
        [
            (scenes.shape, BF),
            (edge, BF),
            (edge, BF),
            (kernel.shape, BF),
            (captions.shape, BF),
        ],
        [scenes, kernel, captions],
        scratch=[pltpu.SemaphoreType.DMA((5,))],
        hbm=(0, 1, 2),
    )
    one = swap_edges(one, False)
    two = swap_edges(two, True)
    theirs = flip(own_captions, "dp", 1)
    part = (scenes.shape[1:], F32)
    first, spread, gathered, win = call(
        first_conv_body,
        [part, ((TAPS * TAPS, cols, channels), F32), (captions.shape, BF), (weight_in.shape, BF)],
        [x, taps, own_captions, weight_in],
        scratch=[pltpu.SemaphoreType.DMA],
        hbm=(3,),
    )
    gathered = rows_joined(join_body, gathered, theirs, 1)
    dp_bits = bits("dp")
    theirs = flip(gathered, "dp", dp_bits[1] + 1)
    second, wout = call(
        functools.partial(later_conv_body, 1),
        [part, (weight_out.shape, BF)],
        [x, spread, weight_out],
        scratch=[pltpu.SemaphoreType.DMA],
        hbm=(2,),
    )
    sums, normed, inv, hidden, before, after, gathered = call(
        forward_body,
        [
            ((images, channels), F32),
            ((pixels, channels), F32),
            ((pixels, LANES), F32),
            ((pixels, hidden_units), F32),
            (edge, BF),
            (edge, BF),
            (gathered.shape, BF),
        ],
        [one, two, spread, x, win, wout, gathered, first, second],
        scratch=[
            pltpu.VMEM((pixels, channels), F32),
            pltpu.VMEM((pixels, channels), BF),
            pltpu.VMEM((3 * images + -3 * images % 8, hidden_units), F32),
        ],
    )
    for bit in dp_bits[1:-1]:
        gathered = rows_joined(join_body, gathered, theirs, bit)
        theirs = flip(gathered, "dp", 2 * bit + 1)
    text_cast = rows_joined(text_cast_body, gathered, theirs, dp_bits[-1])
    space_groups = groups(space_count, 1)
    for stride, members in space_groups[:-1]:
        sums = pair_sum(flipped_parts(sums, "space", stride, members))
    parts = flipped_parts(sums, "space", *space_groups[-1])
    slope, wide = call(
        slope_body,
        [((pixels, hidden_units), F32), ((images, rows + 2 * SIDE, cols, channels), F32)],
        [hidden, x, before, after],
    )

    listed = channels // LANES // 2 * TAPS * TAPS
    listed += -listed % 16
    own_rows = images * (channels // LANES + 1)
    own_rows += -own_rows % 16
    grad, pay = call(
        functools.partial(backward_body, scene_pixels),
        [((pixels, channels), F32), ((listed + own_rows, LANES), BF)],
        [
            text_cast, positives, slope, normed, inv, weight_in, weight_out, wide, *parts,
        ],
        scratch=[
            pltpu.VMEM((listed, LANES), F32),
            pltpu.VMEM((TAPS * TAPS * cols, LANES), F32),
            pltpu.VMEM((pixels, hidden_units), BF),
            pltpu.VMEM((own_rows, LANES), F32),
        ],
        smem=(1,),
    )
    other = flip(pay, "dp", 1)
    (own,) = call(
        own_half_body,
        [((listed, LANES), F32)],
        [grad, wide],
        scratch=[pltpu.VMEM((TAPS * TAPS * cols, LANES), F32)],
    )
    total = own + other[:listed].astype(F32)
    units = join(pay[listed:], other[listed:], "dp", 1)
    for stride, members in groups(lax.axis_size("dp"), 2):
        mine = rounded(total)
        both = jnp.concatenate([mine, units], axis=0)
        near = flip(both, "dp", stride + 1)
        total = mine.astype(F32) + near[:listed].astype(F32)
        joined = join(units, near[listed:], "dp", stride)
        if members == 4:
            far = flip(both, "dp", 2 * stride + 1)
            cross = flip(both, "dp", 3 * stride)
            total = total + (far[:listed].astype(F32) + cross[:listed].astype(F32))
            joined = join(
                joined, join(far[listed:], cross[listed:], "dp", stride), "dp", 2 * stride
            )
        units = joined
    text_grad, loss = call(
        text_body,
        [((images, channels), F32), ((1, 1), F32)],
        [units, own_captions],
        scratch=[pltpu.VMEM(units.shape, F32)],
        placed_out=jax.ShapeDtypeStruct,
    )
    for stride, members in groups(space_count, 1):
        total = group_sum(rounded(total), "space", stride, members)
    mine = rounded(total)
    other = flip(mine, "dp", 1)
    (kernel_grad,) = call(
        merge_body,
        [((TAPS, TAPS, channels), F32)],
        [mine, other],
        scratch=[pltpu.VMEM((listed, LANES), F32)],
        placed_out=jax.ShapeDtypeStruct,
    )
    return (loss.reshape(()), text_grad, kernel_grad)


def solution(mesh):
    return jax.shard_map(
        per_device,
        mesh=mesh,
        in_specs=(P("dp", "space", None, None), P(), P(), P(), P("dp", None), P("dp")),
        out_specs=(P(), P("dp", None), P()),
        check_vma=False,
    )
```

```python
import functools

import jax
import jax.numpy as jnp
from jax import lax
from jax.experimental import pallas as pl
from jax.experimental.pallas import tpu as pltpu
from jax.sharding import PartitionSpec as P

EPS = 1e-06
LOGIT_SCALE = 10.0
LOGIT_BIAS = -1.0
GELU_C = 0.7978845608028654
TAPS = 7
SIDE = 3
LANES = 128
BF = jnp.bfloat16
F32 = jnp.float32


def in_vmem(array):
    return pltpu.with_memory_space_constraint(array, pltpu.VMEM)


def vmem_out(shape, dtype):
    return pltpu.VMEM(shape, dtype)


def in_hbm(array):
    return pltpu.with_memory_space_constraint(array, pltpu.HBM)


def call(body, outs, args, scratch=(), smem=(), hbm=(), limit=10, placed_out=vmem_out):
    specs = []
    placed = []
    for k, arg in enumerate(args):
        if k in smem:
            specs.append(pl.BlockSpec(memory_space=pltpu.SMEM))
            placed.append(arg)
        elif k in hbm:
            specs.append(pl.BlockSpec(memory_space=pl.ANY))
            placed.append(in_hbm(arg))
        else:
            specs.append(pl.BlockSpec(memory_space=pltpu.VMEM))
            placed.append(in_vmem(arg))
    return pl.pallas_call(
        body,
        out_shape=[placed_out(shape, dtype) for shape, dtype in outs],
        in_specs=specs,
        out_specs=[pl.BlockSpec(memory_space=pltpu.VMEM) for _ in outs],
        scratch_shapes=list(scratch),
        compiler_params=pltpu.CompilerParams(vmem_limit_bytes=limit * 1024 * 1024),
        cost_estimate=pl.CostEstimate(flops=0, bytes_accessed=0, transcendentals=0),
    )(*placed)


def column_masks(cols, lanes=LANES):
    at = lax.broadcasted_iota(jnp.int32, (cols, lanes), 0)
    return [
        (at - (j - SIDE) >= 0) & (at - (j - SIDE) < cols) for j in range(TAPS)
    ]


def tile_at(t):
    return pl.ds(pl.multiple_of(t * LANES, LANES), LANES)


def own_half():
    me = lax.axis_index("dp")
    odd = 0
    for k in range(lax.axis_size("dp").bit_length() - 1):
        odd = odd + lax.rem(me // (1 << k), 2)
    return lax.rem(odd, 2)


def load_body(x_hbm, caps_hbm, one_ref, two_ref, caps_ref, sems):
    rows = x_hbm.shape[1]
    odd = lax.rem(lax.axis_index("space"), 2)
    low, high = odd * (rows - SIDE), (1 - odd) * (rows - SIDE)
    copies = [
        pltpu.make_async_copy(x_hbm.at[:, pl.ds(high, SIDE)], one_ref, sems.at[0]),
        pltpu.make_async_copy(x_hbm.at[:, pl.ds(low, SIDE)], two_ref, sems.at[1]),
        pltpu.make_async_copy(caps_hbm, caps_ref, sems.at[2]),
    ]
    for copy in copies:
        copy.start()
    for copy in copies:
        copy.wait()


def conv_rows(x_ref, kw_ref, part_ref, image):
    rows, cols, channels = x_ref.shape[1:]

    def tile(t, carry):
        at = tile_at(t)
        xs = [x_ref[image, r, :, at].astype(F32) for r in range(rows)]
        outs = [None] * rows
        for j in range(TAPS):
            ws = [kw_ref[i * TAPS + j, :, at] for i in range(TAPS)]
            for r in range(rows):
                total = None
                for i in range(TAPS):
                    if 0 <= r + i - SIDE < rows:
                        term = ws[i] * xs[r + i - SIDE]
                        total = term if total is None else total + term
                if j != SIDE:
                    total = pltpu.roll(total, (SIDE - j) % cols, 0)
                outs[r] = total if outs[r] is None else outs[r] + total
        for r in range(rows):
            part_ref[r, :, at] = outs[r]
        return carry

    lax.fori_loop(0, channels // LANES, tile, 0)


def first_conv_body(
    x_hbm, taps_hbm, w_hbm, caps_ref, x_ref, part_ref, kw_ref, same_caps_ref, w_ref, taps_ref, sems
):
    cols, channels = x_hbm.shape[2:]
    copies = [
        pltpu.make_async_copy(taps_hbm, taps_ref, sems.at[0]),
        pltpu.make_async_copy(x_hbm, x_ref, sems.at[1]),
        pltpu.make_async_copy(w_hbm, w_ref, sems.at[2]),
    ]
    for copy in copies:
        copy.start()
    same_caps_ref[...] = caps_ref[...]
    masks = column_masks(cols, channels)
    copies[0].wait()
    for i in range(TAPS):
        taps = taps_ref[i].astype(F32)
        for j in range(TAPS):
            spread = jnp.broadcast_to(taps[j : j + 1], (cols, channels))
            kw_ref[i * TAPS + j] = jnp.where(masks[j], spread, 0.0)
    copies[1].wait()
    conv_rows(x_ref, kw_ref, part_ref, 0)
    copies[2].wait()


def later_conv_body(image, x_ref, kw_ref, part_ref):
    conv_rows(x_ref, kw_ref, part_ref, image)


def gelu_tanh(values):
    return 0.5 * values * (1.0 + jnp.tanh(GELU_C * (values + 0.044715 * values * values * values)))


def gelu_slope(values):
    tangent = jnp.tanh(GELU_C * (values + 0.044715 * values * values * values))
    return 0.5 * (1.0 + tangent) + 0.5 * values * (1.0 - tangent * tangent) * GELU_C * (
        1.0 + 3.0 * 0.044715 * values * values
    )


def three_terms(value):
    high = value.astype(BF).astype(F32)
    rest = value - high
    mid = rest.astype(BF).astype(F32)
    return high, mid, rest - mid


def forward_body(
    one_ref, two_ref, kw_ref, x_ref, win_ref, wout_ref, caps_ref, first_ref, second_ref,
    sums_ref, normed_ref, inv_ref, hid_ref, before_ref, after_ref, same_caps_ref,
    conv_ref, cast_ref, act_ref,
):
    images, rows, cols, channels = x_ref.shape
    hidden_units = win_ref.shape[1]
    pixels = rows * cols
    place = lax.axis_index("space")
    odd = lax.rem(place, 2) == 1
    zeros = jnp.zeros((cols, channels), BF)
    for b in range(images):
        for q in range(SIDE):
            one, two = one_ref[b, q], two_ref[b, q]
            before_ref[b, q] = jnp.where(place > 0, jnp.where(odd, one, two), zeros)
            after_ref[b, q] = jnp.where(
                place < lax.axis_size("space") - 1, jnp.where(odd, two, one), zeros
            )

    def tile(t, carry):
        at = tile_at(t)
        for b in range(images):
            heads = [before_ref[b, q, :, at].astype(F32) for q in range(SIDE)]
            tails = [after_ref[b, q, :, at].astype(F32) for q in range(SIDE)]
            part_ref = (first_ref, second_ref)[b]
            outs = [part_ref[r, :, at] for r in range(rows)]
            for j in range(TAPS):
                ws = [kw_ref[i * TAPS + j, :, at] for i in range(TAPS)]
                for r in list(range(SIDE)) + list(range(rows - SIDE, rows)):
                    total = None
                    for i in range(TAPS):
                        q = r + i
                        if q < SIDE:
                            term = ws[i] * heads[q]
                        elif q >= rows + SIDE:
                            term = ws[i] * tails[q - rows - SIDE]
                        else:
                            continue
                        total = term if total is None else total + term
                    if j != SIDE:
                        total = pltpu.roll(total, (SIDE - j) % cols, 0)
                    outs[r] = outs[r] + total
            for r in range(rows):
                conv_ref[pl.ds((b * rows + r) * cols, cols), at] = outs[r]
        return carry

    lax.fori_loop(0, channels // LANES, tile, 0)

    for start in range(0, images * pixels, 32):
        some = pl.ds(start, 32)
        conv_out = conv_ref[some, :]
        center = conv_out - jnp.mean(conv_out, axis=-1, keepdims=True)
        inv = lax.rsqrt(jnp.mean(center * center, axis=-1, keepdims=True) + EPS)
        normed = center * inv
        normed_ref[some, :] = normed
        inv_ref[some, :] = jnp.broadcast_to(inv, (32, LANES))
        cast_ref[some, :] = normed.astype(BF)

    same_caps_ref[...] = caps_ref[...]
    width = 256
    for start in range(0, hidden_units, width):
        some = pl.ds(start, width)
        hidden = jnp.dot(cast_ref[...], win_ref[:, some], preferred_element_type=F32)
        hid_ref[:, some] = hidden
        activated = gelu_tanh(hidden).astype(BF).astype(F32)
        listed = []
        for b in range(images):
            total = jnp.sum(activated[b * pixels : (b + 1) * pixels], axis=0, keepdims=True)
            listed.extend(three_terms(total))
        listed.append(jnp.zeros((act_ref.shape[0] - 3 * images, width), F32))
        act_ref[:, some] = jnp.concatenate(listed, axis=0)
    mixed = jnp.dot(act_ref[...].astype(BF), wout_ref[...], preferred_element_type=F32)
    for b in range(images):
        own = x_ref[b, 0].astype(F32)
        for r in range(1, rows):
            own = own + x_ref[b, r].astype(F32)
        sums_ref[b : b + 1, :] = jnp.sum(own, axis=0, keepdims=True) + jnp.sum(
            mixed[3 * b : 3 * b + 3], axis=0, keepdims=True
        )


def slope_body(
    hid_ref, x_ref, before_ref, after_ref, win_ref, wout_ref,
    slope_ref, wide_ref, win_t_ref, wout_t_ref,
):
    win_t_ref[...] = win_ref[...].T
    wout_t_ref[...] = wout_ref[...].T
    images, rows = x_ref.shape[:2]
    for b in range(images):
        for q in range(SIDE):
            wide_ref[b, q] = before_ref[b, q].astype(F32)
            wide_ref[b, rows + SIDE + q] = after_ref[b, q].astype(F32)
        for r in range(rows):
            wide_ref[b, SIDE + r] = x_ref[b, r].astype(F32)
    for start in range(0, hid_ref.shape[1], 256):
        some = pl.ds(start, 256)
        slope_ref[:, some] = gelu_slope(hid_ref[:, some])


def unit_rows(values):
    norms = jnp.sqrt(jnp.sum(values * values, axis=-1, keepdims=True) + EPS)
    return (values / norms, norms)


def joined(bit, mine_ref, theirs_ref):
    upper = lax.rem(lax.axis_index("dp") // bit, 2) == 1
    mine, theirs = mine_ref[...].astype(F32), theirs_ref[...].astype(F32)
    return jnp.concatenate(
        [jnp.where(upper, theirs, mine), jnp.where(upper, mine, theirs)], axis=0
    )


def join_body(bit, mine_ref, theirs_ref, out_ref):
    out_ref[...] = joined(bit, mine_ref, theirs_ref).astype(BF)


def text_cast_body(bit, mine_ref, theirs_ref, cast_ref):
    unit = unit_rows(joined(bit, mine_ref, theirs_ref))[0]
    cast_ref[...] = unit.astype(BF).astype(F32)


def kernel_sums(grad_ref, wide_ref, list_ref, tap_ref, half):
    images, padded_rows, cols, channels = wide_ref.shape
    rows = padded_rows - 2 * SIDE
    masks = column_masks(cols)
    tiles = channels // LANES // 2
    taps = TAPS * TAPS

    def tile(t, carry):
        at = tile_at(half * tiles + t)
        for j in range(TAPS):
            sums = [None] * TAPS
            for b in range(images):
                grads = []
                for r in range(rows):
                    grad = grad_ref[pl.ds((b * rows + r) * cols, cols), at]
                    grads.append(grad if j == SIDE else pltpu.roll(grad, (j - SIDE) % cols, 0))
                for q in range(padded_rows):
                    here = wide_ref[b, q, :, at]
                    for i in range(TAPS):
                        if 0 <= q - i < rows:
                            term = here * grads[q - i]
                            sums[i] = term if sums[i] is None else sums[i] + term
            for i in range(TAPS):
                tap_ref[pl.ds((i * TAPS + j) * cols, cols), :] = jnp.where(masks[j], sums[i], 0.0)
        total = tap_ref[pl.ds(0, taps, stride=cols), :]
        for w in range(1, cols):
            total = total + tap_ref[pl.ds(w, taps, stride=cols), :]
        list_ref[pl.ds(t * taps, taps), :] = total
        return carry

    list_ref[...] = jnp.zeros_like(list_ref)
    lax.fori_loop(0, tiles, tile, 0)


def backward_body(
    scene_pixels, text_ref, pos_ref, slope_ref, normed_ref, inv_ref, win_t_ref, wout_t_ref,
    wide_ref, *refs,
):
    *part_refs, grad_ref, pay_ref, list_ref, tap_ref, hg_ref, row_ref = refs
    images, padded_rows, cols, channels = wide_ref.shape
    pixels = (padded_rows - 2 * SIDE) * cols
    count = text_ref.shape[0]
    pooled = pair_sum([ref[...] for ref in part_refs]) / scene_pixels
    image_unit, pooled_norm = unit_rows(pooled)
    image_cast = image_unit.astype(BF)
    text_cast = text_ref[...]
    at = lax.broadcasted_iota(jnp.int32, (count, 1), 0)
    sides, pair_grads, losses = [], [], []
    for b in range(images):
        unit = image_cast[b : b + 1].astype(F32)
        logits = LOGIT_SCALE * jnp.sum(unit * text_cast, axis=1, keepdims=True) + LOGIT_BIAS
        labels = jnp.where(at == pos_ref[b], 1.0, -1.0).astype(F32)
        margin = -labels * logits
        pair_grad = (-labels / (1.0 + jnp.exp(-margin))).astype(BF).astype(F32)
        sides.append(LOGIT_SCALE * jnp.sum(pair_grad * text_cast, axis=0, keepdims=True))
        pair_grads.append(pair_grad)
        losses.append(jnp.maximum(margin, 0.0) + jnp.log(1.0 + jnp.exp(-jnp.abs(margin))))
    image_side = jnp.concatenate(sides, axis=0)
    pooled_grad = (
        image_side - image_unit * jnp.sum(image_unit * image_side, axis=-1, keepdims=True)
    ) / pooled_norm
    slope = (pooled_grad / scene_pixels).astype(BF)
    act_grad = jnp.dot(slope, wout_t_ref[...], preferred_element_type=F32)
    for b in range(images):
        some = pl.ds(b * pixels, pixels)
        hg_ref[some, :] = (act_grad[b : b + 1] * slope_ref[some, :]).astype(BF)
    normed_grad = jnp.dot(hg_ref[...], win_t_ref[...], preferred_element_type=F32)
    normed = normed_ref[...]
    grad_ref[...] = inv_ref[:, 0:1] * (
        normed_grad
        - jnp.mean(normed_grad, axis=-1, keepdims=True)
        - normed * jnp.mean(normed_grad * normed, axis=-1, keepdims=True)
    )
    half = 1 - own_half()
    kernel_sums(grad_ref, wide_ref, list_ref, tap_ref, half)
    listed = list_ref.shape[0]
    pay_ref[0:listed, :] = list_ref[...].astype(BF)

    row_ref[...] = jnp.zeros_like(row_ref)
    chunks = channels // LANES
    high, mid, low = three_terms(jnp.sum(sum(losses), axis=0, keepdims=True))
    lane = lax.broadcasted_iota(jnp.int32, (1, LANES), 1)
    row_at = lax.broadcasted_iota(jnp.int32, (count, LANES), 0)
    column = lax.broadcasted_iota(jnp.int32, (count, LANES), 1)
    for b in range(images):
        for c in range(chunks):
            row_ref[b * (chunks + 1) + c : b * (chunks + 1) + c + 1, :] = image_cast[
                b : b + 1, c * LANES : (c + 1) * LANES
            ].astype(F32)
        at = b * (chunks + 1) + chunks
        placed = jnp.where(column == row_at, pair_grads[b], 0.0)
        known = jnp.sum(placed, axis=0, keepdims=True)
        if b == 0:
            known = jnp.where(lane == LANES - 3, high, known)
            known = jnp.where(lane == LANES - 2, mid, known)
            known = jnp.where(lane == LANES - 1, low, known)
        row_ref[at : at + 1, :] = known
    pay_ref[listed:, :] = row_ref[...].astype(BF)


def own_half_body(grad_ref, wide_ref, list_ref, tap_ref):
    half = own_half()
    kernel_sums(grad_ref, wide_ref, list_ref, tap_ref, half)


def text_body(rows_ref, caps_ref, text_ref, loss_ref, wide_ref):
    images, channels = caps_ref.shape
    chunks = channels // LANES
    stride = wide_ref.shape[0] // lax.axis_size("dp")
    groups = lax.axis_size("dp")
    wide_ref[...] = rows_ref[...].astype(F32)
    lane = lax.broadcasted_iota(jnp.int32, (groups, LANES), 1)
    first = lax.axis_index("dp") * images
    caption_side = [[jnp.zeros((1, LANES), F32) for _ in range(chunks)] for _ in range(images)]
    loss = jnp.zeros((1, 1), F32)
    for b in range(images):
        base = b * (chunks + 1)
        pairs = wide_ref[pl.ds(base + chunks, groups, stride=stride), :]
        if b == 0:
            terms = jnp.where(lane >= LANES - 3, pairs, 0.0)
            loss = jnp.sum(jnp.sum(terms, axis=1, keepdims=True), axis=0, keepdims=True)
        weights = [
            jnp.sum(jnp.where(lane == first + k, pairs, 0.0), axis=1, keepdims=True)
            for k in range(images)
        ]
        for c in range(chunks):
            unit = wide_ref[pl.ds(base + c, groups, stride=stride), :]
            for k in range(images):
                caption_side[k][c] = caption_side[k][c] + jnp.sum(
                    weights[k] * unit, axis=0, keepdims=True
                )
    loss_ref[...] = loss / (groups * images)
    text_unit, text_norm = unit_rows(caps_ref[...].astype(F32))
    for k in range(images):
        side = LOGIT_SCALE * jnp.concatenate(caption_side[k], axis=1)
        unit = text_unit[k : k + 1]
        text_ref[k : k + 1, :] = (
            side - unit * jnp.sum(unit * side, axis=-1, keepdims=True)
        ) / text_norm[k : k + 1]


def merge_body(own_ref, other_ref, out_ref, wide_ref):
    tiles = out_ref.shape[2] // LANES // 2
    half = own_half()
    for source, side in ((own_ref, half), (other_ref, 1 - half)):
        wide_ref[...] = source[...].astype(F32)
        for t in range(tiles):
            at = tile_at(side * tiles + t)
            for i in range(TAPS):
                out_ref[i, :, at] = wide_ref[pl.ds((t * TAPS + i) * TAPS, TAPS), :]


def shifted(array, axis, stride, step, size=4):
    pairs = []
    for i in range(lax.axis_size(axis)):
        place = i // stride % size
        pairs.append((i, i + ((place + step) % size - place) * stride))
    return lax.ppermute(array, axis, pairs)


def flip(array, axis, mask):
    return lax.ppermute(array, axis, [(i, i ^ mask) for i in range(lax.axis_size(axis))])


def groups(size, stride):
    listed = []
    while stride < size:
        members = 4 if size // stride % 4 == 0 else 2
        listed.append((stride, members))
        stride *= members
    return listed


def bits(axis):
    size = lax.axis_size(axis)
    return [1 << k for k in range(size.bit_length() - 1)]


def join(mine, theirs, axis, bit):
    upper = lax.rem(lax.axis_index(axis) // bit, 2) == 1
    return jnp.where(
        upper,
        jnp.concatenate([theirs, mine], axis=0),
        jnp.concatenate([mine, theirs], axis=0),
    )


def rounded(values):
    return lax.reduce_precision(values, 8, 7).astype(BF)


def group_parts(mine, axis, stride, members):
    if members == 2:
        return [mine, flip(mine, axis, stride)]
    one, two, three = [shifted(mine, axis, stride, k) for k in (1, 2, 3)]
    return [mine, two, one, three]


def flipped_parts(mine, axis, stride, members):
    return [mine] + [flip(mine, axis, k * stride) for k in range(1, members)]


def swap_edges(array, second):
    dp, space = lax.axis_size("dp"), lax.axis_size("space")
    pairs = []
    for d in range(dp):
        for s in range(space):
            if not second:
                other = d * space + (s ^ 1)
            elif s in (0, space - 1):
                other = (d ^ 1) * space + s
            else:
                other = d * space + ((s + 1) ^ 1) - 1
            pairs.append((d * space + s, other))
    return lax.ppermute(array, ("dp", "space"), pairs)


def pair_sum(parts):
    parts = [part.astype(F32) for part in parts]
    while len(parts) > 1:
        parts = [parts[k] + parts[k + 1] for k in range(0, len(parts), 2)]
    return parts[0]


def group_sum(mine, axis, stride, members):
    return pair_sum(group_parts(mine, axis, stride, members))


def rows_joined(body, mine, theirs, bit, dtype=BF):
    shape = (2 * mine.shape[0], mine.shape[1])
    (out,) = call(functools.partial(body, bit), [(shape, dtype)], [mine, theirs])
    return out


def per_device(scenes, kernel, weight_in, weight_out, captions, positives):
    images, rows, cols, channels = scenes.shape
    hidden_units = weight_in.shape[1]
    space_count = lax.axis_size("space")
    pixels = images * rows * cols
    scene_pixels = rows * space_count * cols
    edge = (images, SIDE, cols, channels)

    one, two, own_captions = call(
        load_body,
        [(edge, BF), (edge, BF), (captions.shape, BF)],
        [scenes, captions],
        scratch=[pltpu.SemaphoreType.DMA((3,))],
        hbm=(0, 1),
    )
    one = swap_edges(one, False)
    two = swap_edges(two, True)
    theirs = flip(own_captions, "dp", 1)
    part = (scenes.shape[1:], F32)
    x, first, spread, gathered, wout = call(
        first_conv_body,
        [
            (scenes.shape, BF),
            part,
            ((TAPS * TAPS, cols, channels), F32),
            (captions.shape, BF),
            (weight_out.shape, BF),
        ],
        [scenes, kernel, weight_out, own_captions],
        scratch=[pltpu.VMEM(kernel.shape, BF), pltpu.SemaphoreType.DMA((3,))],
        hbm=(0, 1, 2),
    )
    gathered = rows_joined(join_body, gathered, theirs, 1)
    dp_bits = bits("dp")
    theirs = flip(gathered, "dp", dp_bits[1] + 1)
    (second,) = call(functools.partial(later_conv_body, 1), [part], [x, spread])
    sums, normed, inv, hidden, before, after, gathered = call(
        forward_body,
        [
            ((images, channels), F32),
            ((pixels, channels), F32),
            ((pixels, LANES), F32),
            ((pixels, hidden_units), F32),
            (edge, BF),
            (edge, BF),
            (gathered.shape, BF),
        ],
        [one, two, spread, x, weight_in, wout, gathered, first, second],
        scratch=[
            pltpu.VMEM((pixels, channels), F32),
            pltpu.VMEM((pixels, channels), BF),
            pltpu.VMEM((3 * images + -3 * images % 8, hidden_units), F32),
        ],
    )
    for bit in dp_bits[1:-1]:
        gathered = rows_joined(join_body, gathered, theirs, bit)
        theirs = flip(gathered, "dp", 2 * bit + 1)
    text_cast = rows_joined(text_cast_body, gathered, theirs, dp_bits[-1], F32)
    space_groups = groups(space_count, 1)
    for stride, members in space_groups[:-1]:
        sums = pair_sum(flipped_parts(sums, "space", stride, members))
    parts = flipped_parts(sums, "space", *space_groups[-1])
    slope, wide, win_t, wout_t = call(
        slope_body,
        [
            ((pixels, hidden_units), F32),
            ((images, rows + 2 * SIDE, cols, channels), F32),
            (weight_out.shape, BF),
            (weight_in.shape, BF),
        ],
        [hidden, x, before, after, weight_in, wout],
    )

    listed = channels // LANES // 2 * TAPS * TAPS
    listed += -listed % 16
    own_rows = images * (channels // LANES + 1)
    own_rows += -own_rows % 16
    grad, pay = call(
        functools.partial(backward_body, scene_pixels),
        [((pixels, channels), F32), ((listed + own_rows, LANES), BF)],
        [
            text_cast, positives, slope, normed, inv, win_t, wout_t, wide, *parts,
        ],
        scratch=[
            pltpu.VMEM((listed, LANES), F32),
            pltpu.VMEM((TAPS * TAPS * cols, LANES), F32),
            pltpu.VMEM((pixels, hidden_units), BF),
            pltpu.VMEM((own_rows, LANES), F32),
        ],
        smem=(1,),
    )
    other = flip(pay, "dp", 1)
    (own,) = call(
        own_half_body,
        [((listed, LANES), F32)],
        [grad, wide],
        scratch=[pltpu.VMEM((TAPS * TAPS * cols, LANES), F32)],
    )
    total = own + other[:listed].astype(F32)
    units = join(pay[listed:], other[listed:], "dp", 1)
    for stride, members in groups(lax.axis_size("dp"), 2):
        mine = rounded(total)
        both = jnp.concatenate([mine, units], axis=0)
        near = flip(both, "dp", stride + 1)
        total = mine.astype(F32) + near[:listed].astype(F32)
        joined = join(units, near[listed:], "dp", stride)
        if members == 4:
            far = flip(both, "dp", 2 * stride + 1)
            cross = flip(both, "dp", 3 * stride)
            total = total + (far[:listed].astype(F32) + cross[:listed].astype(F32))
            joined = join(
                joined, join(far[listed:], cross[listed:], "dp", stride), "dp", 2 * stride
            )
        units = joined
    text_grad, loss = call(
        text_body,
        [((images, channels), F32), ((1, 1), F32)],
        [units, own_captions],
        scratch=[pltpu.VMEM(units.shape, F32)],
        placed_out=jax.ShapeDtypeStruct,
    )
    for stride, members in groups(space_count, 1):
        total = group_sum(rounded(total), "space", stride, members)
    mine = rounded(total)
    other = flip(mine, "dp", 1)
    (kernel_grad,) = call(
        merge_body,
        [((TAPS, TAPS, channels), F32)],
        [mine, other],
        scratch=[pltpu.VMEM((listed, LANES), F32)],
        placed_out=jax.ShapeDtypeStruct,
    )
    return (loss.reshape(()), text_grad, kernel_grad)


def solution(mesh):
    return jax.shard_map(
        per_device,
        mesh=mesh,
        in_specs=(P("dp", "space", None, None), P(), P(), P(), P("dp", None), P("dp")),
        out_specs=(P(), P("dp", None), P()),
        check_vma=False,
    )
```

```python
import functools

import jax
import jax.numpy as jnp
from jax import lax
from jax.experimental import pallas as pl
from jax.experimental.pallas import tpu as pltpu
from jax.sharding import PartitionSpec as P

EPS = 1e-06
LOGIT_SCALE = 10.0
LOGIT_BIAS = -1.0
GELU_C = 0.7978845608028654
TAPS = 7
SIDE = 3
LANES = 128
SUMS_ORDER = (3, 2, 1, 0)
CHIPS_ORDER = (0, 1, 3, 2)
SPACE_ORDER = (1, 0, 2, 3)
TURNS = (0, 2, 1, 3)
BF = jnp.bfloat16
F32 = jnp.float32


def in_vmem(array):
    return pltpu.with_memory_space_constraint(array, pltpu.VMEM)


def vmem_out(shape, dtype):
    return pltpu.VMEM(shape, dtype)


def in_hbm(array):
    return pltpu.with_memory_space_constraint(array, pltpu.HBM)


def call(body, outs, args, scratch=(), smem=(), hbm=(), limit=10, placed_out=vmem_out):
    specs = []
    placed = []
    for k, arg in enumerate(args):
        if k in smem:
            specs.append(pl.BlockSpec(memory_space=pltpu.SMEM))
            placed.append(arg)
        elif k in hbm:
            specs.append(pl.BlockSpec(memory_space=pl.ANY))
            placed.append(in_hbm(arg))
        else:
            specs.append(pl.BlockSpec(memory_space=pltpu.VMEM))
            placed.append(in_vmem(arg))
    return pl.pallas_call(
        body,
        out_shape=[placed_out(shape, dtype) for shape, dtype in outs],
        in_specs=specs,
        out_specs=[pl.BlockSpec(memory_space=pltpu.VMEM) for _ in outs],
        scratch_shapes=list(scratch),
        compiler_params=pltpu.CompilerParams(vmem_limit_bytes=limit * 1024 * 1024),
        cost_estimate=pl.CostEstimate(flops=0, bytes_accessed=0, transcendentals=0),
    )(*placed)


def column_masks(cols, lanes=LANES):
    at = lax.broadcasted_iota(jnp.int32, (cols, lanes), 0)
    return [
        (at - (j - SIDE) >= 0) & (at - (j - SIDE) < cols) for j in range(TAPS)
    ]


def tile_at(t):
    return pl.ds(pl.multiple_of(t * LANES, LANES), LANES)


def own_half():
    me = lax.axis_index("dp")
    odd = 0
    for k in range(lax.axis_size("dp").bit_length() - 1):
        odd = odd + lax.rem(me // (1 << k), 2)
    return lax.rem(odd, 2)


def load_body(x_hbm, caps_hbm, one_ref, two_ref, caps_ref, sems):
    rows = x_hbm.shape[1]
    odd = lax.rem(lax.axis_index("space"), 2)
    low, high = odd * (rows - SIDE), (1 - odd) * (rows - SIDE)
    copies = [
        pltpu.make_async_copy(x_hbm.at[:, pl.ds(high, SIDE)], one_ref, sems.at[0]),
        pltpu.make_async_copy(x_hbm.at[:, pl.ds(low, SIDE)], two_ref, sems.at[1]),
        pltpu.make_async_copy(caps_hbm, caps_ref, sems.at[2]),
    ]
    for copy in copies:
        copy.start()
    for copy in copies:
        copy.wait()


def conv_rows(x_ref, kw_ref, part_ref, image):
    rows, cols, channels = x_ref.shape[1:]

    def tile(t, carry):
        at = tile_at(t)
        xs = [x_ref[image, r, :, at].astype(F32) for r in range(rows)]
        outs = [None] * rows
        for j in range(TAPS):
            ws = [kw_ref[i * TAPS + j, :, at] for i in range(TAPS)]
            for r in range(rows):
                total = None
                for i in range(TAPS):
                    if 0 <= r + i - SIDE < rows:
                        term = ws[i] * xs[r + i - SIDE]
                        total = term if total is None else total + term
                if j != SIDE:
                    total = pltpu.roll(total, (SIDE - j) % cols, 0)
                outs[r] = total if outs[r] is None else outs[r] + total
        for r in range(rows):
            part_ref[r, :, at] = outs[r]
        return carry

    lax.fori_loop(0, channels // LANES, tile, 0)


def first_conv_body(
    x_hbm, taps_hbm, w_hbm, pos_hbm, caps_ref,
    x_ref, part_ref, kw_ref, same_caps_ref, w_ref, labels_ref, taps_ref, pos_ref, sems,
):
    cols, channels = x_hbm.shape[2:]
    copies = [
        pltpu.make_async_copy(taps_hbm, taps_ref, sems.at[0]),
        pltpu.make_async_copy(x_hbm, x_ref, sems.at[1]),
        pltpu.make_async_copy(w_hbm, w_ref, sems.at[2]),
        pltpu.make_async_copy(pos_hbm, pos_ref, sems.at[3]),
    ]
    for copy in copies:
        copy.start()
    same_caps_ref[...] = caps_ref[...]
    masks = column_masks(cols, channels)
    copies[0].wait()
    for i in range(TAPS):
        taps = taps_ref[i].astype(F32)
        for j in range(TAPS):
            spread = jnp.broadcast_to(taps[j : j + 1], (cols, channels))
            kw_ref[i * TAPS + j] = jnp.where(masks[j], spread, 0.0)
    copies[1].wait()
    conv_rows(x_ref, kw_ref, part_ref, 0)
    copies[3].wait()
    images, count, lanes = labels_ref.shape
    caption = lax.broadcasted_iota(jnp.int32, (count, lanes), 0)
    for b in range(images):
        labels_ref[b] = jnp.where(caption == pos_ref[b], 1.0, -1.0).astype(F32)
    copies[2].wait()


def later_conv_body(image, x_ref, kw_ref, part_ref, own_ref):
    conv_rows(x_ref, kw_ref, part_ref, image)
    images, rows = x_ref.shape[:2]
    for b in range(images):
        own = x_ref[b, 0].astype(F32)
        for r in range(1, rows):
            own = own + x_ref[b, r].astype(F32)
        own_ref[b : b + 1, :] = jnp.sum(own, axis=0, keepdims=True)


def gelu_tanh(values):
    return 0.5 * values * (1.0 + jnp.tanh(GELU_C * (values + 0.044715 * values * values * values)))


def gelu_slope(values):
    tangent = jnp.tanh(GELU_C * (values + 0.044715 * values * values * values))
    return 0.5 * (1.0 + tangent) + 0.5 * values * (1.0 - tangent * tangent) * GELU_C * (
        1.0 + 3.0 * 0.044715 * values * values
    )


def three_terms(value):
    high = value.astype(BF).astype(F32)
    rest = value - high
    mid = rest.astype(BF).astype(F32)
    return high, mid, rest - mid


def forward_body(
    one_ref, two_ref, kw_ref, own_ref, win_ref, wout_ref, caps_ref, first_ref, second_ref,
    sums_ref, normed_ref, inv_ref, hid_ref, before_ref, after_ref, same_caps_ref,
    conv_ref, cast_ref, act_ref,
):
    images = own_ref.shape[0]
    rows, cols, channels = first_ref.shape
    hidden_units = win_ref.shape[1]
    pixels = rows * cols
    place = lax.axis_index("space")
    odd = lax.rem(place, 2) == 1
    zeros = jnp.zeros((cols, channels), BF)
    for b in range(images):
        for q in range(SIDE):
            one, two = one_ref[b, q], two_ref[b, q]
            before_ref[b, q] = jnp.where(place > 0, jnp.where(odd, one, two), zeros)
            after_ref[b, q] = jnp.where(
                place < lax.axis_size("space") - 1, jnp.where(odd, two, one), zeros
            )

    def tile(t, carry):
        at = tile_at(t)
        for b in range(images):
            heads = [before_ref[b, q, :, at].astype(F32) for q in range(SIDE)]
            tails = [after_ref[b, q, :, at].astype(F32) for q in range(SIDE)]
            part_ref = (first_ref, second_ref)[b]
            outs = [part_ref[r, :, at] for r in range(rows)]
            for j in range(TAPS):
                ws = [kw_ref[i * TAPS + j, :, at] for i in range(TAPS)]
                for r in list(range(SIDE)) + list(range(rows - SIDE, rows)):
                    total = None
                    for i in range(TAPS):
                        q = r + i
                        if q < SIDE:
                            term = ws[i] * heads[q]
                        elif q >= rows + SIDE:
                            term = ws[i] * tails[q - rows - SIDE]
                        else:
                            continue
                        total = term if total is None else total + term
                    if j != SIDE:
                        total = pltpu.roll(total, (SIDE - j) % cols, 0)
                    outs[r] = outs[r] + total
            for r in range(rows):
                conv_ref[pl.ds((b * rows + r) * cols, cols), at] = outs[r]
        return carry

    lax.fori_loop(0, channels // LANES, tile, 0)

    for start in range(0, images * pixels, 32):
        some = pl.ds(start, 32)
        conv_out = conv_ref[some, :]
        center = conv_out - jnp.mean(conv_out, axis=-1, keepdims=True)
        inv = lax.rsqrt(jnp.mean(center * center, axis=-1, keepdims=True) + EPS)
        normed = center * inv
        normed_ref[some, :] = normed
        inv_ref[some, :] = jnp.broadcast_to(inv, (32, LANES))
        cast_ref[some, :] = normed.astype(BF)

    same_caps_ref[...] = caps_ref[...]
    width = 256
    for start in range(0, hidden_units, width):
        some = pl.ds(start, width)
        hidden = jnp.dot(cast_ref[...], win_ref[:, some], preferred_element_type=F32)
        hid_ref[:, some] = hidden
        activated = gelu_tanh(hidden).astype(BF).astype(F32)
        listed = []
        for b in range(images):
            total = jnp.sum(activated[b * pixels : (b + 1) * pixels], axis=0, keepdims=True)
            listed.extend(three_terms(total))
        listed.append(jnp.zeros((act_ref.shape[0] - 3 * images, width), F32))
        act_ref[:, some] = jnp.concatenate(listed, axis=0)
    mixed = jnp.dot(act_ref[...].astype(BF), wout_ref[...], preferred_element_type=F32)
    for b in range(images):
        sums_ref[b : b + 1, :] = own_ref[b : b + 1, :] + jnp.sum(
            mixed[3 * b : 3 * b + 3], axis=0, keepdims=True
        )


def slope_body(
    hid_ref, x_ref, before_ref, after_ref, win_ref, wout_ref,
    slope_ref, odd_ref, even_gap_ref, odd_gap_ref, win_t_ref, wout_t_ref,
):
    win_t_ref[...] = win_ref[...].T
    wout_t_ref[...] = wout_ref[...].T
    images, rows = x_ref.shape[:2]
    for b in range(images):
        padded = [before_ref[b, q].astype(F32) for q in range(SIDE)]
        padded += [x_ref[b, r].astype(F32) for r in range(rows)]
        padded += [after_ref[b, q].astype(F32) for q in range(SIDE)]
        for n in range(len(padded) // 2):
            odd_ref[b, n] = padded[2 * n + 1]
            even_gap_ref[b, n] = padded[2 * n] - padded[2 * n + 1]
            if n > 0:
                odd_gap_ref[b, n - 1] = padded[2 * n] - padded[2 * n - 1]
    for start in range(0, hid_ref.shape[1], 256):
        some = pl.ds(start, 256)
        slope_ref[:, some] = gelu_slope(hid_ref[:, some])


def unit_rows(values):
    norms = jnp.sqrt(jnp.sum(values * values, axis=-1, keepdims=True) + EPS)
    return (values / norms, norms)


def joined(bit, mine_ref, theirs_ref):
    upper = lax.rem(lax.axis_index("dp") // bit, 2) == 1
    mine, theirs = mine_ref[...].astype(F32), theirs_ref[...].astype(F32)
    return jnp.concatenate(
        [jnp.where(upper, theirs, mine), jnp.where(upper, mine, theirs)], axis=0
    )


def join_body(bit, mine_ref, theirs_ref, out_ref):
    out_ref[...] = joined(bit, mine_ref, theirs_ref).astype(BF)


def text_cast_body(bit, mine_ref, theirs_ref, cast_ref):
    unit = unit_rows(joined(bit, mine_ref, theirs_ref))[0]
    cast_ref[...] = unit.astype(BF).astype(F32)


def kernel_sums(
    grad_ref, pair_ref, odd_ref, even_gap_ref, odd_gap_ref, list_ref, tap_ref, half
):
    images, pairs, cols, channels = odd_ref.shape
    pairs -= SIDE
    masks = column_masks(cols)
    tiles = channels // LANES // 2
    taps = TAPS * TAPS
    evens, odds = (TAPS + 1) // 2, TAPS // 2

    def tile(t, carry):
        at = tile_at(half * tiles + t)

        def rolled(ref, row, j):
            value = ref[pl.ds(row * cols, cols), at]
            return value if j == SIDE else pltpu.roll(value, (j - SIDE) % cols, 0)

        for j in range(TAPS):
            shared, even, odd = [None] * evens, [None] * evens, [None] * odds

            def add(sums, rows_ref, grads, b, n):
                here = rows_ref[b, n, :, at]
                for l in range(len(sums)):
                    if 0 <= n - l < pairs:
                        term = here * grads[n - l]
                        sums[l] = term if sums[l] is None else sums[l] + term

            for b in range(images):
                first = b * pairs
                both = [rolled(pair_ref, first + m, j) for m in range(pairs)]
                for n in range(pairs + SIDE):
                    add(shared, odd_ref, both, b, n)
                low = [rolled(grad_ref, 2 * (first + m), j) for m in range(pairs)]
                for n in range(pairs + SIDE):
                    add(even, even_gap_ref, low, b, n)
                high = [rolled(grad_ref, 2 * (first + m) + 1, j) for m in range(pairs)]
                for n in range(pairs + SIDE - 1):
                    add(odd, odd_gap_ref, high, b, n)
            for i in range(TAPS):
                total = shared[i // 2] + (odd if i % 2 else even)[i // 2]
                tap_ref[pl.ds((i * TAPS + j) * cols, cols), :] = jnp.where(masks[j], total, 0.0)
        total = tap_ref[pl.ds(0, taps, stride=cols), :]
        for w in range(1, cols):
            total = total + tap_ref[pl.ds(w, taps, stride=cols), :]
        list_ref[pl.ds(t * taps, taps), :] = total
        return carry

    list_ref[...] = jnp.zeros_like(list_ref)
    lax.fori_loop(0, tiles, tile, 0)


def backward_body(
    scene_pixels, patterns, text_ref, labels_ref, slope_ref, normed_ref, inv_ref, win_t_ref, wout_t_ref,
    odd_ref, even_gap_ref, odd_gap_ref, *refs,
):
    *part_refs, grad_ref, pair_ref, pay_ref, list_ref, tap_ref, hg_ref, row_ref = refs
    images, padded_pairs, cols, channels = odd_ref.shape
    pixels = 2 * (padded_pairs - SIDE) * cols
    count = text_ref.shape[0]
    pooled = pair_sum(patterns, [ref[...] for ref in part_refs]) / scene_pixels
    image_unit, pooled_norm = unit_rows(pooled)
    image_cast = image_unit.astype(BF)
    text_cast = text_ref[...]
    sides, pair_grads, losses = [], [], []
    for b in range(images):
        unit = image_cast[b : b + 1].astype(F32)
        logits = LOGIT_SCALE * jnp.sum(unit * text_cast, axis=1, keepdims=True) + LOGIT_BIAS
        labels = labels_ref[b, :, 0:1]
        margin = -labels * logits
        pair_grad = (-labels / (1.0 + jnp.exp(-margin))).astype(BF).astype(F32)
        sides.append(LOGIT_SCALE * jnp.sum(pair_grad * text_cast, axis=0, keepdims=True))
        pair_grads.append(pair_grad)
        losses.append(jnp.maximum(margin, 0.0) + jnp.log(1.0 + jnp.exp(-jnp.abs(margin))))
    image_side = jnp.concatenate(sides, axis=0)
    pooled_grad = (
        image_side - image_unit * jnp.sum(image_unit * image_side, axis=-1, keepdims=True)
    ) / pooled_norm
    slope = (pooled_grad / scene_pixels).astype(BF)
    act_grad = jnp.dot(slope, wout_t_ref[...], preferred_element_type=F32)
    for b in range(images):
        some = pl.ds(b * pixels, pixels)
        hg_ref[some, :] = (act_grad[b : b + 1] * slope_ref[some, :]).astype(BF)
    normed_grad = jnp.dot(hg_ref[...], win_t_ref[...], preferred_element_type=F32)
    normed = normed_ref[...]
    grad_ref[...] = inv_ref[:, 0:1] * (
        normed_grad
        - jnp.mean(normed_grad, axis=-1, keepdims=True)
        - normed * jnp.mean(normed_grad * normed, axis=-1, keepdims=True)
    )
    for m in range(images * (padded_pairs - SIDE)):
        start = 2 * m * cols
        pair_ref[pl.ds(m * cols, cols), :] = (
            grad_ref[pl.ds(start, cols), :] + grad_ref[pl.ds(start + cols, cols), :]
        )
    half = 1 - own_half()
    kernel_sums(
        grad_ref, pair_ref, odd_ref, even_gap_ref, odd_gap_ref, list_ref, tap_ref, half
    )
    listed = list_ref.shape[0]
    pay_ref[0:listed, :] = list_ref[...].astype(BF)

    row_ref[...] = jnp.zeros_like(row_ref)
    chunks = channels // LANES
    high, mid, low = three_terms(jnp.sum(sum(losses), axis=0, keepdims=True))
    lane = lax.broadcasted_iota(jnp.int32, (1, LANES), 1)
    row_at = lax.broadcasted_iota(jnp.int32, (count, LANES), 0)
    column = lax.broadcasted_iota(jnp.int32, (count, LANES), 1)
    for b in range(images):
        for c in range(chunks):
            row_ref[b * (chunks + 1) + c : b * (chunks + 1) + c + 1, :] = image_cast[
                b : b + 1, c * LANES : (c + 1) * LANES
            ].astype(F32)
        at = b * (chunks + 1) + chunks
        placed = jnp.where(column == row_at, pair_grads[b], 0.0)
        known = jnp.sum(placed, axis=0, keepdims=True)
        if b == 0:
            known = jnp.where(lane == LANES - 3, high, known)
            known = jnp.where(lane == LANES - 2, mid, known)
            known = jnp.where(lane == LANES - 1, low, known)
        row_ref[at : at + 1, :] = known
    pay_ref[listed:, :] = row_ref[...].astype(BF)


def own_half_body(grad_ref, pair_ref, odd_ref, even_gap_ref, odd_gap_ref, list_ref, tap_ref):
    kernel_sums(
        grad_ref, pair_ref, odd_ref, even_gap_ref, odd_gap_ref, list_ref, tap_ref, own_half()
    )


def place_units(out_ref, start, blocks):
    for place, rows in blocks:
        count = rows.shape[0]
        out_ref[pl.ds(pl.multiple_of(start + place * count, 16), count), :] = rows


def cores_body(own_ref, pay_ref, other_ref, both_ref):
    listed = own_ref.shape[0]
    both_ref[0:listed, :] = (own_ref[...] + other_ref[0:listed, :].astype(F32)).astype(BF)
    core = lax.rem(lax.axis_index("dp"), 2)
    place_units(
        both_ref, listed, [(core, pay_ref[listed:, :]), (1 - core, other_ref[listed:, :])]
    )


def chips_body(stride, listed, patterns, *refs):
    *part_refs, total_ref, units_ref = refs
    members = len(part_refs)
    total_ref[...] = pair_sum(patterns, [ref[0:listed, :] for ref in part_refs]).astype(BF)
    place = lax.rem(lax.axis_index("dp") // stride, members)
    low, high = lax.rem(place, 2), place // 2
    blocks = []
    for pattern, ref in zip(patterns, part_refs):
        there = low + pattern % 2 * (1 - 2 * low) + 2 * (high + pattern // 2 * (1 - 2 * high))
        blocks.append((there, ref[listed:, :]))
    place_units(units_ref, 0, blocks)


def sum_body(patterns, *refs):
    *part_refs, total_ref = refs
    total_ref[...] = pair_sum(patterns, [ref[...] for ref in part_refs]).astype(BF)


def text_body(rows_ref, caps_ref, text_ref, loss_ref, wide_ref):
    images, channels = caps_ref.shape
    chunks = channels // LANES
    stride = wide_ref.shape[0] // lax.axis_size("dp")
    groups = lax.axis_size("dp")
    wide_ref[...] = rows_ref[...].astype(F32)
    lane = lax.broadcasted_iota(jnp.int32, (groups, LANES), 1)
    first = lax.axis_index("dp") * images
    caption_side = [[jnp.zeros((1, LANES), F32) for _ in range(chunks)] for _ in range(images)]
    loss = jnp.zeros((1, 1), F32)
    for b in range(images):
        base = b * (chunks + 1)
        pairs = wide_ref[pl.ds(base + chunks, groups, stride=stride), :]
        if b == 0:
            terms = jnp.where(lane >= LANES - 3, pairs, 0.0)
            loss = jnp.sum(jnp.sum(terms, axis=1, keepdims=True), axis=0, keepdims=True)
        weights = [
            jnp.sum(jnp.where(lane == first + k, pairs, 0.0), axis=1, keepdims=True)
            for k in range(images)
        ]
        for c in range(chunks):
            unit = wide_ref[pl.ds(base + c, groups, stride=stride), :]
            for k in range(images):
                caption_side[k][c] = caption_side[k][c] + jnp.sum(
                    weights[k] * unit, axis=0, keepdims=True
                )
    loss_ref[...] = loss / (groups * images)
    text_unit, text_norm = unit_rows(caps_ref[...].astype(F32))
    for k in range(images):
        side = LOGIT_SCALE * jnp.concatenate(caption_side[k], axis=1)
        unit = text_unit[k : k + 1]
        text_ref[k : k + 1, :] = (
            side - unit * jnp.sum(unit * side, axis=-1, keepdims=True)
        ) / text_norm[k : k + 1]


def merge_body(own_ref, other_ref, out_ref, wide_ref):
    tiles = out_ref.shape[2] // LANES // 2
    half = own_half()
    for source, side in ((own_ref, half), (other_ref, 1 - half)):
        wide_ref[...] = source[...].astype(F32)
        for t in range(tiles):
            at = tile_at(side * tiles + t)
            for i in range(TAPS):
                out_ref[i, :, at] = wide_ref[pl.ds((t * TAPS + i) * TAPS, TAPS), :]


def shifted(array, axis, stride, step, size):
    pairs = []
    for i in range(lax.axis_size(axis)):
        place = i // stride % size
        pairs.append((i, i + ((place + step) % size - place) * stride))
    return lax.ppermute(array, axis, pairs)


def flip(array, axis, mask):
    return lax.ppermute(array, axis, [(i, i ^ mask) for i in range(lax.axis_size(axis))])


def groups(size, stride):
    listed = []
    while stride < size:
        members = 4 if size // stride % 4 == 0 else 2
        listed.append((stride, members))
        stride *= members
    return listed


def bits(axis):
    size = lax.axis_size(axis)
    return [1 << k for k in range(size.bit_length() - 1)]


def pair_sum(patterns, parts):
    by_pattern = {p: part.astype(F32) for p, part in zip(patterns, parts)}
    parts = [by_pattern[p] for p in sorted(patterns)]
    while len(parts) > 1:
        parts = [parts[k] + parts[k + 1] for k in range(0, len(parts), 2)]
    return parts[0]


def group_parts(send, mine, members, order):
    patterns = [p for p in order if p < members]
    return tuple(patterns), [send(p) if p else mine for p in patterns]


def swap_edges(array, second):
    dp, space = lax.axis_size("dp"), lax.axis_size("space")
    pairs = []
    for d in range(dp):
        for s in range(space):
            if not second:
                other = d * space + (s ^ 1)
            elif s in (0, space - 1):
                other = (d ^ 1) * space + s
            else:
                other = d * space + ((s + 1) ^ 1) - 1
            pairs.append((d * space + s, other))
    return lax.ppermute(array, ("dp", "space"), pairs)


def rows_joined(body, mine, theirs, bit, dtype=BF):
    shape = (2 * mine.shape[0], mine.shape[1])
    (out,) = call(functools.partial(body, bit), [(shape, dtype)], [mine, theirs])
    return out


def per_device(scenes, kernel, weight_in, weight_out, captions, positives):
    images, rows, cols, channels = scenes.shape
    hidden_units = weight_in.shape[1]
    space_count = lax.axis_size("space")
    pixels = images * rows * cols
    scene_pixels = rows * space_count * cols
    edge = (images, SIDE, cols, channels)

    one, two, own_captions = call(
        load_body,
        [(edge, BF), (edge, BF), (captions.shape, BF)],
        [scenes, captions],
        scratch=[pltpu.SemaphoreType.DMA((3,))],
        hbm=(0, 1),
    )
    one = swap_edges(one, False)
    two = swap_edges(two, True)
    theirs = flip(own_captions, "dp", 1)
    part = (scenes.shape[1:], F32)
    x, first, spread, gathered, wout, labels = call(
        first_conv_body,
        [
            (scenes.shape, BF),
            part,
            ((TAPS * TAPS, cols, channels), F32),
            (captions.shape, BF),
            (weight_out.shape, BF),
            ((images, images * lax.axis_size("dp"), LANES), F32),
        ],
        [scenes, kernel, weight_out, positives, own_captions],
        scratch=[
            pltpu.VMEM(kernel.shape, BF),
            pltpu.SMEM(positives.shape, jnp.int32),
            pltpu.SemaphoreType.DMA((4,)),
        ],
        hbm=(0, 1, 2, 3),
    )
    gathered = rows_joined(join_body, gathered, theirs, 1)
    dp_bits = bits("dp")
    theirs = flip(gathered, "dp", dp_bits[1] + 1)
    second, own_sums = call(
        functools.partial(later_conv_body, 1), [part, ((images, channels), F32)], [x, spread]
    )
    sums, normed, inv, hidden, before, after, gathered = call(
        forward_body,
        [
            ((images, channels), F32),
            ((pixels, channels), F32),
            ((pixels, LANES), F32),
            ((pixels, hidden_units), F32),
            (edge, BF),
            (edge, BF),
            (gathered.shape, BF),
        ],
        [one, two, spread, own_sums, weight_in, wout, gathered, first, second],
        scratch=[
            pltpu.VMEM((pixels, channels), F32),
            pltpu.VMEM((pixels, channels), BF),
            pltpu.VMEM((3 * images + -3 * images % 8, hidden_units), F32),
        ],
    )
    for bit in dp_bits[1:-1]:
        gathered = rows_joined(join_body, gathered, theirs, bit)
        theirs = flip(gathered, "dp", 2 * bit + 1)
    text_cast = rows_joined(text_cast_body, gathered, theirs, dp_bits[-1], F32)
    space_groups = groups(space_count, 1)
    for stride, members in space_groups:
        patterns, parts = group_parts(
            lambda p: flip(sums, "space", p * stride), sums, members, SUMS_ORDER
        )
        if stride != space_groups[-1][0]:
            sums = pair_sum(patterns, parts)
    padded_pairs = rows // 2 + SIDE
    slope, odd, even_gap, odd_gap, win_t, wout_t = call(
        slope_body,
        [
            ((pixels, hidden_units), F32),
            ((images, padded_pairs, cols, channels), F32),
            ((images, padded_pairs, cols, channels), F32),
            ((images, padded_pairs - 1, cols, channels), F32),
            (weight_out.shape, BF),
            (weight_in.shape, BF),
        ],
        [hidden, x, before, after, weight_in, wout],
    )

    listed = channels // LANES // 2 * TAPS * TAPS
    listed += -listed % 16
    own_rows = images * (channels // LANES + 1)
    own_rows += -own_rows % 16
    grad, pair, pay = call(
        functools.partial(backward_body, scene_pixels, patterns),
        [
            ((pixels, channels), F32),
            ((pixels // 2, channels), F32),
            ((listed + own_rows, LANES), BF),
        ],
        [
            text_cast, labels, slope, normed, inv, win_t, wout_t,
            odd, even_gap, odd_gap, *parts,
        ],
        scratch=[
            pltpu.VMEM((listed, LANES), F32),
            pltpu.VMEM((TAPS * TAPS * cols, LANES), F32),
            pltpu.VMEM((pixels, hidden_units), BF),
            pltpu.VMEM((own_rows, LANES), F32),
        ],
    )
    other = flip(pay, "dp", 1)
    (own,) = call(
        own_half_body,
        [((listed, LANES), F32)],
        [grad, pair, odd, even_gap, odd_gap],
        scratch=[pltpu.VMEM((TAPS * TAPS * cols, LANES), F32)],
    )
    units_rows = 2 * own_rows
    (both,) = call(cores_body, [((listed + units_rows, LANES), BF)], [own, pay, other])
    chip_groups = groups(lax.axis_size("dp"), 2)
    for stride, members in chip_groups:
        patterns, parts = group_parts(
            lambda p: flip(both, "dp", p * stride + (p != 3)), both, members, CHIPS_ORDER
        )
        units_rows *= members
        total, units = call(
            functools.partial(chips_body, stride, listed, patterns),
            [((listed, LANES), BF), ((units_rows, LANES), BF)],
            parts,
        )
        if stride != chip_groups[-1][0]:
            both = jnp.concatenate([total, units], axis=0)
    text_grad, loss = call(
        text_body,
        [((images, channels), F32), ((1, 1), F32)],
        [units, own_captions],
        scratch=[pltpu.VMEM(units.shape, F32)],
        placed_out=jax.ShapeDtypeStruct,
    )
    for stride, members in space_groups:
        patterns, parts = group_parts(
            lambda p: shifted(total, "space", stride, TURNS[p] if members == 4 else p, members), total, members, SPACE_ORDER
        )
        (total,) = call(
            functools.partial(sum_body, patterns), [((listed, LANES), BF)], parts
        )
    other = flip(total, "dp", 1)
    (kernel_grad,) = call(
        merge_body,
        [((TAPS, TAPS, channels), F32)],
        [total, other],
        scratch=[pltpu.VMEM((listed, LANES), F32)],
        placed_out=jax.ShapeDtypeStruct,
    )
    return (loss.reshape(()), text_grad, kernel_grad)


def solution(mesh):
    return jax.shard_map(
        per_device,
        mesh=mesh,
        in_specs=(P("dp", "space", None, None), P(), P(), P(), P("dp", None), P("dp")),
        out_specs=(P(), P("dp", None), P()),
        check_vma=False,
    )
```

```python
import functools

import jax
import jax.numpy as jnp
from jax import lax
from jax.experimental import pallas as pl
from jax.experimental.pallas import tpu as pltpu
from jax.sharding import PartitionSpec as P

EPS = 1e-06
LOGIT_SCALE = 10.0
LOGIT_BIAS = -1.0
GELU_C = 0.7978845608028654
TAPS = 7
SIDE = 3
LANES = 128
SUMS_ORDER = (3, 2, 1, 0)
CHIPS_ORDER = (0, 1, 3, 2)
SPACE_ORDER = (1, 0, 2, 3)
TURNS = (0, 2, 1, 3)
BF = jnp.bfloat16
F32 = jnp.float32


def in_vmem(array):
    return pltpu.with_memory_space_constraint(array, pltpu.VMEM)


def vmem_out(shape, dtype):
    return pltpu.VMEM(shape, dtype)


def in_hbm(array):
    return pltpu.with_memory_space_constraint(array, pltpu.HBM)


def call(body, outs, args, scratch=(), smem=(), hbm=(), limit=10, placed_out=vmem_out):
    specs = []
    placed = []
    for k, arg in enumerate(args):
        if k in smem:
            specs.append(pl.BlockSpec(memory_space=pltpu.SMEM))
            placed.append(arg)
        elif k in hbm:
            specs.append(pl.BlockSpec(memory_space=pl.ANY))
            placed.append(in_hbm(arg))
        else:
            specs.append(pl.BlockSpec(memory_space=pltpu.VMEM))
            placed.append(in_vmem(arg))
    return pl.pallas_call(
        body,
        out_shape=[placed_out(shape, dtype) for shape, dtype in outs],
        in_specs=specs,
        out_specs=[pl.BlockSpec(memory_space=pltpu.VMEM) for _ in outs],
        scratch_shapes=list(scratch),
        compiler_params=pltpu.CompilerParams(vmem_limit_bytes=limit * 1024 * 1024),
        cost_estimate=pl.CostEstimate(flops=0, bytes_accessed=0, transcendentals=0),
    )(*placed)


def column_masks(cols, lanes=LANES):
    at = lax.broadcasted_iota(jnp.int32, (cols, lanes), 0)
    return [
        (at - (j - SIDE) >= 0) & (at - (j - SIDE) < cols) for j in range(TAPS)
    ]


def tile_at(t):
    return pl.ds(pl.multiple_of(t * LANES, LANES), LANES)


def own_half():
    me = lax.axis_index("dp")
    odd = 0
    for k in range(lax.axis_size("dp").bit_length() - 1):
        odd = odd + lax.rem(me // (1 << k), 2)
    return lax.rem(odd, 2)


def load_body(
    x_hbm, k_hbm, caps_hbm, one_ref, two_ref, caps_ref, taps_ref, x_ref, sems
):
    rows = x_hbm.shape[1]
    odd = lax.rem(lax.axis_index("space"), 2)
    low, high = odd * (rows - SIDE), (1 - odd) * (rows - SIDE)
    copies = [
        pltpu.make_async_copy(x_hbm.at[:, pl.ds(high, SIDE)], one_ref, sems.at[0]),
        pltpu.make_async_copy(x_hbm.at[:, pl.ds(low, SIDE)], two_ref, sems.at[1]),
        pltpu.make_async_copy(caps_hbm, caps_ref, sems.at[2]),
        pltpu.make_async_copy(k_hbm, taps_ref, sems.at[3]),
        pltpu.make_async_copy(x_hbm, x_ref, sems.at[4]),
    ]
    for copy in copies:
        copy.start()
    for copy in copies:
        copy.wait()


def conv_rows(x_ref, kw_ref, part_ref, image):
    rows, cols, channels = x_ref.shape[1:]

    def tile(t, carry):
        at = tile_at(t)
        xs = [x_ref[image, r, :, at].astype(F32) for r in range(rows)]
        outs = [None] * rows
        for j in range(TAPS):
            ws = [kw_ref[i * TAPS + j, :, at] for i in range(TAPS)]
            for r in range(rows):
                total = None
                for i in range(TAPS):
                    if 0 <= r + i - SIDE < rows:
                        term = ws[i] * xs[r + i - SIDE]
                        total = term if total is None else total + term
                if j != SIDE:
                    total = pltpu.roll(total, (SIDE - j) % cols, 0)
                outs[r] = total if outs[r] is None else outs[r] + total
        for r in range(rows):
            part_ref[r, :, at] = outs[r]
        return carry

    lax.fori_loop(0, channels // LANES, tile, 0)


def first_conv_body(
    x_ref, taps_ref, w_hbm, pos_hbm, caps_ref,
    part_ref, kw_ref, same_caps_ref, w_ref, labels_ref, pos_ref, sems,
):
    cols, channels = x_ref.shape[2:]
    copies = [
        pltpu.make_async_copy(w_hbm, w_ref, sems.at[0]),
        pltpu.make_async_copy(pos_hbm, pos_ref, sems.at[1]),
    ]
    for copy in copies:
        copy.start()
    same_caps_ref[...] = caps_ref[...]
    masks = column_masks(cols, channels)
    for i in range(TAPS):
        taps = taps_ref[i].astype(F32)
        for j in range(TAPS):
            spread = jnp.broadcast_to(taps[j : j + 1], (cols, channels))
            kw_ref[i * TAPS + j] = jnp.where(masks[j], spread, 0.0)
    conv_rows(x_ref, kw_ref, part_ref, 0)
    copies[1].wait()
    images, count, lanes = labels_ref.shape
    caption = lax.broadcasted_iota(jnp.int32, (count, lanes), 0)
    for b in range(images):
        labels_ref[b] = jnp.where(caption == pos_ref[b], 1.0, -1.0).astype(F32)
    copies[0].wait()


def later_conv_body(image, x_ref, kw_ref, part_ref, own_ref):
    conv_rows(x_ref, kw_ref, part_ref, image)
    images, rows = x_ref.shape[:2]
    for b in range(images):
        own = x_ref[b, 0].astype(F32)
        for r in range(1, rows):
            own = own + x_ref[b, r].astype(F32)
        own_ref[b : b + 1, :] = jnp.sum(own, axis=0, keepdims=True)


def gelu_tanh(values):
    return 0.5 * values * (1.0 + jnp.tanh(GELU_C * (values + 0.044715 * values * values * values)))


def gelu_slope(values):
    tangent = jnp.tanh(GELU_C * (values + 0.044715 * values * values * values))
    return 0.5 * (1.0 + tangent) + 0.5 * values * (1.0 - tangent * tangent) * GELU_C * (
        1.0 + 3.0 * 0.044715 * values * values
    )


def three_terms(value):
    high = value.astype(BF).astype(F32)
    rest = value - high
    mid = rest.astype(BF).astype(F32)
    return high, mid, rest - mid


def forward_body(
    two_ref, one_ref, kw_ref, own_ref, win_ref, wout_ref, caps_ref, first_ref, second_ref,
    sums_ref, normed_ref, inv_ref, hid_ref, before_ref, after_ref, same_caps_ref,
    conv_ref, cast_ref, act_ref,
):
    images = own_ref.shape[0]
    rows, cols, channels = first_ref.shape
    hidden_units = win_ref.shape[1]
    pixels = rows * cols
    place = lax.axis_index("space")
    odd = lax.rem(place, 2) == 1
    zeros = jnp.zeros((cols, channels), BF)
    for b in range(images):
        for q in range(SIDE):
            one, two = one_ref[b, q], two_ref[b, q]
            before_ref[b, q] = jnp.where(place > 0, jnp.where(odd, one, two), zeros)
            after_ref[b, q] = jnp.where(
                place < lax.axis_size("space") - 1, jnp.where(odd, two, one), zeros
            )

    def tile(t, carry):
        at = tile_at(t)
        for b in range(images):
            heads = [before_ref[b, q, :, at].astype(F32) for q in range(SIDE)]
            tails = [after_ref[b, q, :, at].astype(F32) for q in range(SIDE)]
            part_ref = (first_ref, second_ref)[b]
            outs = [part_ref[r, :, at] for r in range(rows)]
            for j in range(TAPS):
                ws = [kw_ref[i * TAPS + j, :, at] for i in range(TAPS)]
                for r in list(range(SIDE)) + list(range(rows - SIDE, rows)):
                    total = None
                    for i in range(TAPS):
                        q = r + i
                        if q < SIDE:
                            term = ws[i] * heads[q]
                        elif q >= rows + SIDE:
                            term = ws[i] * tails[q - rows - SIDE]
                        else:
                            continue
                        total = term if total is None else total + term
                    if j != SIDE:
                        total = pltpu.roll(total, (SIDE - j) % cols, 0)
                    outs[r] = outs[r] + total
            for r in range(rows):
                conv_ref[pl.ds((b * rows + r) * cols, cols), at] = outs[r]
        return carry

    lax.fori_loop(0, channels // LANES, tile, 0)

    for start in range(0, images * pixels, 32):
        some = pl.ds(start, 32)
        conv_out = conv_ref[some, :]
        center = conv_out - jnp.mean(conv_out, axis=-1, keepdims=True)
        inv = lax.rsqrt(jnp.mean(center * center, axis=-1, keepdims=True) + EPS)
        normed = center * inv
        normed_ref[some, :] = normed
        inv_ref[some, :] = jnp.broadcast_to(inv, (32, LANES))
        cast_ref[some, :] = normed.astype(BF)

    same_caps_ref[...] = caps_ref[...]
    width = 256
    for start in range(0, hidden_units, width):
        some = pl.ds(start, width)
        hidden = jnp.dot(cast_ref[...], win_ref[:, some], preferred_element_type=F32)
        hid_ref[:, some] = hidden
        activated = gelu_tanh(hidden).astype(BF).astype(F32)
        listed = []
        for b in range(images):
            total = jnp.sum(activated[b * pixels : (b + 1) * pixels], axis=0, keepdims=True)
            listed.extend(three_terms(total))
        listed.append(jnp.zeros((act_ref.shape[0] - 3 * images, width), F32))
        act_ref[:, some] = jnp.concatenate(listed, axis=0)
    mixed = jnp.dot(act_ref[...].astype(BF), wout_ref[...], preferred_element_type=F32)
    for b in range(images):
        sums_ref[b : b + 1, :] = own_ref[b : b + 1, :] + jnp.sum(
            mixed[3 * b : 3 * b + 3], axis=0, keepdims=True
        )


def slope_body(
    hid_ref, x_ref, before_ref, after_ref, win_ref, wout_ref,
    slope_ref, odd_ref, even_gap_ref, odd_gap_ref, win_t_ref, wout_t_ref,
):
    win_t_ref[...] = win_ref[...].T
    wout_t_ref[...] = wout_ref[...].T
    images, rows = x_ref.shape[:2]
    for b in range(images):
        padded = [before_ref[b, q].astype(F32) for q in range(SIDE)]
        padded += [x_ref[b, r].astype(F32) for r in range(rows)]
        padded += [after_ref[b, q].astype(F32) for q in range(SIDE)]
        for n in range(len(padded) // 2):
            odd_ref[b, n] = padded[2 * n + 1]
            even_gap_ref[b, n] = padded[2 * n] - padded[2 * n + 1]
            if n > 0:
                odd_gap_ref[b, n - 1] = padded[2 * n] - padded[2 * n - 1]
    for start in range(0, hid_ref.shape[1], 256):
        some = pl.ds(start, 256)
        slope_ref[:, some] = gelu_slope(hid_ref[:, some])


def unit_rows(values):
    norms = jnp.sqrt(jnp.sum(values * values, axis=-1, keepdims=True) + EPS)
    return (values / norms, norms)


def joined(bit, mine_ref, theirs_ref):
    upper = lax.rem(lax.axis_index("dp") // bit, 2) == 1
    mine, theirs = mine_ref[...].astype(F32), theirs_ref[...].astype(F32)
    return jnp.concatenate(
        [jnp.where(upper, theirs, mine), jnp.where(upper, mine, theirs)], axis=0
    )


def join_body(bit, mine_ref, theirs_ref, out_ref):
    out_ref[...] = joined(bit, mine_ref, theirs_ref).astype(BF)


def text_cast_body(bit, mine_ref, theirs_ref, cast_ref):
    unit = unit_rows(joined(bit, mine_ref, theirs_ref))[0]
    cast_ref[...] = unit.astype(BF).astype(F32)


def kernel_sums(
    grad_ref, pair_ref, odd_ref, even_gap_ref, odd_gap_ref, list_ref, tap_ref, half
):
    images, pairs, cols, channels = odd_ref.shape
    pairs -= SIDE
    masks = column_masks(cols)
    tiles = channels // LANES // 2
    taps = TAPS * TAPS
    evens, odds = (TAPS + 1) // 2, TAPS // 2

    def tile(t, carry):
        at = tile_at(half * tiles + t)

        def rolled(ref, row, j):
            value = ref[pl.ds(row * cols, cols), at]
            return value if j == SIDE else pltpu.roll(value, (j - SIDE) % cols, 0)

        for j in range(TAPS):
            shared, even, odd = [None] * evens, [None] * evens, [None] * odds

            def add(sums, rows_ref, grads, b, n):
                here = rows_ref[b, n, :, at]
                for l in range(len(sums)):
                    if 0 <= n - l < pairs:
                        term = here * grads[n - l]
                        sums[l] = term if sums[l] is None else sums[l] + term

            for b in range(images):
                first = b * pairs
                both = [rolled(pair_ref, first + m, j) for m in range(pairs)]
                for n in range(pairs + SIDE):
                    add(shared, odd_ref, both, b, n)
                low = [rolled(grad_ref, 2 * (first + m), j) for m in range(pairs)]
                for n in range(pairs + SIDE):
                    add(even, even_gap_ref, low, b, n)
                high = [rolled(grad_ref, 2 * (first + m) + 1, j) for m in range(pairs)]
                for n in range(pairs + SIDE - 1):
                    add(odd, odd_gap_ref, high, b, n)
            for i in range(TAPS):
                total = shared[i // 2] + (odd if i % 2 else even)[i // 2]
                tap_ref[pl.ds((i * TAPS + j) * cols, cols), :] = jnp.where(masks[j], total, 0.0)
        total = tap_ref[pl.ds(0, taps, stride=cols), :]
        for w in range(1, cols):
            total = total + tap_ref[pl.ds(w, taps, stride=cols), :]
        list_ref[pl.ds(t * taps, taps), :] = total
        return carry

    list_ref[...] = jnp.zeros_like(list_ref)
    lax.fori_loop(0, tiles, tile, 0)


def backward_body(
    scene_pixels, patterns, text_ref, labels_ref, slope_ref, normed_ref, inv_ref, win_t_ref, wout_t_ref,
    odd_ref, even_gap_ref, odd_gap_ref, *refs,
):
    *part_refs, grad_ref, pair_ref, pay_ref, list_ref, tap_ref, hg_ref, row_ref = refs
    images, padded_pairs, cols, channels = odd_ref.shape
    pixels = 2 * (padded_pairs - SIDE) * cols
    count = text_ref.shape[0]
    pooled = pair_sum(patterns, [ref[...] for ref in part_refs]) / scene_pixels
    image_unit, pooled_norm = unit_rows(pooled)
    image_cast = image_unit.astype(BF)
    text_cast = text_ref[...]
    sides, pair_grads, losses = [], [], []
    for b in range(images):
        unit = image_cast[b : b + 1].astype(F32)
        logits = LOGIT_SCALE * jnp.sum(unit * text_cast, axis=1, keepdims=True) + LOGIT_BIAS
        labels = labels_ref[b, :, 0:1]
        margin = -labels * logits
        pair_grad = (-labels / (1.0 + jnp.exp(-margin))).astype(BF).astype(F32)
        sides.append(LOGIT_SCALE * jnp.sum(pair_grad * text_cast, axis=0, keepdims=True))
        pair_grads.append(pair_grad)
        losses.append(jnp.maximum(margin, 0.0) + jnp.log(1.0 + jnp.exp(-jnp.abs(margin))))
    image_side = jnp.concatenate(sides, axis=0)
    pooled_grad = (
        image_side - image_unit * jnp.sum(image_unit * image_side, axis=-1, keepdims=True)
    ) / pooled_norm
    slope = (pooled_grad / scene_pixels).astype(BF)
    act_grad = jnp.dot(slope, wout_t_ref[...], preferred_element_type=F32)
    for b in range(images):
        some = pl.ds(b * pixels, pixels)
        hg_ref[some, :] = (act_grad[b : b + 1] * slope_ref[some, :]).astype(BF)
    normed_grad = jnp.dot(hg_ref[...], win_t_ref[...], preferred_element_type=F32)
    normed = normed_ref[...]
    grad_ref[...] = inv_ref[:, 0:1] * (
        normed_grad
        - jnp.mean(normed_grad, axis=-1, keepdims=True)
        - normed * jnp.mean(normed_grad * normed, axis=-1, keepdims=True)
    )
    for m in range(images * (padded_pairs - SIDE)):
        start = 2 * m * cols
        pair_ref[pl.ds(m * cols, cols), :] = (
            grad_ref[pl.ds(start, cols), :] + grad_ref[pl.ds(start + cols, cols), :]
        )
    half = 1 - own_half()
    kernel_sums(
        grad_ref, pair_ref, odd_ref, even_gap_ref, odd_gap_ref, list_ref, tap_ref, half
    )
    listed = list_ref.shape[0]
    pay_ref[0:listed, :] = list_ref[...].astype(BF)

    row_ref[...] = jnp.zeros_like(row_ref)
    chunks = channels // LANES
    high, mid, low = three_terms(jnp.sum(sum(losses), axis=0, keepdims=True))
    lane = lax.broadcasted_iota(jnp.int32, (1, LANES), 1)
    row_at = lax.broadcasted_iota(jnp.int32, (count, LANES), 0)
    column = lax.broadcasted_iota(jnp.int32, (count, LANES), 1)
    for b in range(images):
        for c in range(chunks):
            row_ref[b * (chunks + 1) + c : b * (chunks + 1) + c + 1, :] = image_cast[
                b : b + 1, c * LANES : (c + 1) * LANES
            ].astype(F32)
        at = b * (chunks + 1) + chunks
        placed = jnp.where(column == row_at, pair_grads[b], 0.0)
        known = jnp.sum(placed, axis=0, keepdims=True)
        if b == 0:
            known = jnp.where(lane == LANES - 3, high, known)
            known = jnp.where(lane == LANES - 2, mid, known)
            known = jnp.where(lane == LANES - 1, low, known)
        row_ref[at : at + 1, :] = known
    pay_ref[listed:, :] = row_ref[...].astype(BF)


def own_half_body(grad_ref, pair_ref, odd_ref, even_gap_ref, odd_gap_ref, list_ref, tap_ref):
    kernel_sums(
        grad_ref, pair_ref, odd_ref, even_gap_ref, odd_gap_ref, list_ref, tap_ref, own_half()
    )


def place_units(out_ref, start, blocks):
    for place, rows in blocks:
        count = rows.shape[0]
        out_ref[pl.ds(pl.multiple_of(start + place * count, 16), count), :] = rows


def cores_body(own_ref, pay_ref, other_ref, both_ref):
    listed = own_ref.shape[0]
    both_ref[0:listed, :] = (own_ref[...] + other_ref[0:listed, :].astype(F32)).astype(BF)
    core = lax.rem(lax.axis_index("dp"), 2)
    place_units(
        both_ref, listed, [(core, pay_ref[listed:, :]), (1 - core, other_ref[listed:, :])]
    )


def chips_body(stride, listed, patterns, *refs):
    *part_refs, total_ref, units_ref = refs
    members = len(part_refs)
    total_ref[...] = pair_sum(patterns, [ref[0:listed, :] for ref in part_refs]).astype(BF)
    place = lax.rem(lax.axis_index("dp") // stride, members)
    low, high = lax.rem(place, 2), place // 2
    blocks = []
    for pattern, ref in zip(patterns, part_refs):
        there = low + pattern % 2 * (1 - 2 * low) + 2 * (high + pattern // 2 * (1 - 2 * high))
        blocks.append((there, ref[listed:, :]))
    place_units(units_ref, 0, blocks)


def sum_body(patterns, *refs):
    *part_refs, total_ref = refs
    total_ref[...] = pair_sum(patterns, [ref[...] for ref in part_refs]).astype(BF)


def text_body(rows_ref, caps_ref, text_ref, loss_ref, wide_ref):
    images, channels = caps_ref.shape
    chunks = channels // LANES
    stride = wide_ref.shape[0] // lax.axis_size("dp")
    groups = lax.axis_size("dp")
    wide_ref[...] = rows_ref[...].astype(F32)
    lane = lax.broadcasted_iota(jnp.int32, (groups, LANES), 1)
    first = lax.axis_index("dp") * images
    caption_side = [[jnp.zeros((1, LANES), F32) for _ in range(chunks)] for _ in range(images)]
    loss = jnp.zeros((1, 1), F32)
    for b in range(images):
        base = b * (chunks + 1)
        pairs = wide_ref[pl.ds(base + chunks, groups, stride=stride), :]
        if b == 0:
            terms = jnp.where(lane >= LANES - 3, pairs, 0.0)
            loss = jnp.sum(jnp.sum(terms, axis=1, keepdims=True), axis=0, keepdims=True)
        weights = [
            jnp.sum(jnp.where(lane == first + k, pairs, 0.0), axis=1, keepdims=True)
            for k in range(images)
        ]
        for c in range(chunks):
            unit = wide_ref[pl.ds(base + c, groups, stride=stride), :]
            for k in range(images):
                caption_side[k][c] = caption_side[k][c] + jnp.sum(
                    weights[k] * unit, axis=0, keepdims=True
                )
    loss_ref[...] = loss / (groups * images)
    text_unit, text_norm = unit_rows(caps_ref[...].astype(F32))
    for k in range(images):
        side = LOGIT_SCALE * jnp.concatenate(caption_side[k], axis=1)
        unit = text_unit[k : k + 1]
        text_ref[k : k + 1, :] = (
            side - unit * jnp.sum(unit * side, axis=-1, keepdims=True)
        ) / text_norm[k : k + 1]


def merge_body(own_ref, other_ref, out_ref, wide_ref):
    tiles = out_ref.shape[2] // LANES // 2
    half = own_half()
    for source, side in ((own_ref, half), (other_ref, 1 - half)):
        wide_ref[...] = source[...].astype(F32)
        for t in range(tiles):
            at = tile_at(side * tiles + t)
            for i in range(TAPS):
                out_ref[i, :, at] = wide_ref[pl.ds((t * TAPS + i) * TAPS, TAPS), :]


def shifted(array, axis, stride, step, size):
    pairs = []
    for i in range(lax.axis_size(axis)):
        place = i // stride % size
        pairs.append((i, i + ((place + step) % size - place) * stride))
    return lax.ppermute(array, axis, pairs)


def flip(array, axis, mask):
    return lax.ppermute(array, axis, [(i, i ^ mask) for i in range(lax.axis_size(axis))])


def groups(size, stride):
    listed = []
    while stride < size:
        members = 4 if size // stride % 4 == 0 else 2
        listed.append((stride, members))
        stride *= members
    return listed


def bits(axis):
    size = lax.axis_size(axis)
    return [1 << k for k in range(size.bit_length() - 1)]


def pair_sum(patterns, parts):
    by_pattern = {p: part.astype(F32) for p, part in zip(patterns, parts)}
    parts = [by_pattern[p] for p in sorted(patterns)]
    while len(parts) > 1:
        parts = [parts[k] + parts[k + 1] for k in range(0, len(parts), 2)]
    return parts[0]


def group_parts(send, mine, members, order):
    patterns = [p for p in order if p < members]
    return tuple(patterns), [send(p) if p else mine for p in patterns]


def swap_edges(array, second):
    dp, space = lax.axis_size("dp"), lax.axis_size("space")
    pairs = []
    for d in range(dp):
        for s in range(space):
            if not second:
                other = d * space + (s ^ 1)
            elif s in (0, space - 1):
                other = (d ^ 1) * space + s
            else:
                other = d * space + ((s + 1) ^ 1) - 1
            pairs.append((d * space + s, other))
    return lax.ppermute(array, ("dp", "space"), pairs)


def rows_joined(body, mine, theirs, bit, dtype=BF):
    shape = (2 * mine.shape[0], mine.shape[1])
    (out,) = call(functools.partial(body, bit), [(shape, dtype)], [mine, theirs])
    return out


def per_device(scenes, kernel, weight_in, weight_out, captions, positives):
    images, rows, cols, channels = scenes.shape
    hidden_units = weight_in.shape[1]
    space_count = lax.axis_size("space")
    pixels = images * rows * cols
    scene_pixels = rows * space_count * cols
    edge = (images, SIDE, cols, channels)

    one, two, own_captions, taps, x = call(
        load_body,
        [(edge, BF), (edge, BF), (captions.shape, BF), (kernel.shape, BF), (scenes.shape, BF)],
        [scenes, kernel, captions],
        scratch=[pltpu.SemaphoreType.DMA((5,))],
        hbm=(0, 1, 2),
    )
    two = swap_edges(two, True)
    one = swap_edges(one, False)
    theirs = flip(own_captions, "dp", 1)
    part = (scenes.shape[1:], F32)
    first, spread, gathered, wout, labels = call(
        first_conv_body,
        [
            part,
            ((TAPS * TAPS, cols, channels), F32),
            (captions.shape, BF),
            (weight_out.shape, BF),
            ((images, images * lax.axis_size("dp"), LANES), F32),
        ],
        [x, taps, weight_out, positives, own_captions],
        scratch=[
            pltpu.SMEM(positives.shape, jnp.int32),
            pltpu.SemaphoreType.DMA((2,)),
        ],
        hbm=(2, 3),
    )
    gathered = rows_joined(join_body, gathered, theirs, 1)
    dp_bits = bits("dp")
    theirs = flip(gathered, "dp", dp_bits[1] + 1)
    second, own_sums = call(
        functools.partial(later_conv_body, 1), [part, ((images, channels), F32)], [x, spread]
    )
    sums, normed, inv, hidden, before, after, gathered = call(
        forward_body,
        [
            ((images, channels), F32),
            ((pixels, channels), F32),
            ((pixels, LANES), F32),
            ((pixels, hidden_units), F32),
            (edge, BF),
            (edge, BF),
            (gathered.shape, BF),
        ],
        [two, one, spread, own_sums, weight_in, wout, gathered, first, second],
        scratch=[
            pltpu.VMEM((pixels, channels), F32),
            pltpu.VMEM((pixels, channels), BF),
            pltpu.VMEM((3 * images + -3 * images % 8, hidden_units), F32),
        ],
    )
    for bit in dp_bits[1:-1]:
        gathered = rows_joined(join_body, gathered, theirs, bit)
        theirs = flip(gathered, "dp", 2 * bit + 1)
    text_cast = rows_joined(text_cast_body, gathered, theirs, dp_bits[-1], F32)
    space_groups = groups(space_count, 1)
    for stride, members in space_groups:
        patterns, parts = group_parts(
            lambda p: flip(sums, "space", p * stride), sums, members, SUMS_ORDER
        )
        if stride != space_groups[-1][0]:
            sums = pair_sum(patterns, parts)
    padded_pairs = rows // 2 + SIDE
    slope, odd, even_gap, odd_gap, win_t, wout_t = call(
        slope_body,
        [
            ((pixels, hidden_units), F32),
            ((images, padded_pairs, cols, channels), F32),
            ((images, padded_pairs, cols, channels), F32),
            ((images, padded_pairs - 1, cols, channels), F32),
            (weight_out.shape, BF),
            (weight_in.shape, BF),
        ],
        [hidden, x, before, after, weight_in, wout],
    )

    listed = channels // LANES // 2 * TAPS * TAPS
    listed += -listed % 16
    own_rows = images * (channels // LANES + 1)
    own_rows += -own_rows % 16
    grad, pair, pay = call(
        functools.partial(backward_body, scene_pixels, patterns),
        [
            ((pixels, channels), F32),
            ((pixels // 2, channels), F32),
            ((listed + own_rows, LANES), BF),
        ],
        [
            text_cast, labels, slope, normed, inv, win_t, wout_t,
            odd, even_gap, odd_gap, *parts,
        ],
        scratch=[
            pltpu.VMEM((listed, LANES), F32),
            pltpu.VMEM((TAPS * TAPS * cols, LANES), F32),
            pltpu.VMEM((pixels, hidden_units), BF),
            pltpu.VMEM((own_rows, LANES), F32),
        ],
    )
    other = flip(pay, "dp", 1)
    (own,) = call(
        own_half_body,
        [((listed, LANES), F32)],
        [grad, pair, odd, even_gap, odd_gap],
        scratch=[pltpu.VMEM((TAPS * TAPS * cols, LANES), F32)],
    )
    units_rows = 2 * own_rows
    (both,) = call(cores_body, [((listed + units_rows, LANES), BF)], [own, pay, other])
    chip_groups = groups(lax.axis_size("dp"), 2)
    for stride, members in chip_groups:
        patterns, parts = group_parts(
            lambda p: flip(both, "dp", p * stride + (p != 3)), both, members, CHIPS_ORDER
        )
        units_rows *= members
        total, units = call(
            functools.partial(chips_body, stride, listed, patterns),
            [((listed, LANES), BF), ((units_rows, LANES), BF)],
            parts,
        )
        if stride != chip_groups[-1][0]:
            both = jnp.concatenate([total, units], axis=0)
    text_grad, loss = call(
        text_body,
        [((images, channels), F32), ((1, 1), F32)],
        [units, own_captions],
        scratch=[pltpu.VMEM(units.shape, F32)],
        placed_out=jax.ShapeDtypeStruct,
    )
    for stride, members in space_groups:
        patterns, parts = group_parts(
            lambda p: shifted(total, "space", stride, TURNS[p] if members == 4 else p, members), total, members, SPACE_ORDER
        )
        (total,) = call(
            functools.partial(sum_body, patterns), [((listed, LANES), BF)], parts
        )
    other = flip(total, "dp", 1)
    (kernel_grad,) = call(
        merge_body,
        [((TAPS, TAPS, channels), F32)],
        [total, other],
        scratch=[pltpu.VMEM((listed, LANES), F32)],
        placed_out=jax.ShapeDtypeStruct,
    )
    return (loss.reshape(()), text_grad, kernel_grad)


def solution(mesh):
    return jax.shard_map(
        per_device,
        mesh=mesh,
        in_specs=(P("dp", "space", None, None), P(), P(), P(), P("dp", None), P("dp")),
        out_specs=(P(), P("dp", None), P()),
        check_vma=False,
    )
```
